32 devices in a mesh: seq: 8 (over y, x, core), tp: 4 (over z).
Axes of the slice: x: 2, y: 2, z: 4, core: 2. Of those that a mesh axis runs over, the one named last changes fastest.
Arguments:
- queries: bfloat16 [2048, 4096], P('seq', 'tp'), may hold values from -4.5 to 4.5
- sequence_keys: bfloat16 [2048, 1024], P('seq', 'tp'), may hold values from -4.5 to 4.5
- sequence_values: bfloat16 [2048, 1024], P('seq', 'tp'), may hold values from -6 to 6
- output_gradient: bfloat16 [2048, 4096], P('seq', 'tp'), may hold values from -6 to 6
- enc_keys: bfloat16 [512, 16, 1024], P('seq', 'tp'), may hold values from -4.5 to 4.5
- encoded_values: bfloat16 [512, 16, 1024], P('seq', 'tp'), may hold values from -6 to 6
- nbr_owner: int32 [32, 4], P('seq'), may hold values from 0 to 7, as said below
- nbr_slot: int32 [32, 4], P('seq'), may hold values from 0 to 63
Outputs:
- attended: bfloat16 [2048, 4096], P('seq', 'tp')
- query_gradient: bfloat16 [2048, 4096], P('seq', 'tp')
- key_gradient: bfloat16 [2048, 1024], P('seq', 'tp')
- value_gradient: bfloat16 [2048, 1024], P('seq', 'tp')
- encoded_key_gradient: bfloat16 [512, 16, 1024], P('seq', 'tp')
- encoded_value_gradient: bfloat16 [512, 16, 1024], P('seq', 'tp')
The draws below stay inside these ranges and needn't reach their ends.
Inputs may be any that keep to these rules, and one draw needn't show every extreme that they name: `nbr_owner`: among the 16 entries of the stretches of one index of seq, at most 4 name the same owner; in every draw one owner is named exactly 4 times by the entries of every index of seq. The same owner may appear twice in one stretch.
All inputs are finite; a program needn't handle non-finite values.
Results may differ from the reference program's by a relative error of at most 0.0083.
Values may be sent and summed in bfloat16 or wider, within the bound.
No kernel may reach another device: no remote copies, remote signals or barrier semaphores. Data moves between devices by JAX's collectives and lax.ppermute only.
A program may use at most 64 MiB of HBM per device.

```python
import math
import jax
import jax.numpy as jnp
from jax import lax

QUERY_HEADS = 32
KEY_VALUE_HEADS = 8
HEAD_SIZE = 128
TOK_DEV = 256
SPAN_TOKENS = 64
NEIGHBOUR_COUNT = 4
NEIGHBOUR_LENGTH = 16
ENC_DEV = 64
WINDOW_KEYS = 128
LOCAL_SPANS = 4
CAP = 4
SEQUENCE_TOKENS = 2048
SPAN_COUNT = 32
ENCODED_SLOTS = 512
N_SEQ = 8


def base_region(key, salt, shape):
    return jnp.clip(jax.random.normal(jax.random.fold_in(key, salt), shape, jnp.float32), -4.5, 4.5)


def draw_queries(key, part):
    region = base_region(key, 11, (SEQUENCE_TOKENS, QUERY_HEADS * HEAD_SIZE))
    return region.astype(jnp.bfloat16)


def draw_sequence_keys(key, part):
    region = base_region(key, 12, (SEQUENCE_TOKENS, KEY_VALUE_HEADS * HEAD_SIZE))
    return region.astype(jnp.bfloat16)


def draw_enc_keys(key, part):
    region = base_region(key, 13, (ENCODED_SLOTS, NEIGHBOUR_LENGTH, KEY_VALUE_HEADS * HEAD_SIZE))
    return region.astype(jnp.bfloat16)


def draw_nbr_owner(key, part):
    requests = LOCAL_SPANS * NEIGHBOUR_COUNT
    extra_rows = requests - CAP
    spread = min(N_SEQ - 1, max(-(-extra_rows // CAP), 2 * extra_rows // 3))
    hot_owner = jax.random.randint(jax.random.fold_in(key, 21), (), 0, N_SEQ).astype(jnp.int32)

    def one_device(device_key):
        shuffled = jax.random.permutation(jax.random.fold_in(device_key, 1), N_SEQ - 1).astype(jnp.int32)
        others = (hot_owner + 1 + shuffled) % N_SEQ
        listed = jnp.concatenate([jnp.full((CAP,), hot_owner, jnp.int32), others[jnp.arange(extra_rows, dtype=jnp.int32) % spread]])
        return listed[jax.random.permutation(jax.random.fold_in(device_key, 2), requests)]
    device_keys = jax.random.split(jax.random.fold_in(key, 22), N_SEQ)
    return jax.vmap(one_device)(device_keys).reshape(SPAN_COUNT, NEIGHBOUR_COUNT).astype(jnp.int32)


def touch_ends(array, own_key, least, largest):
    extent = array.shape
    index_at = [jax.random.randint(jax.random.fold_in(own_key, axis), (), 0, extent[axis]) for axis in range(len(extent))]
    array = array.at[tuple(index_at)].set(least)
    longest = extent.index(max(extent))
    index_at[longest] = (index_at[longest] + 1) % extent[longest]
    return array.at[tuple(index_at)].set(largest)


def block_levels(own_key, shape, cuts, smallest, largest):
    factor_of, own = 1.0, jax.random.fold_in(own_key, 6)
    for axis_at, blocks in cuts:
        draws = jnp.exp(jax.random.uniform(jax.random.fold_in(own, axis_at), (blocks,), jnp.float32, smallest / len(cuts), largest / len(cuts)))
        factor_of = factor_of * jnp.repeat(draws, shape[axis_at] // blocks).reshape([-1 if axis == axis_at else 1 for axis in range(len(shape))])
    return factor_of


def bell_draw(own_key, dims, scale, most, shards=(), kind=jnp.bfloat16):
    loudness = block_levels(own_key, dims, shards, -0.22, 0.18) if shards else 1.0
    array = jax.random.normal(own_key, dims, jnp.float32) * scale * loudness
    return jnp.minimum(jnp.maximum(array, -most), most).astype(kind)


def setup_inputs(seed: int = 0) -> dict:
    splits = jax.random.split(jax.random.key(seed), 9)
    return {
        "queries": draw_queries(jax.random.fold_in(splits[8], 71), 0),
        "sequence_keys": draw_sequence_keys(jax.random.fold_in(splits[8], 71), 0),
        "sequence_values": bell_draw(splits[2], (SEQUENCE_TOKENS, KEY_VALUE_HEADS * HEAD_SIZE), 1.0, 6.0, ((0, 8), (1, 4))),
        "output_gradient": bell_draw(splits[3], (SEQUENCE_TOKENS, QUERY_HEADS * HEAD_SIZE), 1.0, 6.0, ((0, 8), (1, 4))),
        "enc_keys": draw_enc_keys(jax.random.fold_in(splits[8], 71), 0),
        "encoded_values": bell_draw(splits[5], (ENCODED_SLOTS, NEIGHBOUR_LENGTH, KEY_VALUE_HEADS * HEAD_SIZE), 1.0, 6.0, ((0, 8), (1, 4))),
        "nbr_owner": draw_nbr_owner(jax.random.fold_in(splits[8], 71), 0),
        "nbr_slot": touch_ends(jax.random.randint(splits[7], (SPAN_COUNT, NEIGHBOUR_COUNT), 0, ENC_DEV), jax.random.fold_in(splits[7], 1), 0, ENC_DEV - 1).astype(jnp.int32),
    }


HIGHEST = lax.Precision.HIGHEST

def settle(array_f):
    return lax.optimization_barrier(array_f.astype(jnp.bfloat16)).astype(jnp.float32)

def attend(query_in, rows_of_keys, rows_of_values, grad_rows, allowed):
    score_scale = 1.0 / math.sqrt(HEAD_SIZE)
    scores = jnp.einsum('cqhgd,ckhd->chgqk', query_in, rows_of_keys, precision=HIGHEST) * score_scale
    if allowed is not None:
        scores = jnp.where(allowed, scores, -jnp.inf)
    top_score = lax.optimization_barrier(jnp.max(scores, axis=-1, keepdims=True))
    raised = jnp.exp(scores - top_score)
    probability = raised / lax.optimization_barrier(jnp.sum(raised, axis=-1, keepdims=True))
    weights = settle(probability)
    attended = jnp.einsum('chgqk,ckhd->cqhgd', weights, rows_of_values, precision=HIGHEST)
    grad_prob = jnp.einsum('cqhgd,ckhd->chgqk', grad_rows, rows_of_values, precision=HIGHEST)
    delta_row = lax.optimization_barrier(jnp.sum(probability * grad_prob, axis=-1, keepdims=True))
    grad_score = settle(probability * (grad_prob - delta_row) * score_scale)
    query_gradient = jnp.einsum('chgqk,ckhd->cqhgd', grad_score, rows_of_keys, precision=HIGHEST)
    key_gradient = jnp.einsum('chgqk,cqhgd->ckhd', grad_score, query_in, precision=HIGHEST)
    value_gradient = jnp.einsum('chgqk,cqhgd->ckhd', weights, grad_rows, precision=HIGHEST)
    return (attended, query_gradient, key_gradient, value_gradient)

def self_part(queries, sequence_keys, sequence_values, output_gradient):
    heads_per_group = QUERY_HEADS // KEY_VALUE_HEADS
    rows_per_block = min(512, TOK_DEV)
    key_span = WINDOW_KEYS + rows_per_block
    count_blocks = SEQUENCE_TOKENS // rows_per_block
    query_total = queries.astype(jnp.float32).reshape(count_blocks, rows_per_block, KEY_VALUE_HEADS, heads_per_group, HEAD_SIZE)
    gradient_total = output_gradient.astype(jnp.float32).reshape(count_blocks, rows_per_block, KEY_VALUE_HEADS, heads_per_group, HEAD_SIZE)
    padding_rows = jnp.zeros((WINDOW_KEYS, KEY_VALUE_HEADS, HEAD_SIZE), jnp.float32)
    key_padded_rows = jnp.concatenate([padding_rows, sequence_keys.astype(jnp.float32).reshape(SEQUENCE_TOKENS, KEY_VALUE_HEADS, HEAD_SIZE)], 0)
    value_padded_rows = jnp.concatenate([padding_rows, sequence_values.astype(jnp.float32).reshape(SEQUENCE_TOKENS, KEY_VALUE_HEADS, HEAD_SIZE)], 0)

    def block_step(carried, sliced):
        key_accumulator, value_accumulator = carried
        number, query_block, grad_block = sliced
        first_row = number * rows_per_block
        key_block = lax.dynamic_slice_in_dim(key_padded_rows, first_row, key_span, 0)
        value_block = lax.dynamic_slice_in_dim(value_padded_rows, first_row, key_span, 0)
        rows_at = first_row + jnp.arange(rows_per_block, dtype=jnp.int32)[:, None]
        cols_at = first_row - WINDOW_KEYS + jnp.arange(key_span, dtype=jnp.int32)[None, :]
        allowed = (cols_at >= 0) & (cols_at <= rows_at) & (cols_at > rows_at - WINDOW_KEYS)
        attended, query_gradient, key_gradient, value_gradient = attend(query_block[None], key_block[None], value_block[None], grad_block[None], allowed[None, None, None])
        key_accumulator = lax.dynamic_update_slice_in_dim(key_accumulator, lax.dynamic_slice_in_dim(key_accumulator, first_row, key_span, 0) + key_gradient[0], first_row, 0)
        value_accumulator = lax.dynamic_update_slice_in_dim(value_accumulator, lax.dynamic_slice_in_dim(value_accumulator, first_row, key_span, 0) + value_gradient[0], first_row, 0)
        return ((key_accumulator, value_accumulator), (attended[0], query_gradient[0]))
    empty_accumulator = jnp.zeros((WINDOW_KEYS + SEQUENCE_TOKENS, KEY_VALUE_HEADS, HEAD_SIZE), jnp.float32)
    (key_accumulator, value_accumulator), (attended, query_gradient) = lax.scan(block_step, (empty_accumulator, empty_accumulator), (jnp.arange(count_blocks, dtype=jnp.int32), query_total, gradient_total))
    return (attended.reshape(SEQUENCE_TOKENS, QUERY_HEADS * HEAD_SIZE), query_gradient.reshape(SEQUENCE_TOKENS, QUERY_HEADS * HEAD_SIZE), key_accumulator[WINDOW_KEYS:].reshape(SEQUENCE_TOKENS, KEY_VALUE_HEADS * HEAD_SIZE), value_accumulator[WINDOW_KEYS:].reshape(SEQUENCE_TOKENS, KEY_VALUE_HEADS * HEAD_SIZE))

def cross_part(queries, output_gradient, enc_keys, encoded_values, nbr_owner, nbr_slot):
    heads_per_group = QUERY_HEADS // KEY_VALUE_HEADS
    query_total = queries.astype(jnp.float32).reshape(N_SEQ, LOCAL_SPANS, SPAN_TOKENS, KEY_VALUE_HEADS, heads_per_group, HEAD_SIZE)
    gradient_total = output_gradient.astype(jnp.float32).reshape(N_SEQ, LOCAL_SPANS, SPAN_TOKENS, KEY_VALUE_HEADS, heads_per_group, HEAD_SIZE)
    slot_all = (nbr_owner * ENC_DEV + nbr_slot).astype(jnp.int32)
    slot_groups = slot_all.reshape(N_SEQ, LOCAL_SPANS * NEIGHBOUR_COUNT)
    stored_key_rows = enc_keys.astype(jnp.float32)
    stored_value_rows = encoded_values.astype(jnp.float32)

    def one_group(sliced):
        query_in, grad_in, slot_indices = sliced
        rows_of_keys = jnp.take(stored_key_rows, slot_indices, axis=0).reshape(LOCAL_SPANS, NEIGHBOUR_COUNT * NEIGHBOUR_LENGTH, KEY_VALUE_HEADS, HEAD_SIZE)
        rows_of_values = jnp.take(stored_value_rows, slot_indices, axis=0).reshape(LOCAL_SPANS, NEIGHBOUR_COUNT * NEIGHBOUR_LENGTH, KEY_VALUE_HEADS, HEAD_SIZE)
        attended, query_gradient, key_gradient, value_gradient = attend(query_in, rows_of_keys, rows_of_values, grad_in, None)
        return (attended, query_gradient, key_gradient.reshape(LOCAL_SPANS * NEIGHBOUR_COUNT, NEIGHBOUR_LENGTH, KEY_VALUE_HEADS * HEAD_SIZE), value_gradient.reshape(LOCAL_SPANS * NEIGHBOUR_COUNT, NEIGHBOUR_LENGTH, KEY_VALUE_HEADS * HEAD_SIZE))
    result_list = lax.map(one_group, (query_total, gradient_total, slot_groups))
    flattened_slots = slot_all.reshape(SPAN_COUNT * NEIGHBOUR_COUNT)
    encoded_key_gradient = jax.ops.segment_sum(result_list[2].reshape(SPAN_COUNT * NEIGHBOUR_COUNT, NEIGHBOUR_LENGTH, KEY_VALUE_HEADS * HEAD_SIZE), flattened_slots, num_segments=ENCODED_SLOTS)
    encoded_value_gradient = jax.ops.segment_sum(result_list[3].reshape(SPAN_COUNT * NEIGHBOUR_COUNT, NEIGHBOUR_LENGTH, KEY_VALUE_HEADS * HEAD_SIZE), flattened_slots, num_segments=ENCODED_SLOTS)
    return (result_list[0].reshape(SEQUENCE_TOKENS, QUERY_HEADS * HEAD_SIZE), result_list[1].reshape(SEQUENCE_TOKENS, QUERY_HEADS * HEAD_SIZE), encoded_key_gradient, encoded_value_gradient)

def reference(queries, sequence_keys, sequence_values, output_gradient, enc_keys, encoded_values, nbr_owner, nbr_slot):
    self_out, self_qgrad, key_gradient, value_gradient = self_part(queries, sequence_keys, sequence_values, output_gradient)
    cross_out, cross_qgrad, encoded_key_gradient, encoded_value_gradient = cross_part(queries, output_gradient, enc_keys, encoded_values, nbr_owner, nbr_slot)
    attended = (self_out + cross_out).astype(jnp.bfloat16)
    query_gradient = (self_qgrad + cross_qgrad).astype(jnp.bfloat16)
    return (attended, query_gradient, key_gradient.astype(jnp.bfloat16), value_gradient.astype(jnp.bfloat16), encoded_key_gradient.astype(jnp.bfloat16), encoded_value_gradient.astype(jnp.bfloat16))
```

```python
import math

import jax
import jax.numpy as jnp
from jax import lax
from jax.experimental import pallas as pl
from jax.experimental.pallas import tpu as pltpu
from jax.sharding import PartitionSpec as P

QUERY_HEADS = 32
KEY_VALUE_HEADS = 8
HEAD_SIZE = 128
SPAN_TOKENS = 64
NEIGHBOUR_COUNT = 4
NEIGHBOUR_LENGTH = 16
WINDOW_KEYS = 128
GROUP = QUERY_HEADS // KEY_VALUE_HEADS
SCALE = 1.0 / math.sqrt(HEAD_SIZE)
LOG2E = math.log2(math.e)

F32 = jnp.float32
BF16 = jnp.bfloat16
VMEM = pl.BlockSpec(memory_space=pltpu.VMEM)
SMEM = pl.BlockSpec(memory_space=pltpu.SMEM)
PARAMS = pltpu.CompilerParams(vmem_limit_bytes=48 * 1024 * 1024)


def dot_nn(a, b):
    return lax.dot_general(a, b, (((1,), (0,)), ((), ())), preferred_element_type=F32)


def dot_nt(a, b):
    return lax.dot_general(a, b, (((1,), (1,)), ((), ())), preferred_element_type=F32)


def dot_tn(a, b):
    return lax.dot_general(a, b, (((0,), (0,)), ((), ())), preferred_element_type=F32)


def stacked_heads(ref, first_row, rows, group):
    return jnp.concatenate(
        [
            ref[
                first_row : first_row + rows,
                (group * GROUP + h) * HEAD_SIZE : (group * GROUP + h + 1) * HEAD_SIZE,
            ]
            for h in range(GROUP)
        ],
        axis=0,
    )


def probs_and_grads(keys, values, query_rows, grad_rows, allowed):
    scores = dot_nt(keys, query_rows) * (SCALE * LOG2E)
    if allowed is not None:
        scores = jnp.where(allowed, scores, -jnp.inf)
    raised = jnp.exp2(scores - jnp.max(scores, axis=0, keepdims=True))
    probs = raised * (1.0 / jnp.sum(raised, axis=0, keepdims=True))
    grad_probs = dot_nt(values, grad_rows)
    delta = jnp.sum(probs * grad_probs, axis=0, keepdims=True)
    grad_scores = (probs * (grad_probs - delta) * SCALE).astype(BF16)
    return probs.astype(BF16), grad_scores


def pack_kernel(asked_ref, k_ref, v_ref, send_ref, table_ref):
    devices, spans, per_span = asked_ref.shape
    cap = table_ref.shape[1] - 1
    tokens = k_ref.shape[1]
    tp = NEIGHBOUR_LENGTH // tokens
    width = k_ref.shape[2] // tp

    def one(source, carry):
        for c in range(cap + 1):
            table_ref[source, c] = -1
        count = jnp.int32(0)
        for i in range(spans):
            for j in range(per_span):
                slot = asked_ref[source, i, j]
                table_ref[source, count] = slot
                count = jnp.where(slot >= 0, count + 1, count)
        for c in range(cap):
            slot = jnp.maximum(table_ref[source, c], 0)
            key_rows = k_ref[slot]
            value_rows = v_ref[slot]
            for z in range(tp):
                rows = slice(c * tokens, (c + 1) * tokens)
                cols = slice(z * width, (z + 1) * width)
                send_ref[source * tp + z, rows, 0:width] = key_rows[:, cols]
                send_ref[source * tp + z, rows, width : 2 * width] = value_rows[:, cols]
        return carry

    lax.fori_loop(0, devices, one, 0)


def self_kernel(
    rank_ref, q_ref, k_ref, v_ref, do_ref, halo_ref, out_ref, dq_ref, dkv_ref, back_ref
):
    tokens, kv_width = k_ref.shape
    block = WINDOW_KEYS
    blocks = tokens // block
    key_at = lax.broadcasted_iota(jnp.int32, (2 * block, GROUP * block), 0)
    query_at = lax.broadcasted_iota(jnp.int32, (2 * block, GROUP * block), 1) % block
    band = (key_at > query_at) & (key_at <= query_at + block)
    first_band = band & ((key_at >= block) | (rank_ref[0] > 0))
    for group in range(kv_width // HEAD_SIZE):
        cols = slice(group * HEAD_SIZE, (group + 1) * HEAD_SIZE)
        vcols = slice(kv_width + group * HEAD_SIZE, kv_width + (group + 1) * HEAD_SIZE)
        carried_k = carried_v = None
        for b in range(blocks):
            here = slice(b * block, (b + 1) * block)
            if b == 0:
                keys = jnp.concatenate([halo_ref[:, cols], k_ref[here, cols]], 0)
                values = jnp.concatenate([halo_ref[:, vcols], v_ref[here, cols]], 0)
            else:
                keys = k_ref[(b - 1) * block : (b + 1) * block, cols]
                values = v_ref[(b - 1) * block : (b + 1) * block, cols]
            query_rows = stacked_heads(q_ref, b * block, block, group)
            grad_rows = stacked_heads(do_ref, b * block, block, group)
            weights, grad_scores = probs_and_grads(
                keys, values, query_rows, grad_rows, first_band if b == 0 else band
            )
            out = dot_tn(weights, values)
            dq = dot_tn(grad_scores, keys)
            for h in range(GROUP):
                head = slice((group * GROUP + h) * HEAD_SIZE, (group * GROUP + h + 1) * HEAD_SIZE)
                out_ref[here, head] = out[h * block : (h + 1) * block]
                dq_ref[here, head] = dq[h * block : (h + 1) * block]
            dk = dot_nn(grad_scores, query_rows)
            dv = dot_nn(weights, grad_rows)
            if b == 0:
                back_ref[:, cols] = dk[:block].astype(BF16)
                back_ref[:, vcols] = dv[:block].astype(BF16)
            else:
                before = slice((b - 1) * block, b * block)
                dkv_ref[before, cols] = carried_k + dk[:block]
                dkv_ref[before, vcols] = carried_v + dv[:block]
            carried_k, carried_v = dk[block:], dv[block:]
        last = slice((blocks - 1) * block, blocks * block)
        dkv_ref[last, cols] = carried_k
        dkv_ref[last, vcols] = carried_v


def cross_kernel(
    owner_ref, q_ref, do_ref, got_ref, send_ref, w_ref, ds_ref, near_ref, grad_ref, count_ref
):
    spans, per_span = owner_ref.shape
    devices = count_ref.shape[0]
    all_devices, rows_each, both = got_ref.shape
    tp = all_devices // devices
    tokens = NEIGHBOUR_LENGTH // tp
    kv_width = both // 2
    rows_all = all_devices * rows_each
    rows_near = spans * per_span * NEIGHBOUR_LENGTH
    rows_span = per_span * NEIGHBOUR_LENGTH

    def clear(i, carry):
        count_ref[i] = 0
        return carry

    lax.fori_loop(0, devices, clear, 0)
    lane = lax.broadcasted_iota(jnp.int32, (1, rows_near), 1)
    request = lane // NEIGHBOUR_LENGTH
    within = lane % NEIGHBOUR_LENGTH
    place = (within // tokens) * rows_each + within % tokens
    for i in range(spans):
        for j in range(per_span):
            owner = owner_ref[i, j]
            rank = count_ref[owner]
            count_ref[owner] = rank + 1
            first = owner * (tp * rows_each) + rank * tokens
            place = place + jnp.where(request == i * per_span + j, first, 0)
    row = lax.broadcasted_iota(jnp.int32, (rows_all, rows_near), 0)
    placed = jnp.where(row == place, 1.0, 0.0).astype(BF16)
    near_ref[...] = dot_tn(placed, got_ref[...].reshape(rows_all, both)).astype(BF16)
    for span in range(spans):
        here = slice(span * rows_span, (span + 1) * rows_span)
        for group in range(kv_width // HEAD_SIZE):
            cols = slice(group * HEAD_SIZE, (group + 1) * HEAD_SIZE)
            vcols = slice(kv_width + group * HEAD_SIZE, kv_width + (group + 1) * HEAD_SIZE)
            query_rows = stacked_heads(q_ref, span * SPAN_TOKENS, SPAN_TOKENS, group)
            grad_rows = stacked_heads(do_ref, span * SPAN_TOKENS, SPAN_TOKENS, group)
            weights, grad_scores = probs_and_grads(
                near_ref[here, cols], near_ref[here, vcols], query_rows, grad_rows, None
            )
            at = span * (kv_width // HEAD_SIZE) + group
            w_ref[at] = weights
            ds_ref[at] = grad_scores
            grad_ref[here, cols] = dot_nn(grad_scores, query_rows).astype(BF16)
            grad_ref[here, vcols] = dot_nn(weights, grad_rows).astype(BF16)
    send_ref[...] = dot_nn(placed, grad_ref[...]).astype(BF16).reshape(send_ref.shape)


def join_kernel(
    w_ref, ds_ref, near_ref, out_ref, dq_ref, dkv_ref, back_ref, att_ref, qg_ref, kg_ref, vg_ref
):
    tokens, kv_width = kg_ref.shape
    groups = kv_width // HEAD_SIZE
    spans = w_ref.shape[0] // groups
    rows_span = near_ref.shape[0] // spans
    for span in range(spans):
        here = slice(span * rows_span, (span + 1) * rows_span)
        rows = slice(span * SPAN_TOKENS, (span + 1) * SPAN_TOKENS)
        for group in range(groups):
            cols = slice(group * HEAD_SIZE, (group + 1) * HEAD_SIZE)
            vcols = slice(kv_width + group * HEAD_SIZE, kv_width + (group + 1) * HEAD_SIZE)
            at = span * groups + group
            out = dot_tn(w_ref[at], near_ref[here, vcols])
            dq = dot_tn(ds_ref[at], near_ref[here, cols])
            for h in range(GROUP):
                head = slice((group * GROUP + h) * HEAD_SIZE, (group * GROUP + h + 1) * HEAD_SIZE)
                part = slice(h * SPAN_TOKENS, (h + 1) * SPAN_TOKENS)
                att_ref[rows, head] = (out_ref[rows, head] + out[part]).astype(BF16)
                qg_ref[rows, head] = (dq_ref[rows, head] + dq[part]).astype(BF16)
    halo = back_ref.shape[0]
    kg_ref[: tokens - halo] = dkv_ref[: tokens - halo, :kv_width].astype(BF16)
    vg_ref[: tokens - halo] = dkv_ref[: tokens - halo, kv_width:].astype(BF16)
    kg_ref[tokens - halo :] = (
        dkv_ref[tokens - halo :, :kv_width] + back_ref[:, :kv_width].astype(F32)
    ).astype(BF16)
    vg_ref[tokens - halo :] = (
        dkv_ref[tokens - halo :, kv_width:] + back_ref[:, kv_width:].astype(F32)
    ).astype(BF16)


def sum_kernel(table_ref, got_ref, kg_ref, vg_ref):
    devices, cap = table_ref.shape[0], table_ref.shape[1] - 1
    all_devices, rows_each, both = got_ref.shape
    store_rows, tokens, _ = kg_ref.shape
    tp = all_devices // devices
    width = both // 2
    lanes = devices * rows_each
    lane = lax.broadcasted_iota(jnp.int32, (1, lanes), 1)
    request = lane // tokens
    target = jnp.full((1, lanes), -1, jnp.int32)
    for s in range(devices):
        for c in range(cap):
            target = jnp.where(request == s * cap + c, table_ref[s, c], target)
    target = jnp.where(target >= 0, target * tokens + lane % tokens, -1)
    row = lax.broadcasted_iota(jnp.int32, (store_rows * tokens, lanes), 0)
    owned = jnp.where(row == target, 1.0, 0.0).astype(BF16)
    for z in range(tp):
        got = jnp.concatenate([got_ref[s * tp + z] for s in range(devices)], axis=0)
        total = dot_nn(owned, got).astype(BF16)
        cols = slice(z * width, (z + 1) * width)
        for e in range(store_rows):
            rows = total[e * tokens : (e + 1) * tokens]
            kg_ref[e, :, cols] = rows[:, :width]
            vg_ref[e, :, cols] = rows[:, width:]


def cost(flops, bytes_accessed, transcendentals=0):
    return pl.CostEstimate(
        flops=flops, bytes_accessed=bytes_accessed, transcendentals=transcendentals
    )


def body(
    queries,
    sequence_keys,
    sequence_values,
    output_gradient,
    enc_keys,
    encoded_values,
    nbr_owner,
    nbr_slot,
):
    tokens_here, query_width = queries.shape
    kv_width = sequence_keys.shape[1]
    groups = kv_width // HEAD_SIZE
    devices = lax.axis_size("seq")
    tp = lax.axis_size("tp")
    spans, per_span = nbr_owner.shape
    requests = spans * per_span
    cap = max(2, 2 * requests // devices)
    tokens = enc_keys.shape[1]
    rows_near = requests * NEIGHBOUR_LENGTH
    rows_each = cap * tokens
    window = WINDOW_KEYS
    struct = jax.ShapeDtypeStruct

    ids = jnp.arange(devices, dtype=jnp.int32)[:, None, None]
    asked = jnp.where(nbr_owner[None] == ids, nbr_slot[None], -1)
    asked = lax.all_to_all(asked, "seq", split_axis=0, concat_axis=0, tiled=True)

    halo = jnp.concatenate(
        [sequence_keys[tokens_here - window :], sequence_values[tokens_here - window :]], axis=1
    )
    halo = lax.ppermute(halo, "seq", [(i, i + 1) for i in range(devices - 1)])

    packed, table = pl.pallas_call(
        pack_kernel,
        out_shape=(
            struct((devices * tp, rows_each, 2 * kv_width), BF16),
            struct((devices, cap + 1), jnp.int32),
        ),
        in_specs=[SMEM, VMEM, VMEM],
        out_specs=(VMEM, SMEM),
        compiler_params=PARAMS,
        cost_estimate=cost(0, 2_000_000),
        name="pack_requests",
    )(asked, enc_keys, encoded_values)
    fetched = lax.all_to_all(packed, ("seq", "tp"), split_axis=0, concat_axis=0, tiled=True)

    rank = lax.axis_index("seq").astype(jnp.int32).reshape(1)
    self_out, self_dq, self_dkv, back = pl.pallas_call(
        self_kernel,
        out_shape=(
            struct((tokens_here, query_width), F32),
            struct((tokens_here, query_width), F32),
            struct((tokens_here, 2 * kv_width), F32),
            struct((window, 2 * kv_width), BF16),
        ),
        in_specs=[SMEM] + [VMEM] * 5,
        out_specs=(VMEM,) * 4,
        compiler_params=PARAMS,
        cost_estimate=cost(1_600_000_000, 6_000_000, 1_000_000),
        name="self_attention",
    )(rank, queries, sequence_keys, sequence_values, output_gradient, halo)
    back = lax.ppermute(back, "seq", [(i + 1, i) for i in range(devices - 1)])

    blocks = spans * groups
    columns = GROUP * SPAN_TOKENS
    rows_span = per_span * NEIGHBOUR_LENGTH
    send, weights, grad_scores, near = pl.pallas_call(
        cross_kernel,
        out_shape=(
            struct((devices * tp, rows_each, 2 * kv_width), BF16),
            struct((blocks, rows_span, columns), BF16),
            struct((blocks, rows_span, columns), BF16),
            struct((rows_near, 2 * kv_width), BF16),
        ),
        in_specs=[SMEM] + [VMEM] * 3,
        out_specs=(VMEM,) * 4,
        scratch_shapes=[
            pltpu.VMEM((rows_near, 2 * kv_width), BF16),
            pltpu.SMEM((devices,), jnp.int32),
        ],
        compiler_params=PARAMS,
        cost_estimate=cost(600_000_000, 3_000_000, 200_000),
        name="cross_attention",
    )(nbr_owner, queries, output_gradient, fetched)
    returned = lax.all_to_all(send, ("seq", "tp"), split_axis=0, concat_axis=0, tiled=True)

    attended, query_gradient, key_gradient, value_gradient = pl.pallas_call(
        join_kernel,
        out_shape=(
            struct((tokens_here, query_width), BF16),
            struct((tokens_here, query_width), BF16),
            struct((tokens_here, kv_width), BF16),
            struct((tokens_here, kv_width), BF16),
        ),
        in_specs=[VMEM] * 7,
        out_specs=(VMEM,) * 4,
        compiler_params=PARAMS,
        cost_estimate=cost(300_000_000, 5_000_000),
        name="join_outputs",
    )(weights, grad_scores, near, self_out, self_dq, self_dkv, back)

    store_kgrad, store_vgrad = pl.pallas_call(
        sum_kernel,
        out_shape=(struct(enc_keys.shape, BF16), struct(encoded_values.shape, BF16)),
        in_specs=[SMEM, VMEM],
        out_specs=(VMEM,) * 2,
        compiler_params=PARAMS,
        cost_estimate=cost(200_000_000, 2_000_000),
        name="sum_store_gradients",
    )(table, returned)

    return (
        attended,
        query_gradient,
        key_gradient,
        value_gradient,
        store_kgrad,
        store_vgrad,
    )


def solution(mesh):
    arguments = (P("seq", "tp"),) * 4 + (P("seq", "tp", None),) * 2 + (P("seq", None),) * 2
    results = (P("seq", "tp"),) * 4 + (P("seq", "tp", None),) * 2
    return jax.shard_map(
        body, mesh=mesh, in_specs=arguments, out_specs=results, check_vma=False
    )
```

```python
import functools
import math

import jax
import jax.numpy as jnp
from jax import lax
from jax.experimental import pallas as pl
from jax.experimental.pallas import tpu as pltpu
from jax.sharding import PartitionSpec as P

QUERY_HEADS = 32
KEY_VALUE_HEADS = 8
HEAD_SIZE = 128
SPAN_TOKENS = 64
NEIGHBOUR_COUNT = 4
NEIGHBOUR_LENGTH = 16
WINDOW_KEYS = 128
GROUP = QUERY_HEADS // KEY_VALUE_HEADS
SCALE = 1.0 / math.sqrt(HEAD_SIZE)
LOG2E = math.log2(math.e)

F32 = jnp.float32
BF16 = jnp.bfloat16
VMEM = pl.BlockSpec(memory_space=pltpu.VMEM)
SMEM = pl.BlockSpec(memory_space=pltpu.SMEM)
PARAMS = pltpu.CompilerParams(vmem_limit_bytes=48 * 1024 * 1024)


def dot_nn(a, b):
    return lax.dot_general(a, b, (((1,), (0,)), ((), ())), preferred_element_type=F32)


def dot_nt(a, b):
    return lax.dot_general(a, b, (((1,), (1,)), ((), ())), preferred_element_type=F32)


def dot_tn(a, b):
    return lax.dot_general(a, b, (((0,), (0,)), ((), ())), preferred_element_type=F32)


def stacked_heads(ref, first_row, rows, group):
    return jnp.concatenate(
        [
            ref[
                first_row : first_row + rows,
                (group * GROUP + h) * HEAD_SIZE : (group * GROUP + h + 1) * HEAD_SIZE,
            ]
            for h in range(GROUP)
        ],
        axis=0,
    )


def probs_and_grads(scores, grad_probs, allowed):
    scores = scores * (SCALE * LOG2E)
    if allowed is not None:
        scores = jnp.where(allowed, scores, -jnp.inf)
    raised = jnp.exp2(scores - jnp.max(scores, axis=0, keepdims=True))
    probs = raised * (1.0 / jnp.sum(raised, axis=0, keepdims=True))
    delta = jnp.sum(probs * grad_probs, axis=0, keepdims=True)
    grad_scores = (probs * (grad_probs - delta) * SCALE).astype(BF16)
    return probs.astype(BF16), grad_scores


def plan_kernel(tokens, cap, tp, owner_ref, slot_ref, want_ref, first_ref):
    spans, per_span = owner_ref.shape
    devices, lanes = want_ref.shape
    row = lax.broadcasted_iota(jnp.int32, (devices, lanes), 0)
    lane = lax.broadcasted_iota(jnp.int32, (devices, lanes), 1)
    place = row * cap + (lane // tokens) % cap
    token = lane % tokens
    want = jnp.full((devices, lanes), -1, jnp.int32)
    owners = []
    for i in range(spans):
        for j in range(per_span):
            owner = owner_ref[i, j]
            rank = jnp.int32(0)
            for earlier in owners:
                rank = rank + jnp.where(earlier == owner, 1, 0)
            owners.append(owner)
            want = jnp.where(place == owner * cap + rank, slot_ref[i, j] * tokens + token, want)
            first_ref[i * per_span + j] = owner * (tp * cap * tokens) + rank * tokens
    want_ref[...] = want


def stage_kernel(k_ref, v_ref, sk_ref, sv_ref, store_ref, halo_ref):
    slots, tokens, features = k_ref.shape
    rows, columns = store_ref.shape
    kv_width = sk_ref.shape[1]
    for z in range(features // kv_width):
        cols = slice(z * kv_width, (z + 1) * kv_width)
        at = 2 * z * kv_width
        store_ref[:, at : at + kv_width] = k_ref[:, :, cols].reshape(rows, kv_width)
        store_ref[:, at + kv_width : at + 2 * kv_width] = v_ref[:, :, cols].reshape(rows, kv_width)
    halo_ref[:, :kv_width] = sk_ref[sk_ref.shape[0] - halo_ref.shape[0] :]
    halo_ref[:, kv_width:] = sv_ref[sv_ref.shape[0] - halo_ref.shape[0] :]


def pack_kernel(tp, me_ref, store_ref, *refs):
    *wanted_refs, send_ref, owned_ref = refs
    rows_each, both = send_ref.shape[1:]
    rows, lanes = owned_ref.shape
    me = me_ref[0]
    lane = lax.broadcasted_iota(jnp.int32, (1, lanes), 1)
    target = jnp.full((1, lanes), -1, jnp.int32)
    apart = 0
    for wanted_ref in wanted_refs:
        for i in range(wanted_ref.shape[0]):
            from_there = wanted_ref[i, pl.ds(me, 1), :]
            target = jnp.where(lane // rows_each == me ^ apart, from_there, target)
            apart += 1
    row = lax.broadcasted_iota(jnp.int32, (rows, lanes), 0)
    owned = jnp.where(row == target, 1.0, 0.0).astype(BF16)
    owned_ref[...] = owned
    picked = dot_tn(owned, store_ref[...]).astype(BF16)
    for s in range(lanes // rows_each):
        for z in range(tp):
            send_ref[s * tp + z] = picked[
                s * rows_each : (s + 1) * rows_each, z * both : (z + 1) * both
            ]


def self_kernel(
    tokens_each,
    rows_each,
    rank_ref,
    first_ref,
    q_ref,
    k_ref,
    v_ref,
    do_ref,
    halo_ref,
    out_ref,
    dq_ref,
    dkv_ref,
    back_ref,
    placed_ref,
    gather_ref,
):
    tokens, kv_width = k_ref.shape
    rows_all, rows_near = placed_ref.shape
    lane = lax.broadcasted_iota(jnp.int32, (1, rows_near), 1)
    within = lane % NEIGHBOUR_LENGTH
    place = (within // tokens_each) * rows_each + within % tokens_each
    row = lax.broadcasted_iota(jnp.int32, (NEIGHBOUR_LENGTH, rows_all), 0)
    col = lax.broadcasted_iota(jnp.int32, (NEIGHBOUR_LENGTH, rows_all), 1)
    offset = col - (row // tokens_each) * rows_each - row % tokens_each
    for r in range(rows_near // NEIGHBOUR_LENGTH):
        first = first_ref[r]
        place = place + jnp.where(lane // NEIGHBOUR_LENGTH == r, first, 0)
        gather_ref[r * NEIGHBOUR_LENGTH : (r + 1) * NEIGHBOUR_LENGTH] = jnp.where(
            offset == first, 1.0, 0.0
        ).astype(BF16)
    all_rows = lax.broadcasted_iota(jnp.int32, (rows_all, rows_near), 0)
    placed_ref[...] = jnp.where(all_rows == place, 1.0, 0.0).astype(BF16)
    block = WINDOW_KEYS
    blocks = tokens // block
    key_at = lax.broadcasted_iota(jnp.int32, (2 * block, GROUP * block), 0)
    query_at = lax.broadcasted_iota(jnp.int32, (2 * block, GROUP * block), 1) % block
    band = (key_at > query_at) & (key_at <= query_at + block)
    first_band = band & ((key_at >= block) | (rank_ref[0] > 0))
    for group in range(kv_width // HEAD_SIZE):
        cols = slice(group * HEAD_SIZE, (group + 1) * HEAD_SIZE)
        vcols = slice(kv_width + group * HEAD_SIZE, kv_width + (group + 1) * HEAD_SIZE)
        carried_k = carried_v = None
        for b in range(blocks):
            here = slice(b * block, (b + 1) * block)
            if b == 0:
                keys = jnp.concatenate([halo_ref[:, cols], k_ref[here, cols]], 0)
                values = jnp.concatenate([halo_ref[:, vcols], v_ref[here, cols]], 0)
            else:
                keys = k_ref[(b - 1) * block : (b + 1) * block, cols]
                values = v_ref[(b - 1) * block : (b + 1) * block, cols]
            query_rows = stacked_heads(q_ref, b * block, block, group)
            grad_rows = stacked_heads(do_ref, b * block, block, group)
            weights, grad_scores = probs_and_grads(
                dot_nt(keys, query_rows),
                dot_nt(values, grad_rows),
                first_band if b == 0 else band,
            )
            out = dot_tn(weights, values)
            dq = dot_tn(grad_scores, keys)
            for h in range(GROUP):
                head = slice((group * GROUP + h) * HEAD_SIZE, (group * GROUP + h + 1) * HEAD_SIZE)
                out_ref[here, head] = out[h * block : (h + 1) * block]
                dq_ref[here, head] = dq[h * block : (h + 1) * block]
            dk = dot_nn(grad_scores, query_rows)
            dv = dot_nn(weights, grad_rows)
            if b == 0:
                back_ref[:, cols] = dk[:block].astype(BF16)
                back_ref[:, vcols] = dv[:block].astype(BF16)
            else:
                before = slice((b - 1) * block, b * block)
                dkv_ref[before, cols] = carried_k + dk[:block]
                dkv_ref[before, vcols] = carried_v + dv[:block]
            carried_k, carried_v = dk[block:], dv[block:]
        last = slice((blocks - 1) * block, blocks * block)
        dkv_ref[last, cols] = carried_k
        dkv_ref[last, vcols] = carried_v


def cross_kernel(
    q_ref, do_ref, placed_ref, gather_ref, got_ref, send_ref, w_ref, ds_ref, near_ref, grad_ref
):
    all_devices, rows_each, both = got_ref.shape
    kv_width = both // 2
    groups = kv_width // HEAD_SIZE
    blocks, rows_span, columns = w_ref.shape
    near = dot_nn(gather_ref[...], got_ref[...].reshape(all_devices * rows_each, both)).astype(BF16)
    near_ref[...] = near
    queries, grads, scores, grad_probs = [], [], [], []
    for at in range(blocks):
        span, group = at // groups, at % groups
        here = slice(span * rows_span, (span + 1) * rows_span)
        cols = slice(group * HEAD_SIZE, (group + 1) * HEAD_SIZE)
        vcols = slice(kv_width + group * HEAD_SIZE, kv_width + (group + 1) * HEAD_SIZE)
        queries.append(stacked_heads(q_ref, span * SPAN_TOKENS, SPAN_TOKENS, group))
        grads.append(stacked_heads(do_ref, span * SPAN_TOKENS, SPAN_TOKENS, group))
        scores.append(dot_nt(near[here, cols], queries[at]))
        grad_probs.append(dot_nt(near[here, vcols], grads[at]))
    weights, grad_scores = probs_and_grads(
        jnp.concatenate(scores, axis=1), jnp.concatenate(grad_probs, axis=1), None
    )
    for at in range(blocks):
        span, group = at // groups, at % groups
        here = slice(span * rows_span, (span + 1) * rows_span)
        cols = slice(group * HEAD_SIZE, (group + 1) * HEAD_SIZE)
        vcols = slice(kv_width + group * HEAD_SIZE, kv_width + (group + 1) * HEAD_SIZE)
        part = slice(at * columns, (at + 1) * columns)
        w_ref[at] = weights[:, part]
        ds_ref[at] = grad_scores[:, part]
        grad_ref[here, cols] = dot_nn(grad_scores[:, part], queries[at]).astype(BF16)
        grad_ref[here, vcols] = dot_nn(weights[:, part], grads[at]).astype(BF16)
    send_ref[...] = dot_nn(placed_ref[...], grad_ref[...]).astype(BF16).reshape(send_ref.shape)


def join_kernel(
    w_ref, ds_ref, near_ref, out_ref, dq_ref, dkv_ref, back_ref, att_ref, qg_ref, kg_ref, vg_ref
):
    tokens, kv_width = kg_ref.shape
    groups = kv_width // HEAD_SIZE
    spans = w_ref.shape[0] // groups
    rows_span = near_ref.shape[0] // spans
    for span in range(spans):
        here = slice(span * rows_span, (span + 1) * rows_span)
        rows = slice(span * SPAN_TOKENS, (span + 1) * SPAN_TOKENS)
        for group in range(groups):
            cols = slice(group * HEAD_SIZE, (group + 1) * HEAD_SIZE)
            vcols = slice(kv_width + group * HEAD_SIZE, kv_width + (group + 1) * HEAD_SIZE)
            at = span * groups + group
            out = dot_tn(w_ref[at], near_ref[here, vcols])
            dq = dot_tn(ds_ref[at], near_ref[here, cols])
            for h in range(GROUP):
                head = slice((group * GROUP + h) * HEAD_SIZE, (group * GROUP + h + 1) * HEAD_SIZE)
                part = slice(h * SPAN_TOKENS, (h + 1) * SPAN_TOKENS)
                att_ref[rows, head] = (out_ref[rows, head] + out[part]).astype(BF16)
                qg_ref[rows, head] = (dq_ref[rows, head] + dq[part]).astype(BF16)
    halo = back_ref.shape[0]
    kg_ref[: tokens - halo] = dkv_ref[: tokens - halo, :kv_width].astype(BF16)
    vg_ref[: tokens - halo] = dkv_ref[: tokens - halo, kv_width:].astype(BF16)
    kg_ref[tokens - halo :] = (
        dkv_ref[tokens - halo :, :kv_width] + back_ref[:, :kv_width].astype(F32)
    ).astype(BF16)
    vg_ref[tokens - halo :] = (
        dkv_ref[tokens - halo :, kv_width:] + back_ref[:, kv_width:].astype(F32)
    ).astype(BF16)


def sum_kernel(tp, owned_ref, got_ref, kg_ref, vg_ref):
    all_devices, rows_each, both = got_ref.shape
    store_rows, tokens, _ = kg_ref.shape
    width = both // 2
    owned = owned_ref[...]
    for z in range(tp):
        got = jnp.concatenate([got_ref[d] for d in range(z, all_devices, tp)], axis=0)
        total = dot_nn(owned, got).astype(BF16)
        cols = slice(z * width, (z + 1) * width)
        kg_ref[:, :, cols] = total[:, :width].reshape(store_rows, tokens, width)
        vg_ref[:, :, cols] = total[:, width:].reshape(store_rows, tokens, width)


def cost(flops, bytes_accessed, transcendentals=0):
    return pl.CostEstimate(
        flops=flops, bytes_accessed=bytes_accessed, transcendentals=transcendentals
    )


def body(
    queries,
    sequence_keys,
    sequence_values,
    output_gradient,
    enc_keys,
    encoded_values,
    nbr_owner,
    nbr_slot,
):
    tokens_here, query_width = queries.shape
    kv_width = sequence_keys.shape[1]
    groups = kv_width // HEAD_SIZE
    devices = lax.axis_size("seq")
    tp = lax.axis_size("tp")
    spans, per_span = nbr_owner.shape
    requests = spans * per_span
    cap = max(2, 2 * requests // devices)
    tokens = enc_keys.shape[1]
    rows_near = requests * NEIGHBOUR_LENGTH
    rows_each = cap * tokens
    window = WINDOW_KEYS
    struct = jax.ShapeDtypeStruct

    store_rows = enc_keys.shape[0] * tokens
    lanes = devices * rows_each
    want, first = pl.pallas_call(
        functools.partial(plan_kernel, tokens, cap, tp),
        out_shape=(struct((devices, lanes), jnp.int32), struct((requests,), jnp.int32)),
        in_specs=[SMEM, SMEM],
        out_specs=(VMEM, SMEM),
        compiler_params=PARAMS,
        cost_estimate=cost(0, 10_000),
        name="plan_requests",
    )(nbr_owner, nbr_slot)
    pieces = [want[None]]
    step = 1
    while step < devices:
        known = jnp.concatenate(pieces, axis=0) if step > 1 else pieces[0]
        pieces.append(lax.ppermute(known, "seq", [(i, i ^ step) for i in range(devices)]))
        step *= 2

    store, halo = pl.pallas_call(
        stage_kernel,
        out_shape=(
            struct((store_rows, 2 * enc_keys.shape[2]), BF16),
            struct((window, 2 * kv_width), BF16),
        ),
        in_specs=[VMEM] * 4,
        out_specs=(VMEM,) * 2,
        compiler_params=PARAMS,
        cost_estimate=cost(0, 3_000_000),
        name="stage_store",
    )(enc_keys, encoded_values, sequence_keys, sequence_values)

    rank = lax.axis_index("seq").astype(jnp.int32).reshape(1)
    packed, owned = pl.pallas_call(
        functools.partial(pack_kernel, tp),
        out_shape=(
            struct((devices * tp, rows_each, 2 * kv_width), BF16),
            struct((store_rows, lanes), BF16),
        ),
        in_specs=[SMEM] + [VMEM] * (1 + len(pieces)),
        out_specs=(VMEM,) * 2,
        compiler_params=PARAMS,
        cost_estimate=cost(200_000_000, 2_000_000),
        name="pack_requests",
    )(rank, store, *pieces)
    packed, halo = lax.optimization_barrier((packed, halo))
    fetched = lax.all_to_all(packed, ("seq", "tp"), split_axis=0, concat_axis=0, tiled=True)
    halo = lax.ppermute(halo, "seq", [(i, i + 1) for i in range(devices - 1)])

    rows_all = devices * tp * rows_each
    self_out, self_dq, self_dkv, back, placed, gather = pl.pallas_call(
        functools.partial(self_kernel, tokens, rows_each),
        out_shape=(
            struct((tokens_here, query_width), F32),
            struct((tokens_here, query_width), F32),
            struct((tokens_here, 2 * kv_width), F32),
            struct((window, 2 * kv_width), BF16),
            struct((rows_all, rows_near), BF16),
            struct((rows_near, rows_all), BF16),
        ),
        in_specs=[SMEM] * 2 + [VMEM] * 5,
        out_specs=(VMEM,) * 6,
        compiler_params=PARAMS,
        cost_estimate=cost(1_600_000_000, 6_000_000, 1_000_000),
        name="self_attention",
    )(rank, first, queries, sequence_keys, sequence_values, output_gradient, halo)
    back = lax.ppermute(back, "seq", [(i + 1, i) for i in range(devices - 1)])

    blocks = spans * groups
    columns = GROUP * SPAN_TOKENS
    rows_span = per_span * NEIGHBOUR_LENGTH
    send, weights, grad_scores, near = pl.pallas_call(
        cross_kernel,
        out_shape=(
            struct((devices * tp, rows_each, 2 * kv_width), BF16),
            struct((blocks, rows_span, columns), BF16),
            struct((blocks, rows_span, columns), BF16),
            struct((rows_near, 2 * kv_width), BF16),
        ),
        in_specs=[VMEM] * 5,
        out_specs=(VMEM,) * 4,
        scratch_shapes=[pltpu.VMEM((rows_near, 2 * kv_width), BF16)],
        compiler_params=PARAMS,
        cost_estimate=cost(600_000_000, 3_000_000, 200_000),
        name="cross_attention",
    )(queries, output_gradient, placed, gather, fetched)
    returned = lax.all_to_all(send, ("seq", "tp"), split_axis=0, concat_axis=0, tiled=True)

    attended, query_gradient, key_gradient, value_gradient = pl.pallas_call(
        join_kernel,
        out_shape=(
            struct((tokens_here, query_width), BF16),
            struct((tokens_here, query_width), BF16),
            struct((tokens_here, kv_width), BF16),
            struct((tokens_here, kv_width), BF16),
        ),
        in_specs=[VMEM] * 7,
        out_specs=(VMEM,) * 4,
        compiler_params=PARAMS,
        cost_estimate=cost(300_000_000, 5_000_000),
        name="join_outputs",
    )(weights, grad_scores, near, self_out, self_dq, self_dkv, back)

    store_kgrad, store_vgrad = pl.pallas_call(
        functools.partial(sum_kernel, tp),
        out_shape=(struct(enc_keys.shape, BF16), struct(encoded_values.shape, BF16)),
        in_specs=[VMEM] * 2,
        out_specs=(VMEM,) * 2,
        compiler_params=PARAMS,
        cost_estimate=cost(200_000_000, 2_000_000),
        name="sum_store_gradients",
    )(owned, returned)

    return (
        attended,
        query_gradient,
        key_gradient,
        value_gradient,
        store_kgrad,
        store_vgrad,
    )


def solution(mesh):
    arguments = (P("seq", "tp"),) * 4 + (P("seq", "tp", None),) * 2 + (P("seq", None),) * 2
    results = (P("seq", "tp"),) * 4 + (P("seq", "tp", None),) * 2
    return jax.shard_map(
        body, mesh=mesh, in_specs=arguments, out_specs=results, check_vma=False
    )
```

```python
import functools
import math

import jax
import jax.numpy as jnp
from jax import lax
from jax.experimental import pallas as pl
from jax.experimental.pallas import tpu as pltpu
from jax.sharding import PartitionSpec as P

QUERY_HEADS = 32
KEY_VALUE_HEADS = 8
HEAD_SIZE = 128
SPAN_TOKENS = 64
NEIGHBOUR_COUNT = 4
NEIGHBOUR_LENGTH = 16
WINDOW_KEYS = 128
GROUP = QUERY_HEADS // KEY_VALUE_HEADS
SCALE = 1.0 / math.sqrt(HEAD_SIZE)
LOG2E = math.log2(math.e)

F32 = jnp.float32
BF16 = jnp.bfloat16
VMEM = pl.BlockSpec(memory_space=pltpu.VMEM)
SMEM = pl.BlockSpec(memory_space=pltpu.SMEM)
HBM = pl.BlockSpec(memory_space=pltpu.HBM)
LANES = 128
PARAMS = pltpu.CompilerParams(vmem_limit_bytes=16 * 1024 * 1024)


def dot_nn(a, b):
    return lax.dot_general(a, b, (((1,), (0,)), ((), ())), preferred_element_type=F32)


def dot_nt(a, b):
    return lax.dot_general(a, b, (((1,), (1,)), ((), ())), preferred_element_type=F32)


def dot_tn(a, b):
    return lax.dot_general(a, b, (((0,), (0,)), ((), ())), preferred_element_type=F32)


def stacked_heads(ref, first_row, rows, group):
    return jnp.concatenate(
        [
            ref[
                first_row : first_row + rows,
                (group * GROUP + h) * HEAD_SIZE : (group * GROUP + h + 1) * HEAD_SIZE,
            ]
            for h in range(GROUP)
        ],
        axis=0,
    )


def probs_and_grads(scores, grad_probs, allowed):
    scores = scores * (SCALE * LOG2E)
    if allowed is not None:
        scores = jnp.where(allowed, scores, -jnp.inf)
    raised = jnp.exp2(scores - jnp.max(scores, axis=0, keepdims=True))
    probs = raised * (1.0 / jnp.sum(raised, axis=0, keepdims=True))
    delta = jnp.sum(probs * grad_probs, axis=0, keepdims=True)
    grad_scores = (probs * (grad_probs - delta) * SCALE).astype(BF16)
    return probs.astype(BF16), grad_scores


def plan_kernel(
    tokens, cap, owner_hbm, slot_hbm, want_ref, owner_out, rank_out, owner_ref, slot_ref, sems
):
    copies = [
        pltpu.make_async_copy(owner_hbm, owner_ref, sems.at[0]),
        pltpu.make_async_copy(slot_hbm, slot_ref, sems.at[1]),
    ]
    for copy in copies:
        copy.start()
    spans, per_span = owner_ref.shape
    row = lax.broadcasted_iota(jnp.int32, want_ref.shape, 0)
    lane = lax.broadcasted_iota(jnp.int32, want_ref.shape, 1)
    place = row * cap + (lane // tokens) % cap
    token = lane % tokens
    want = jnp.full(want_ref.shape, -1, jnp.int32)
    for copy in copies:
        copy.wait()
    owners = []
    for i in range(spans):
        for j in range(per_span):
            owner = owner_ref[i, j]
            rank = jnp.int32(0)
            for earlier in owners:
                rank = rank + jnp.where(earlier == owner, 1, 0)
            owners.append(owner)
            want = jnp.where(place == owner * cap + rank, slot_ref[i, j] * tokens + token, want)
            owner_out[i * per_span + j] = owner
            rank_out[i * per_span + j] = rank
    want_ref[...] = want


def stage_kernel(
    rows_each, me_ref, owner_ref, rank_ref, k_ref, v_ref, sk_ref, sv_ref, store_ref, halo_ref, placed_ref
):
    slots, tokens, features = k_ref.shape
    rows, columns = store_ref.shape
    kv_width = sk_ref.shape[1]
    for z in range(features // kv_width):
        cols = slice(z * kv_width, (z + 1) * kv_width)
        at = 2 * z * kv_width
        store_ref[:, at : at + kv_width] = k_ref[:, :, cols].reshape(rows, kv_width)
        store_ref[:, at + kv_width : at + 2 * kv_width] = v_ref[:, :, cols].reshape(rows, kv_width)
    halo_ref[:, :kv_width] = sk_ref[sk_ref.shape[0] - halo_ref.shape[0] :]
    halo_ref[:, kv_width:] = sv_ref[sv_ref.shape[0] - halo_ref.shape[0] :]
    lanes, used = placed_ref.shape
    me = me_ref[0]
    lane = lax.broadcasted_iota(jnp.int32, (1, used), 1)
    place = lane % tokens
    for r in range(used // tokens):
        first = (owner_ref[r] ^ me) * rows_each + rank_ref[r] * tokens
        place = place + jnp.where(lane // tokens == r, first, 0)
    row = lax.broadcasted_iota(jnp.int32, (lanes, used), 0)
    placed_ref[...] = jnp.where(row == place, 1.0, 0.0).astype(BF16)


def pack_kernel(pieces, me_ref, store_ref, *refs):
    wanted_refs, send_refs, owned_ref = refs[:pieces], refs[pieces:-1], refs[-1]
    rows_each = send_refs[0].shape[0]
    rows, lanes = owned_ref.shape
    me = me_ref[0]
    width = wanted_refs[0].shape[2]
    lane = lax.broadcasted_iota(jnp.int32, (1, width), 1)
    parts = [jnp.full((1, width), -1, jnp.int32) for _ in range(lanes // width)]
    apart = 0
    for wanted_ref in wanted_refs:
        for i in range(wanted_ref.shape[0]):
            part, at = divmod(apart * rows_each, width)
            from_there = wanted_ref[i, pl.ds(me, 1), :]
            here = (lane >= at) & (lane < at + rows_each)
            parts[part] = jnp.where(here, from_there, parts[part])
            apart += 1
    target = jnp.concatenate(parts, axis=1)
    row = lax.broadcasted_iota(jnp.int32, (rows, lanes), 0)
    owned = jnp.where(row == target, 1.0, 0.0).astype(BF16)
    owned_ref[...] = owned
    picked = dot_tn(owned, store_ref[...]).astype(BF16)
    for at, send_ref in enumerate(send_refs):
        send_ref[...] = picked[at * rows_each : (at + 1) * rows_each]


def spread_kernel(tp, z_ref, placed_ref, *refs):
    got_refs, send_refs, near_ref = refs[: -tp - 1], refs[-tp - 1 : -1], refs[-1]
    both = send_refs[0].shape[1]
    got = jnp.concatenate([ref[...] for ref in got_refs], axis=0)
    near_ref[...] = dot_tn(placed_ref[...], got).astype(BF16)
    for apart, send_ref in enumerate(send_refs):
        start = pl.multiple_of((z_ref[0] ^ apart) * both, both)
        send_ref[...] = near_ref[:, pl.ds(start, both)]


def scatter_kernel(tp, z_ref, placed_ref, *refs):
    grad_refs, send_refs, all_ref = refs[:tp], refs[tp:-1], refs[-1]
    both = grad_refs[0].shape[1]
    rows_each = send_refs[0].shape[0]
    for apart, grad_ref in enumerate(grad_refs):
        start = pl.multiple_of((z_ref[0] ^ apart) * both, both)
        all_ref[:, pl.ds(start, both)] = grad_ref[...]
    rows = dot_nn(placed_ref[...], all_ref[...]).astype(BF16)
    for at, send_ref in enumerate(send_refs):
        send_ref[...] = rows[at * rows_each : (at + 1) * rows_each]


def self_kernel(
    rank_ref, q_ref, k_ref, v_ref, do_ref, halo_ref, out_ref, dq_ref, dkv_ref, back_ref
):
    tokens, kv_width = k_ref.shape
    block = WINDOW_KEYS
    blocks = tokens // block
    key_at = lax.broadcasted_iota(jnp.int32, (2 * block, GROUP * block), 0)
    query_at = lax.broadcasted_iota(jnp.int32, (2 * block, GROUP * block), 1) % block
    band = (key_at > query_at) & (key_at <= query_at + block)
    first_band = band & ((key_at >= block) | (rank_ref[0] > 0))
    for group in range(kv_width // HEAD_SIZE):
        cols = slice(group * HEAD_SIZE, (group + 1) * HEAD_SIZE)
        vcols = slice(kv_width + group * HEAD_SIZE, kv_width + (group + 1) * HEAD_SIZE)
        carried_k = carried_v = None
        for b in range(blocks):
            here = slice(b * block, (b + 1) * block)
            if b == 0:
                keys = jnp.concatenate([halo_ref[:, cols], k_ref[here, cols]], 0)
                values = jnp.concatenate([halo_ref[:, vcols], v_ref[here, cols]], 0)
            else:
                keys = k_ref[(b - 1) * block : (b + 1) * block, cols]
                values = v_ref[(b - 1) * block : (b + 1) * block, cols]
            query_rows = stacked_heads(q_ref, b * block, block, group)
            grad_rows = stacked_heads(do_ref, b * block, block, group)
            weights, grad_scores = probs_and_grads(
                dot_nt(keys, query_rows),
                dot_nt(values, grad_rows),
                first_band if b == 0 else band,
            )
            out = dot_tn(weights, values)
            dq = dot_tn(grad_scores, keys)
            for h in range(GROUP):
                head = slice((group * GROUP + h) * HEAD_SIZE, (group * GROUP + h + 1) * HEAD_SIZE)
                out_ref[here, head] = out[h * block : (h + 1) * block]
                dq_ref[here, head] = dq[h * block : (h + 1) * block]
            dk = dot_nn(grad_scores, query_rows)
            dv = dot_nn(weights, grad_rows)
            if b == 0:
                back_ref[:, cols] = dk[:block].astype(BF16)
                back_ref[:, vcols] = dv[:block].astype(BF16)
            else:
                before = slice((b - 1) * block, b * block)
                dkv_ref[before, cols] = carried_k + dk[:block]
                dkv_ref[before, vcols] = carried_v + dv[:block]
            carried_k, carried_v = dk[block:], dv[block:]
        last = slice((blocks - 1) * block, blocks * block)
        dkv_ref[last, cols] = carried_k
        dkv_ref[last, vcols] = carried_v


def span_rows(near_refs, span, rows, cols):
    return jnp.concatenate([ref[span * rows : (span + 1) * rows, cols] for ref in near_refs], axis=0)


def cross_kernel(tp, q_ref, do_ref, *refs):
    near_refs, grad_refs, w_ref, ds_ref = refs[:tp], refs[tp : 2 * tp], refs[2 * tp], refs[2 * tp + 1]
    kv_width = near_refs[0].shape[1] // 2
    groups = kv_width // HEAD_SIZE
    blocks, rows_span, columns = w_ref.shape
    rows = rows_span // tp
    queries, grads, scores, grad_probs = [], [], [], []
    for at in range(blocks):
        span, group = at // groups, at % groups
        cols = slice(group * HEAD_SIZE, (group + 1) * HEAD_SIZE)
        vcols = slice(kv_width + group * HEAD_SIZE, kv_width + (group + 1) * HEAD_SIZE)
        queries.append(stacked_heads(q_ref, span * SPAN_TOKENS, SPAN_TOKENS, group))
        grads.append(stacked_heads(do_ref, span * SPAN_TOKENS, SPAN_TOKENS, group))
        scores.append(dot_nt(span_rows(near_refs, span, rows, cols), queries[at]))
        grad_probs.append(dot_nt(span_rows(near_refs, span, rows, vcols), grads[at]))
    weights, grad_scores = probs_and_grads(
        jnp.concatenate(scores, axis=1), jnp.concatenate(grad_probs, axis=1), None
    )
    for at in range(blocks):
        span, group = at // groups, at % groups
        here = slice(span * rows, (span + 1) * rows)
        cols = slice(group * HEAD_SIZE, (group + 1) * HEAD_SIZE)
        vcols = slice(kv_width + group * HEAD_SIZE, kv_width + (group + 1) * HEAD_SIZE)
        part = slice(at * columns, (at + 1) * columns)
        w_ref[at] = weights[:, part]
        ds_ref[at] = grad_scores[:, part]
        dk = dot_nn(grad_scores[:, part], queries[at]).astype(BF16)
        dv = dot_nn(weights[:, part], grads[at]).astype(BF16)
        for apart, grad_ref in enumerate(grad_refs):
            grad_ref[here, cols] = dk[apart * rows : (apart + 1) * rows]
            grad_ref[here, vcols] = dv[apart * rows : (apart + 1) * rows]


def join_kernel(tp, w_ref, ds_ref, out_ref, dq_ref, dkv_ref, back_ref, *refs):
    near_refs, (att_ref, qg_ref, kg_ref, vg_ref) = refs[:tp], refs[tp:]
    tokens, kv_width = kg_ref.shape
    groups = kv_width // HEAD_SIZE
    blocks, rows_span, _ = w_ref.shape
    for span in range(blocks // groups):
        rows = slice(span * SPAN_TOKENS, (span + 1) * SPAN_TOKENS)
        for group in range(groups):
            cols = slice(group * HEAD_SIZE, (group + 1) * HEAD_SIZE)
            vcols = slice(kv_width + group * HEAD_SIZE, kv_width + (group + 1) * HEAD_SIZE)
            at = span * groups + group
            out = dot_tn(w_ref[at], span_rows(near_refs, span, rows_span // tp, vcols))
            dq = dot_tn(ds_ref[at], span_rows(near_refs, span, rows_span // tp, cols))
            for h in range(GROUP):
                head = slice((group * GROUP + h) * HEAD_SIZE, (group * GROUP + h + 1) * HEAD_SIZE)
                part = slice(h * SPAN_TOKENS, (h + 1) * SPAN_TOKENS)
                att_ref[rows, head] = (out_ref[rows, head] + out[part]).astype(BF16)
                qg_ref[rows, head] = (dq_ref[rows, head] + dq[part]).astype(BF16)
    halo = back_ref.shape[0]
    kg_ref[: tokens - halo] = dkv_ref[: tokens - halo, :kv_width].astype(BF16)
    vg_ref[: tokens - halo] = dkv_ref[: tokens - halo, kv_width:].astype(BF16)
    kg_ref[tokens - halo :] = (
        dkv_ref[tokens - halo :, :kv_width] + back_ref[:, :kv_width].astype(F32)
    ).astype(BF16)
    vg_ref[tokens - halo :] = (
        dkv_ref[tokens - halo :, kv_width:] + back_ref[:, kv_width:].astype(F32)
    ).astype(BF16)


def sum_kernel(tp, owned_ref, *refs):
    got_refs, (kg_ref, vg_ref) = refs[:-2], refs[-2:]
    store_rows, tokens, features = kg_ref.shape
    width = features // tp
    owned = owned_ref[...]
    got = jnp.concatenate([ref[...] for ref in got_refs], axis=0)
    for z in range(tp):
        total = dot_nn(owned, got[:, 2 * z * width : 2 * (z + 1) * width]).astype(BF16)
        cols = slice(z * width, (z + 1) * width)
        kg_ref[:, :, cols] = total[:, :width].reshape(store_rows, tokens, width)
        vg_ref[:, :, cols] = total[:, width:].reshape(store_rows, tokens, width)


def call(kernel, name, ins, outs, flops, bytes_accessed, scratch=(), scalars=0, places=None):
    return pl.pallas_call(
        kernel,
        out_shape=tuple(outs),
        in_specs=places or [SMEM] * scalars + [VMEM] * (len(ins) - scalars),
        out_specs=tuple(SMEM if len(out.shape) == 1 else VMEM for out in outs),
        scratch_shapes=list(scratch),
        compiler_params=PARAMS,
        cost_estimate=pl.CostEstimate(
            flops=flops, bytes_accessed=bytes_accessed, transcendentals=0
        ),
        name=name,
    )(*ins)


def swapped(block, axis, apart):
    return lax.ppermute(block, axis, [(i, i ^ apart) for i in range(lax.axis_size(axis))])


def body(
    queries,
    sequence_keys,
    sequence_values,
    output_gradient,
    enc_keys,
    encoded_values,
    nbr_owner,
    nbr_slot,
):
    tokens_here, query_width = queries.shape
    kv_width = sequence_keys.shape[1]
    both = 2 * kv_width
    groups = kv_width // HEAD_SIZE
    devices = lax.axis_size("seq")
    tp = lax.axis_size("tp")
    spans, per_span = nbr_owner.shape
    requests = spans * per_span
    cap = max(2, 2 * requests // devices)
    tokens = enc_keys.shape[1]
    rows_each = cap * tokens
    window = WINDOW_KEYS
    struct = jax.ShapeDtypeStruct
    store_rows = enc_keys.shape[0] * tokens
    lanes = devices * rows_each
    used = requests * tokens
    int32 = jnp.int32
    rank = lax.axis_index("seq").astype(int32).reshape(1)
    z_rank = lax.axis_index("tp").astype(int32).reshape(1)

    want, owner_of, rank_of = call(
        functools.partial(plan_kernel, tokens, cap),
        "plan_requests",
        (nbr_owner, nbr_slot),
        (
            struct((devices, min(lanes, LANES)), int32),
            struct((requests,), int32),
            struct((requests,), int32),
        ),
        0,
        10_000,
        scratch=[
            pltpu.SMEM(nbr_owner.shape, int32),
            pltpu.SMEM(nbr_slot.shape, int32),
            pltpu.SemaphoreType.DMA((2,)),
        ],
        places=[HBM, HBM],
    )
    pieces = [want[None]]
    step = 1
    while step < devices:
        known = jnp.concatenate(pieces, axis=0) if step > 1 else pieces[0]
        pieces.append(swapped(known, "seq", step))
        step *= 2

    store, halo, placed = call(
        functools.partial(stage_kernel, rows_each),
        "stage_store",
        (rank, owner_of, rank_of, enc_keys, encoded_values, sequence_keys, sequence_values),
        (
            struct((store_rows, 2 * enc_keys.shape[2]), BF16),
            struct((window, both), BF16),
            struct((lanes, used), BF16),
        ),
        0,
        3_000_000,
        scalars=3,
    )
    *sent, owned = call(
        functools.partial(pack_kernel, len(pieces)),
        "pack_requests",
        (rank, store, *pieces),
        [struct((rows_each, tp * both), BF16)] * devices + [struct((store_rows, lanes), BF16)],
        200_000_000,
        2_000_000,
        scalars=1,
    )
    sent, halo = lax.optimization_barrier((sent, halo))
    got = [sent[0]] + [swapped(sent[j], "seq", j) for j in range(1, devices)]
    halo = lax.ppermute(halo, "seq", [(i, i + 1) for i in range(devices - 1)])

    self_out, self_dq, self_dkv, back = call(
        self_kernel,
        "self_attention",
        (rank, queries, sequence_keys, sequence_values, output_gradient, halo),
        (
            struct((tokens_here, query_width), F32),
            struct((tokens_here, query_width), F32),
            struct((tokens_here, both), F32),
            struct((window, both), BF16),
        ),
        1_600_000_000,
        6_000_000,
        scalars=1,
    )

    spread = call(
        functools.partial(spread_kernel, tp),
        "spread_rows",
        (z_rank, placed, *got),
        [struct((used, both), BF16)] * tp,
        50_000_000,
        1_000_000,
        scratch=[pltpu.VMEM((used, tp * both), BF16)],
        scalars=1,
    )
    near = [spread[0]] + [swapped(spread[j], "tp", j) for j in range(1, tp)]

    blocks = spans * groups
    rows_span = per_span * NEIGHBOUR_LENGTH
    *grads, weights, grad_scores = call(
        functools.partial(cross_kernel, tp),
        "cross_attention",
        (queries, output_gradient, *near),
        [struct((used, both), BF16)] * tp
        + [struct((blocks, rows_span, GROUP * SPAN_TOKENS), BF16)] * 2,
        600_000_000,
        3_000_000,
    )
    grads = [grads[0]] + [swapped(grads[j], "tp", j) for j in range(1, tp)]
    back = lax.ppermute(back, "seq", [(i + 1, i) for i in range(devices - 1)])

    returned = call(
        functools.partial(scatter_kernel, tp),
        "scatter_gradients",
        (z_rank, placed, *grads),
        [struct((rows_each, tp * both), BF16)] * devices,
        50_000_000,
        1_000_000,
        scratch=[pltpu.VMEM((used, tp * both), BF16)],
        scalars=1,
    )
    returned = [returned[0]] + [swapped(returned[j], "seq", j) for j in range(1, devices)]

    attended, query_gradient, key_gradient, value_gradient = call(
        functools.partial(join_kernel, tp),
        "join_outputs",
        (weights, grad_scores, self_out, self_dq, self_dkv, back, *near),
        (
            struct((tokens_here, query_width), BF16),
            struct((tokens_here, query_width), BF16),
            struct((tokens_here, kv_width), BF16),
            struct((tokens_here, kv_width), BF16),
        ),
        300_000_000,
        5_000_000,
    )
    store_kgrad, store_vgrad = call(
        functools.partial(sum_kernel, tp),
        "sum_store_gradients",
        (owned, *returned),
        (struct(enc_keys.shape, BF16), struct(encoded_values.shape, BF16)),
        200_000_000,
        2_000_000,
    )
    return (
        attended,
        query_gradient,
        key_gradient,
        value_gradient,
        store_kgrad,
        store_vgrad,
    )


def solution(mesh):
    arguments = (P("seq", "tp"),) * 4 + (P("seq", "tp", None),) * 2 + (P("seq", None),) * 2
    results = (P("seq", "tp"),) * 4 + (P("seq", "tp", None),) * 2
    return jax.shard_map(
        body, mesh=mesh, in_specs=arguments, out_specs=results, check_vma=False
    )
```

```python
import functools
import math

import jax
import jax.numpy as jnp
from jax import lax
from jax.experimental import pallas as pl
from jax.experimental.pallas import tpu as pltpu
from jax.sharding import PartitionSpec as P

QUERY_HEADS = 32
KEY_VALUE_HEADS = 8
HEAD_SIZE = 128
SPAN_TOKENS = 64
NEIGHBOUR_COUNT = 4
NEIGHBOUR_LENGTH = 16
WINDOW_KEYS = 128
GROUP = QUERY_HEADS // KEY_VALUE_HEADS
SCALE = 1.0 / math.sqrt(HEAD_SIZE)
LOG2E = math.log2(math.e)

F32 = jnp.float32
BF16 = jnp.bfloat16
VMEM = pl.BlockSpec(memory_space=pltpu.VMEM)
SMEM = pl.BlockSpec(memory_space=pltpu.SMEM)
ANY = pl.BlockSpec(memory_space=pl.ANY)
LANES = 128


def dot_nn(a, b):
    return lax.dot_general(a, b, (((1,), (0,)), ((), ())), preferred_element_type=F32)


def dot_nt(a, b):
    return lax.dot_general(a, b, (((1,), (1,)), ((), ())), preferred_element_type=F32)


def dot_tn(a, b):
    return lax.dot_general(a, b, (((0,), (0,)), ((), ())), preferred_element_type=F32)


def stacked_heads(ref, first_row, rows, group):
    return jnp.concatenate(
        [
            ref[
                first_row : first_row + rows,
                (group * GROUP + h) * HEAD_SIZE : (group * GROUP + h + 1) * HEAD_SIZE,
            ]
            for h in range(GROUP)
        ],
        axis=0,
    )


def probs_and_grads(scores, grad_probs, allowed):
    scores = scores * (SCALE * LOG2E)
    if allowed is not None:
        scores = jnp.where(allowed, scores, -jnp.inf)
    raised = jnp.exp2(scores - jnp.max(scores, axis=0, keepdims=True))
    probs = raised * (1.0 / jnp.sum(raised, axis=0, keepdims=True))
    delta = jnp.sum(probs * grad_probs, axis=0, keepdims=True)
    grad_scores = (probs * (grad_probs - delta) * SCALE).astype(BF16)
    return probs.astype(BF16), grad_scores


def plan_kernel(tokens, cap, owner_any, slot_any, want_ref, owner_ref, slot_ref, sems):
    copies = [
        pltpu.make_async_copy(owner_any, owner_ref, sems.at[0]),
        pltpu.make_async_copy(slot_any, slot_ref, sems.at[1]),
    ]
    for copy in copies:
        copy.start()
    row = lax.broadcasted_iota(jnp.int32, want_ref.shape, 0)
    lane = lax.broadcasted_iota(jnp.int32, want_ref.shape, 1)
    place = row * cap + (lane // tokens) % cap
    token = lane % tokens
    want = jnp.full(want_ref.shape, -1, jnp.int32)
    for copy in copies:
        copy.wait()
    for i, j, owner, rank in ranked(owner_ref):
        want = jnp.where(place == owner * cap + rank, slot_ref[i, j] * tokens + token, want)
    want_ref[...] = want


def ranked(owner_ref):
    spans, per_span = owner_ref.shape
    owners, found = [], []
    for i in range(spans):
        for j in range(per_span):
            owner = owner_ref[i, j]
            rank = jnp.int32(0)
            for earlier in owners:
                rank = rank + jnp.where(earlier == owner, 1, 0)
            owners.append(owner)
            found.append((i, j, owner, rank))
    return found


def stage_kernel(
    rows_each,
    chunks,
    owner_any,
    k_any,
    v_any,
    sk_any,
    sv_any,
    store_ref,
    halo_ref,
    placed_ref,
    owner_ref,
    k_ref,
    v_ref,
    sems,
):
    slots, tokens, features = k_ref.shape
    kv_width = sk_any.shape[1]
    window = halo_ref.shape[0]
    tail = slice(sk_any.shape[0] - window, sk_any.shape[0])
    step = slots // chunks
    fetch_owner = pltpu.make_async_copy(owner_any, owner_ref, sems.at[2 * chunks + 2])
    fetch_owner.start()
    copies = []
    for i in range(chunks):
        part = slice(i * step, (i + 1) * step)
        copies.append(pltpu.make_async_copy(k_any.at[part], k_ref.at[part], sems.at[2 * i]))
        copies.append(pltpu.make_async_copy(v_any.at[part], v_ref.at[part], sems.at[2 * i + 1]))
    left, right = slice(0, kv_width), slice(kv_width, 2 * kv_width)
    copies.append(pltpu.make_async_copy(sk_any.at[tail], halo_ref.at[:, left], sems.at[2 * chunks]))
    copies.append(
        pltpu.make_async_copy(sv_any.at[tail], halo_ref.at[:, right], sems.at[2 * chunks + 1])
    )
    for copy in copies:
        copy.start()
    fetch_owner.wait()
    lanes, used = placed_ref.shape
    lane = lax.broadcasted_iota(jnp.int32, (1, used), 1)
    place = lane % tokens
    for r, (_, _, owner, rank) in enumerate(ranked(owner_ref)):
        place = place + jnp.where(lane // tokens == r, owner * rows_each + rank * tokens, 0)
    row = lax.broadcasted_iota(jnp.int32, (lanes, used), 0)
    placed_ref[...] = jnp.where(row == place, 1.0, 0.0).astype(BF16)
    for i in range(chunks):
        copies[2 * i].wait()
        copies[2 * i + 1].wait()
        part = slice(i * step, (i + 1) * step)
        rows = slice(i * step * tokens, (i + 1) * step * tokens)
        for z in range(features // kv_width):
            cols = slice(z * kv_width, (z + 1) * kv_width)
            at = 2 * z * kv_width
            for ref in (k_ref, v_ref):
                store_ref[rows, at : at + kv_width] = ref[part, :, cols].reshape(
                    step * tokens, kv_width
                )
                at += kv_width
    for copy in copies[2 * chunks :]:
        copy.wait()


def pack_kernel(sources, me_ref, store_ref, *refs):
    *wanted_refs, send_ref, owned_ref = refs
    devices, rows_each, columns = send_ref.shape
    rows, lanes = owned_ref.shape
    me = me_ref[0]
    width = wanted_refs[0].shape[2]
    lane = lax.broadcasted_iota(jnp.int32, (1, width), 1) // rows_each
    parts = [jnp.full((1, width), -1, jnp.int32) for _ in range(lanes // width)]
    entries = [(ref, i) for ref in wanted_refs for i in range(ref.shape[0])]
    for apart, (wanted_ref, i) in zip(sources, entries):
        from_there = wanted_ref[i, pl.ds(me, 1), :]
        for p in range(len(parts)):
            here = lane + p * (width // rows_each) == me ^ apart
            parts[p] = jnp.where(here, from_there, parts[p])
    target = jnp.concatenate(parts, axis=1)
    row = lax.broadcasted_iota(jnp.int32, (rows, lanes), 0)
    owned = jnp.where(row == target, 1.0, 0.0).astype(BF16)
    owned_ref[...] = owned
    picked = dot_tn(owned, store_ref[...]).astype(BF16)
    send_ref[...] = picked.reshape(devices, rows_each, columns)


def spread_kernel(tp, z_ref, placed_ref, got_ref, *refs):
    send_refs, near_ref = refs[:-1], refs[-1]
    both = send_refs[0].shape[1]
    got = got_ref[...].reshape(placed_ref.shape[0], tp * both)
    near_ref[...] = dot_tn(placed_ref[...], got).astype(BF16)
    for apart, send_ref in zip(distances(tp), send_refs):
        start = pl.multiple_of((z_ref[0] ^ apart) * both, both)
        send_ref[...] = near_ref[:, pl.ds(start, both)]


def scatter_kernel(tp, z_ref, placed_ref, *refs):
    grad_refs, (send_ref, all_ref) = refs[:tp], refs[tp:]
    both = grad_refs[0].shape[1]
    for apart, grad_ref in zip(distances(tp), grad_refs):
        start = pl.multiple_of((z_ref[0] ^ apart) * both, both)
        all_ref[:, pl.ds(start, both)] = grad_ref[...]
    send_ref[...] = dot_nn(placed_ref[...], all_ref[...]).astype(BF16).reshape(send_ref.shape)


def self_kernel(
    rank_ref, q_ref, k_ref, v_ref, do_ref, halo_ref, out_ref, dq_ref, dkv_ref, back_ref
):
    tokens, kv_width = k_ref.shape
    block = WINDOW_KEYS
    blocks = tokens // block
    key_at = lax.broadcasted_iota(jnp.int32, (2 * block, GROUP * block), 0)
    query_at = lax.broadcasted_iota(jnp.int32, (2 * block, GROUP * block), 1) % block
    band = (key_at > query_at) & (key_at <= query_at + block)
    first_band = band & ((key_at >= block) | (rank_ref[0] > 0))
    for group in range(kv_width // HEAD_SIZE):
        cols = slice(group * HEAD_SIZE, (group + 1) * HEAD_SIZE)
        vcols = slice(kv_width + group * HEAD_SIZE, kv_width + (group + 1) * HEAD_SIZE)
        carried_k = carried_v = None
        for b in range(blocks):
            here = slice(b * block, (b + 1) * block)
            if b == 0:
                keys = jnp.concatenate([halo_ref[:, cols], k_ref[here, cols]], 0)
                values = jnp.concatenate([halo_ref[:, vcols], v_ref[here, cols]], 0)
            else:
                keys = k_ref[(b - 1) * block : (b + 1) * block, cols]
                values = v_ref[(b - 1) * block : (b + 1) * block, cols]
            query_rows = stacked_heads(q_ref, b * block, block, group)
            grad_rows = stacked_heads(do_ref, b * block, block, group)
            weights, grad_scores = probs_and_grads(
                dot_nt(keys, query_rows),
                dot_nt(values, grad_rows),
                first_band if b == 0 else band,
            )
            out = dot_tn(weights, values)
            dq = dot_tn(grad_scores, keys)
            for h in range(GROUP):
                head = slice((group * GROUP + h) * HEAD_SIZE, (group * GROUP + h + 1) * HEAD_SIZE)
                out_ref[here, head] = out[h * block : (h + 1) * block]
                dq_ref[here, head] = dq[h * block : (h + 1) * block]
            dk = dot_nn(grad_scores, query_rows)
            dv = dot_nn(weights, grad_rows)
            if b == 0:
                back_ref[:, cols] = dk[:block].astype(BF16)
                back_ref[:, vcols] = dv[:block].astype(BF16)
            else:
                before = slice((b - 1) * block, b * block)
                dkv_ref[before, cols] = carried_k + dk[:block]
                dkv_ref[before, vcols] = carried_v + dv[:block]
            carried_k, carried_v = dk[block:], dv[block:]
        last = slice((blocks - 1) * block, blocks * block)
        dkv_ref[last, cols] = carried_k
        dkv_ref[last, vcols] = carried_v


def span_rows(near_refs, span, rows, cols):
    return jnp.concatenate([ref[span * rows : (span + 1) * rows, cols] for ref in near_refs], axis=0)


def cross_kernel(tp, q_ref, do_ref, *refs):
    near_refs, grad_refs, w_ref, ds_ref = refs[:tp], refs[tp : 2 * tp], refs[2 * tp], refs[2 * tp + 1]
    kv_width = near_refs[0].shape[1] // 2
    groups = kv_width // HEAD_SIZE
    blocks, rows_span, columns = w_ref.shape
    rows = rows_span // tp
    queries, grads, scores, grad_probs = [], [], [], []
    for at in range(blocks):
        span, group = at // groups, at % groups
        cols = slice(group * HEAD_SIZE, (group + 1) * HEAD_SIZE)
        vcols = slice(kv_width + group * HEAD_SIZE, kv_width + (group + 1) * HEAD_SIZE)
        queries.append(stacked_heads(q_ref, span * SPAN_TOKENS, SPAN_TOKENS, group))
        grads.append(stacked_heads(do_ref, span * SPAN_TOKENS, SPAN_TOKENS, group))
        scores.append(dot_nt(span_rows(near_refs, span, rows, cols), queries[at]))
        grad_probs.append(dot_nt(span_rows(near_refs, span, rows, vcols), grads[at]))
    weights, grad_scores = probs_and_grads(
        jnp.concatenate(scores, axis=1), jnp.concatenate(grad_probs, axis=1), None
    )
    for at in range(blocks):
        span, group = at // groups, at % groups
        here = slice(span * rows, (span + 1) * rows)
        cols = slice(group * HEAD_SIZE, (group + 1) * HEAD_SIZE)
        vcols = slice(kv_width + group * HEAD_SIZE, kv_width + (group + 1) * HEAD_SIZE)
        part = slice(at * columns, (at + 1) * columns)
        w_ref[at] = weights[:, part]
        ds_ref[at] = grad_scores[:, part]
        dk = dot_nn(grad_scores[:, part], queries[at]).astype(BF16)
        dv = dot_nn(weights[:, part], grads[at]).astype(BF16)
        for i, grad_ref in enumerate(grad_refs):
            grad_ref[here, cols] = dk[i * rows : (i + 1) * rows]
            grad_ref[here, vcols] = dv[i * rows : (i + 1) * rows]


def join_kernel(tp, w_ref, ds_ref, out_ref, dq_ref, dkv_ref, back_ref, *refs):
    near_refs, (att_ref, qg_ref, kg_ref, vg_ref) = refs[:tp], refs[tp:]
    tokens, kv_width = kg_ref.shape
    groups = kv_width // HEAD_SIZE
    blocks, rows_span, _ = w_ref.shape
    for span in range(blocks // groups):
        rows = slice(span * SPAN_TOKENS, (span + 1) * SPAN_TOKENS)
        for group in range(groups):
            cols = slice(group * HEAD_SIZE, (group + 1) * HEAD_SIZE)
            vcols = slice(kv_width + group * HEAD_SIZE, kv_width + (group + 1) * HEAD_SIZE)
            at = span * groups + group
            out = dot_tn(w_ref[at], span_rows(near_refs, span, rows_span // tp, vcols))
            dq = dot_tn(ds_ref[at], span_rows(near_refs, span, rows_span // tp, cols))
            for h in range(GROUP):
                head = slice((group * GROUP + h) * HEAD_SIZE, (group * GROUP + h + 1) * HEAD_SIZE)
                part = slice(h * SPAN_TOKENS, (h + 1) * SPAN_TOKENS)
                att_ref[rows, head] = (out_ref[rows, head] + out[part]).astype(BF16)
                qg_ref[rows, head] = (dq_ref[rows, head] + dq[part]).astype(BF16)
    halo = back_ref.shape[0]
    kg_ref[: tokens - halo] = dkv_ref[: tokens - halo, :kv_width].astype(BF16)
    vg_ref[: tokens - halo] = dkv_ref[: tokens - halo, kv_width:].astype(BF16)
    kg_ref[tokens - halo :] = (
        dkv_ref[tokens - halo :, :kv_width] + back_ref[:, :kv_width].astype(F32)
    ).astype(BF16)
    vg_ref[tokens - halo :] = (
        dkv_ref[tokens - halo :, kv_width:] + back_ref[:, kv_width:].astype(F32)
    ).astype(BF16)


def sum_kernel(tp, owned_ref, got_ref, kg_ref, vg_ref):
    store_rows, tokens, features = kg_ref.shape
    width = features // tp
    owned = owned_ref[...]
    got = got_ref[...].reshape(owned.shape[1], 2 * features)
    for z in range(tp):
        total = dot_nn(owned, got[:, 2 * z * width : 2 * (z + 1) * width]).astype(BF16)
        cols = slice(z * width, (z + 1) * width)
        kg_ref[:, :, cols] = total[:, :width].reshape(store_rows, tokens, width)
        vg_ref[:, :, cols] = total[:, width:].reshape(store_rows, tokens, width)


def call(kernel, name, ins, outs, flops, bytes_accessed, scratch=(), scalars=0, fetched=0):
    direct = len(ins) - fetched
    ins = ins[:direct] + tuple(
        pltpu.with_memory_space_constraint(each, pltpu.HBM) for each in ins[direct:]
    )
    return pl.pallas_call(
        kernel,
        out_shape=tuple(outs),
        in_specs=[SMEM] * scalars + [VMEM] * (direct - scalars) + [ANY] * fetched,
        out_specs=tuple(SMEM if len(out.shape) == 1 else VMEM for out in outs),
        scratch_shapes=list(scratch),
        compiler_params=pltpu.CompilerParams(vmem_limit_bytes=16 * 1024 * 1024),
        cost_estimate=pl.CostEstimate(
            flops=flops, bytes_accessed=bytes_accessed, transcendentals=0
        ),
        name=name,
    )(*ins)


def swapped(block, axis, apart):
    return lax.ppermute(block, axis, [(i, i ^ apart) for i in range(lax.axis_size(axis))])


def distances(tp):
    return [0] + sorted(range(1, tp), key=lambda j: (j < 2, j))


def exchanged(blocks):
    apart = distances(len(blocks))
    return [blocks[0]] + [swapped(b, "tp", j) for b, j in zip(blocks[1:], apart[1:])]


def body(
    queries,
    sequence_keys,
    sequence_values,
    output_gradient,
    enc_keys,
    encoded_values,
    nbr_owner,
    nbr_slot,
):
    tokens_here, query_width = queries.shape
    kv_width = sequence_keys.shape[1]
    both = 2 * kv_width
    groups = kv_width // HEAD_SIZE
    devices = lax.axis_size("seq")
    tp = lax.axis_size("tp")
    spans, per_span = nbr_owner.shape
    requests = spans * per_span
    cap = max(2, 2 * requests // devices)
    tokens = enc_keys.shape[1]
    rows_each = cap * tokens
    window = WINDOW_KEYS
    struct = jax.ShapeDtypeStruct
    store_rows = enc_keys.shape[0] * tokens
    lanes = devices * rows_each
    used = requests * tokens
    int32 = jnp.int32
    rank = lax.axis_index("seq").astype(int32).reshape(1)
    z_rank = lax.axis_index("tp").astype(int32).reshape(1)

    (want,) = call(
        functools.partial(plan_kernel, tokens, cap),
        "plan_requests",
        (nbr_owner, nbr_slot),
        (struct((devices, min(lanes, LANES)), int32),),
        0,
        100_000,
        scratch=[
            pltpu.SMEM(nbr_owner.shape, int32),
            pltpu.SMEM(nbr_slot.shape, int32),
            pltpu.SemaphoreType.DMA((2,)),
        ],
        fetched=2,
    )
    known, step = want[None], 1
    while devices // step > 4:
        known = jnp.concatenate([known, swapped(known, "seq", step)], axis=0)
        step *= 2
    pieces = [known] + [swapped(known, "seq", far) for far in range(step, devices, step)]
    sources = list(range(devices))

    chunks = 4
    store, halo, placed = call(
        functools.partial(stage_kernel, rows_each, chunks),
        "stage_store",
        (nbr_owner, enc_keys, encoded_values, sequence_keys, sequence_values),
        (
            struct((store_rows, 2 * enc_keys.shape[2]), BF16),
            struct((window, both), BF16),
            struct((lanes, used), BF16),
        ),
        0,
        3_000_000,
        scratch=[
            pltpu.SMEM(nbr_owner.shape, int32),
            pltpu.VMEM(enc_keys.shape, BF16),
            pltpu.VMEM(encoded_values.shape, BF16),
            pltpu.SemaphoreType.DMA((2 * chunks + 3,)),
        ],
        fetched=5,
    )
    sent, owned = call(
        functools.partial(pack_kernel, sources),
        "pack_requests",
        (rank, store, *pieces),
        (struct((devices, rows_each, tp * both), BF16), struct((store_rows, lanes), BF16)),
        200_000_000,
        2_000_000,
        scalars=1,
    )
    sent, halo = lax.optimization_barrier((sent, halo))
    got = lax.all_to_all(sent, "seq", split_axis=0, concat_axis=0, tiled=True)
    halo = lax.ppermute(halo, "seq", [(i, i + 1) for i in range(devices - 1)])

    self_out, self_dq, self_dkv, back = call(
        self_kernel,
        "self_attention",
        (rank, queries, sequence_keys, sequence_values, output_gradient, halo),
        (
            struct((tokens_here, query_width), F32),
            struct((tokens_here, query_width), F32),
            struct((tokens_here, both), F32),
            struct((window, both), BF16),
        ),
        1_600_000_000,
        6_000_000,
        scalars=1,
    )

    got, self_out, self_dq, self_dkv, back = lax.optimization_barrier(
        (got, self_out, self_dq, self_dkv, back)
    )
    spread = call(
        functools.partial(spread_kernel, tp),
        "spread_rows",
        (z_rank, placed, got),
        [struct((used, both), BF16)] * tp,
        50_000_000,
        1_000_000,
        scratch=[pltpu.VMEM((used, tp * both), BF16)],
        scalars=1,
    )
    near = exchanged(spread)

    blocks = spans * groups
    rows_span = per_span * NEIGHBOUR_LENGTH
    *grads, weights, grad_scores = call(
        functools.partial(cross_kernel, tp),
        "cross_attention",
        (queries, output_gradient, *near),
        [struct((used, both), BF16)] * tp
        + [struct((blocks, rows_span, GROUP * SPAN_TOKENS), BF16)] * 2,
        600_000_000,
        3_000_000,
    )
    grads = exchanged(grads)
    back = lax.ppermute(back, "seq", [(i + 1, i) for i in range(devices - 1)])

    (returned,) = call(
        functools.partial(scatter_kernel, tp),
        "scatter_gradients",
        (z_rank, placed, *grads),
        (struct((devices, rows_each, tp * both), BF16),),
        50_000_000,
        1_000_000,
        scratch=[pltpu.VMEM((used, tp * both), BF16)],
        scalars=1,
    )
    returned, weights = lax.optimization_barrier((returned, weights))
    returned = lax.all_to_all(returned, "seq", split_axis=0, concat_axis=0, tiled=True)

    attended, query_gradient, key_gradient, value_gradient = call(
        functools.partial(join_kernel, tp),
        "join_outputs",
        (weights, grad_scores, self_out, self_dq, self_dkv, back, *near),
        (
            struct((tokens_here, query_width), BF16),
            struct((tokens_here, query_width), BF16),
            struct((tokens_here, kv_width), BF16),
            struct((tokens_here, kv_width), BF16),
        ),
        300_000_000,
        5_000_000,
    )
    store_kgrad, store_vgrad = call(
        functools.partial(sum_kernel, tp),
        "sum_store_gradients",
        (owned, returned),
        (struct(enc_keys.shape, BF16), struct(encoded_values.shape, BF16)),
        200_000_000,
        2_000_000,
    )
    return (
        attended,
        query_gradient,
        key_gradient,
        value_gradient,
        store_kgrad,
        store_vgrad,
    )


def solution(mesh):
    arguments = (P("seq", "tp"),) * 4 + (P("seq", "tp", None),) * 2 + (P("seq", None),) * 2
    results = (P("seq", "tp"),) * 4 + (P("seq", "tp", None),) * 2
    return jax.shard_map(
        body, mesh=mesh, in_specs=arguments, out_specs=results, check_vma=False
    )
```

```python
import functools
import math

import jax
import jax.numpy as jnp
from jax import lax
from jax.experimental import pallas as pl
from jax.experimental.pallas import tpu as pltpu
from jax.sharding import PartitionSpec as P

QUERY_HEADS = 32
KEY_VALUE_HEADS = 8
HEAD_SIZE = 128
SPAN_TOKENS = 64
NEIGHBOUR_COUNT = 4
NEIGHBOUR_LENGTH = 16
WINDOW_KEYS = 128
GROUP = QUERY_HEADS // KEY_VALUE_HEADS
SCALE = 1.0 / math.sqrt(HEAD_SIZE)
LOG2E = math.log2(math.e)

F32 = jnp.float32
BF16 = jnp.bfloat16
VMEM = pl.BlockSpec(memory_space=pltpu.VMEM)
SMEM = pl.BlockSpec(memory_space=pltpu.SMEM)
ANY = pl.BlockSpec(memory_space=pl.ANY)
LANES = 128


def dot_nn(a, b):
    return lax.dot_general(a, b, (((1,), (0,)), ((), ())), preferred_element_type=F32)


def dot_nt(a, b):
    return lax.dot_general(a, b, (((1,), (1,)), ((), ())), preferred_element_type=F32)


def dot_tn(a, b):
    return lax.dot_general(a, b, (((0,), (0,)), ((), ())), preferred_element_type=F32)


def stacked_heads(ref, first_row, rows, group):
    return jnp.concatenate(
        [
            ref[
                first_row : first_row + rows,
                (group * GROUP + h) * HEAD_SIZE : (group * GROUP + h + 1) * HEAD_SIZE,
            ]
            for h in range(GROUP)
        ],
        axis=0,
    )


def probs_and_grads(scores, grad_probs, allowed):
    scores = scores * (SCALE * LOG2E)
    if allowed is not None:
        scores = jnp.where(allowed, scores, -jnp.inf)
    raised = jnp.exp2(scores - jnp.max(scores, axis=0, keepdims=True))
    probs = raised * (1.0 / jnp.sum(raised, axis=0, keepdims=True))
    delta = jnp.sum(probs * grad_probs, axis=0, keepdims=True)
    grad_scores = (probs * (grad_probs - delta) * SCALE).astype(BF16)
    return probs.astype(BF16), grad_scores


def plan_kernel(tokens, cap, owner_any, slot_any, want_ref, owner_ref, slot_ref, sems):
    copies = [
        pltpu.make_async_copy(owner_any, owner_ref, sems.at[0]),
        pltpu.make_async_copy(slot_any, slot_ref, sems.at[1]),
    ]
    for copy in copies:
        copy.start()
    row = lax.broadcasted_iota(jnp.int32, want_ref.shape, 0)
    lane = lax.broadcasted_iota(jnp.int32, want_ref.shape, 1)
    place = row * cap + (lane // tokens) % cap
    token = lane % tokens
    want = jnp.full(want_ref.shape, -1, jnp.int32)
    for copy in copies:
        copy.wait()
    for i, j, owner, rank in ranked(owner_ref):
        want = jnp.where(place == owner * cap + rank, slot_ref[i, j] * tokens + token, want)
    want_ref[...] = want


def ranked(owner_ref):
    spans, per_span = owner_ref.shape
    owners, found = [], []
    for i in range(spans):
        for j in range(per_span):
            owner = owner_ref[i, j]
            rank = jnp.int32(0)
            for earlier in owners:
                rank = rank + jnp.where(earlier == owner, 1, 0)
            owners.append(owner)
            found.append((i, j, owner, rank))
    return found


def stage_kernel(
    rows_each,
    chunks,
    me_ref,
    owner_any,
    k_any,
    v_any,
    sk_any,
    sv_any,
    store_ref,
    halo_ref,
    placed_ref,
    owner_ref,
    k_ref,
    v_ref,
    sems,
):
    slots, tokens, features = k_ref.shape
    kv_width = sk_any.shape[1]
    window = halo_ref.shape[0]
    tail = slice(sk_any.shape[0] - window, sk_any.shape[0])
    step = slots // chunks
    fetch_owner = pltpu.make_async_copy(owner_any, owner_ref, sems.at[2 * chunks + 2])
    fetch_owner.start()
    copies = []
    for i in range(chunks):
        part = slice(i * step, (i + 1) * step)
        copies.append(pltpu.make_async_copy(k_any.at[part], k_ref.at[part], sems.at[2 * i]))
        copies.append(pltpu.make_async_copy(v_any.at[part], v_ref.at[part], sems.at[2 * i + 1]))
    left, right = slice(0, kv_width), slice(kv_width, 2 * kv_width)
    copies.append(pltpu.make_async_copy(sk_any.at[tail], halo_ref.at[:, left], sems.at[2 * chunks]))
    copies.append(
        pltpu.make_async_copy(sv_any.at[tail], halo_ref.at[:, right], sems.at[2 * chunks + 1])
    )
    for copy in copies:
        copy.start()
    fetch_owner.wait()
    me = me_ref[0]
    lanes, used = placed_ref.shape
    lane = lax.broadcasted_iota(jnp.int32, (1, used), 1)
    place = lane % tokens
    for r, (_, _, owner, rank) in enumerate(ranked(owner_ref)):
        place = place + jnp.where(lane // tokens == r, (owner ^ me) * rows_each + rank * tokens, 0)
    row = lax.broadcasted_iota(jnp.int32, (lanes, used), 0)
    placed_ref[...] = jnp.where(row == place, 1.0, 0.0).astype(BF16)
    for i in range(chunks):
        copies[2 * i].wait()
        copies[2 * i + 1].wait()
        part = slice(i * step, (i + 1) * step)
        rows = slice(i * step * tokens, (i + 1) * step * tokens)
        for z in range(features // kv_width):
            cols = slice(z * kv_width, (z + 1) * kv_width)
            at = 2 * z * kv_width
            for ref in (k_ref, v_ref):
                store_ref[rows, at : at + kv_width] = ref[part, :, cols].reshape(
                    step * tokens, kv_width
                )
                at += kv_width
    for copy in copies[2 * chunks :]:
        copy.wait()


def pack_kernel(pieces, me_ref, store_ref, *refs):
    wanted_refs, send_refs, owned_ref = refs[:pieces], refs[pieces:-1], refs[-1]
    rows_each = send_refs[0].shape[0]
    rows, lanes = owned_ref.shape
    me = me_ref[0]
    width = wanted_refs[0].shape[2]
    lane = lax.broadcasted_iota(jnp.int32, (1, width), 1)
    parts = [jnp.full((1, width), -1, jnp.int32) for _ in range(lanes // width)]
    entries = [(ref, i) for ref in wanted_refs for i in range(ref.shape[0])]
    for apart, (wanted_ref, i) in enumerate(entries):
        part, at = divmod(apart * rows_each, width)
        from_there = wanted_ref[i, pl.ds(me, 1), :]
        here = (lane >= at) & (lane < at + rows_each)
        parts[part] = jnp.where(here, from_there, parts[part])
    target = jnp.concatenate(parts, axis=1)
    row = lax.broadcasted_iota(jnp.int32, (rows, lanes), 0)
    owned = jnp.where(row == target, 1.0, 0.0).astype(BF16)
    owned_ref[...] = owned
    picked = dot_tn(owned, store_ref[...]).astype(BF16)
    for at, send_ref in enumerate(send_refs):
        send_ref[...] = picked[at * rows_each : (at + 1) * rows_each]


def spread_kernel(tp, z_ref, placed_ref, *refs):
    got_refs, send_refs, near_ref = refs[: -tp - 1], refs[-tp - 1 : -1], refs[-1]
    both = send_refs[0].shape[1]
    got = jnp.concatenate([ref[...] for ref in got_refs], axis=0)
    near_ref[...] = dot_tn(placed_ref[...], got).astype(BF16)
    for apart, send_ref in zip(distances(tp), send_refs):
        start = pl.multiple_of((z_ref[0] ^ apart) * both, both)
        send_ref[...] = near_ref[:, pl.ds(start, both)]


def scatter_kernel(tp, z_ref, placed_ref, *refs):
    grad_refs, send_refs, all_ref = refs[:tp], refs[tp:-1], refs[-1]
    both = grad_refs[0].shape[1]
    rows_each = send_refs[0].shape[0]
    for apart, grad_ref in zip(distances(tp), grad_refs):
        start = pl.multiple_of((z_ref[0] ^ apart) * both, both)
        all_ref[:, pl.ds(start, both)] = grad_ref[...]
    rows = dot_nn(placed_ref[...], all_ref[...]).astype(BF16)
    for at, send_ref in enumerate(send_refs):
        send_ref[...] = rows[at * rows_each : (at + 1) * rows_each]


def self_kernel(
    rank_ref, q_ref, k_ref, v_ref, do_ref, halo_ref, out_ref, dq_ref, dkv_ref, back_ref
):
    tokens, kv_width = k_ref.shape
    block = WINDOW_KEYS
    blocks = tokens // block
    key_at = lax.broadcasted_iota(jnp.int32, (2 * block, GROUP * block), 0)
    query_at = lax.broadcasted_iota(jnp.int32, (2 * block, GROUP * block), 1) % block
    band = (key_at > query_at) & (key_at <= query_at + block)
    first_band = band & ((key_at >= block) | (rank_ref[0] > 0))
    for group in range(kv_width // HEAD_SIZE):
        cols = slice(group * HEAD_SIZE, (group + 1) * HEAD_SIZE)
        vcols = slice(kv_width + group * HEAD_SIZE, kv_width + (group + 1) * HEAD_SIZE)
        carried_k = carried_v = None
        for b in range(blocks):
            here = slice(b * block, (b + 1) * block)
            if b == 0:
                keys = jnp.concatenate([halo_ref[:, cols], k_ref[here, cols]], 0)
                values = jnp.concatenate([halo_ref[:, vcols], v_ref[here, cols]], 0)
            else:
                keys = k_ref[(b - 1) * block : (b + 1) * block, cols]
                values = v_ref[(b - 1) * block : (b + 1) * block, cols]
            query_rows = stacked_heads(q_ref, b * block, block, group)
            grad_rows = stacked_heads(do_ref, b * block, block, group)
            weights, grad_scores = probs_and_grads(
                dot_nt(keys, query_rows),
                dot_nt(values, grad_rows),
                first_band if b == 0 else band,
            )
            out = dot_tn(weights, values)
            dq = dot_tn(grad_scores, keys)
            for h in range(GROUP):
                head = slice((group * GROUP + h) * HEAD_SIZE, (group * GROUP + h + 1) * HEAD_SIZE)
                out_ref[here, head] = out[h * block : (h + 1) * block]
                dq_ref[here, head] = dq[h * block : (h + 1) * block]
            dk = dot_nn(grad_scores, query_rows)
            dv = dot_nn(weights, grad_rows)
            if b == 0:
                back_ref[:, cols] = dk[:block].astype(BF16)
                back_ref[:, vcols] = dv[:block].astype(BF16)
            else:
                before = slice((b - 1) * block, b * block)
                dkv_ref[before, cols] = carried_k + dk[:block]
                dkv_ref[before, vcols] = carried_v + dv[:block]
            carried_k, carried_v = dk[block:], dv[block:]
        last = slice((blocks - 1) * block, blocks * block)
        dkv_ref[last, cols] = carried_k
        dkv_ref[last, vcols] = carried_v


def span_rows(near_refs, span, rows, cols):
    return jnp.concatenate([ref[span * rows : (span + 1) * rows, cols] for ref in near_refs], axis=0)


def cross_kernel(tp, q_ref, do_ref, *refs):
    near_refs, grad_refs, w_ref, ds_ref = refs[:tp], refs[tp : 2 * tp], refs[2 * tp], refs[2 * tp + 1]
    kv_width = near_refs[0].shape[1] // 2
    groups = kv_width // HEAD_SIZE
    blocks, rows_span, columns = w_ref.shape
    rows = rows_span // tp
    queries, grads, scores, grad_probs = [], [], [], []
    for at in range(blocks):
        span, group = at // groups, at % groups
        cols = slice(group * HEAD_SIZE, (group + 1) * HEAD_SIZE)
        vcols = slice(kv_width + group * HEAD_SIZE, kv_width + (group + 1) * HEAD_SIZE)
        queries.append(stacked_heads(q_ref, span * SPAN_TOKENS, SPAN_TOKENS, group))
        grads.append(stacked_heads(do_ref, span * SPAN_TOKENS, SPAN_TOKENS, group))
        scores.append(dot_nt(span_rows(near_refs, span, rows, cols), queries[at]))
        grad_probs.append(dot_nt(span_rows(near_refs, span, rows, vcols), grads[at]))
    weights, grad_scores = probs_and_grads(
        jnp.concatenate(scores, axis=1), jnp.concatenate(grad_probs, axis=1), None
    )
    for at in range(blocks):
        span, group = at // groups, at % groups
        here = slice(span * rows, (span + 1) * rows)
        cols = slice(group * HEAD_SIZE, (group + 1) * HEAD_SIZE)
        vcols = slice(kv_width + group * HEAD_SIZE, kv_width + (group + 1) * HEAD_SIZE)
        part = slice(at * columns, (at + 1) * columns)
        w_ref[at] = weights[:, part]
        ds_ref[at] = grad_scores[:, part]
        dk = dot_nn(grad_scores[:, part], queries[at]).astype(BF16)
        dv = dot_nn(weights[:, part], grads[at]).astype(BF16)
        for i, grad_ref in enumerate(grad_refs):
            grad_ref[here, cols] = dk[i * rows : (i + 1) * rows]
            grad_ref[here, vcols] = dv[i * rows : (i + 1) * rows]


def join_kernel(tp, w_ref, ds_ref, out_ref, dq_ref, dkv_ref, back_ref, *refs):
    near_refs, (att_ref, qg_ref, kg_ref, vg_ref) = refs[:tp], refs[tp:]
    tokens, kv_width = kg_ref.shape
    groups = kv_width // HEAD_SIZE
    blocks, rows_span, _ = w_ref.shape
    for span in range(blocks // groups):
        rows = slice(span * SPAN_TOKENS, (span + 1) * SPAN_TOKENS)
        for group in range(groups):
            cols = slice(group * HEAD_SIZE, (group + 1) * HEAD_SIZE)
            vcols = slice(kv_width + group * HEAD_SIZE, kv_width + (group + 1) * HEAD_SIZE)
            at = span * groups + group
            out = dot_tn(w_ref[at], span_rows(near_refs, span, rows_span // tp, vcols))
            dq = dot_tn(ds_ref[at], span_rows(near_refs, span, rows_span // tp, cols))
            for h in range(GROUP):
                head = slice((group * GROUP + h) * HEAD_SIZE, (group * GROUP + h + 1) * HEAD_SIZE)
                part = slice(h * SPAN_TOKENS, (h + 1) * SPAN_TOKENS)
                att_ref[rows, head] = (out_ref[rows, head] + out[part]).astype(BF16)
                qg_ref[rows, head] = (dq_ref[rows, head] + dq[part]).astype(BF16)
    halo = back_ref.shape[0]
    kg_ref[: tokens - halo] = dkv_ref[: tokens - halo, :kv_width].astype(BF16)
    vg_ref[: tokens - halo] = dkv_ref[: tokens - halo, kv_width:].astype(BF16)
    kg_ref[tokens - halo :] = (
        dkv_ref[tokens - halo :, :kv_width] + back_ref[:, :kv_width].astype(F32)
    ).astype(BF16)
    vg_ref[tokens - halo :] = (
        dkv_ref[tokens - halo :, kv_width:] + back_ref[:, kv_width:].astype(F32)
    ).astype(BF16)


def sum_kernel(chunks, owned_ref, *refs):
    got_refs, (kg_any, vg_any, kg_ref, vg_ref, sems) = refs[:-5], refs[-5:]
    slots, tokens, features = kg_ref.shape
    tp = NEIGHBOUR_LENGTH // tokens
    width = features // tp
    got = jnp.concatenate([ref[...] for ref in got_refs], axis=0)
    step = slots // chunks
    copies = []
    for i in range(chunks):
        part = slice(i * step, (i + 1) * step)
        total = dot_nn(owned_ref[i * step * tokens : (i + 1) * step * tokens], got).astype(BF16)
        for z in range(tp):
            cols = slice(z * width, (z + 1) * width)
            at = 2 * z * width
            kg_ref[part, :, cols] = total[:, at : at + width].reshape(step, tokens, width)
            vg_ref[part, :, cols] = total[:, at + width : at + 2 * width].reshape(
                step, tokens, width
            )
        for j, (ref, out) in enumerate(((kg_ref, kg_any), (vg_ref, vg_any))):
            copies.append(pltpu.make_async_copy(ref.at[part], out.at[part], sems.at[2 * i + j]))
            copies[-1].start()
    for copy in copies:
        copy.wait()


def call(kernel, name, ins, outs, flops, bytes_accessed, scratch=(), scalars=0, fetched=0, stores=False):
    direct = len(ins) - fetched
    ins = ins[:direct] + tuple(
        pltpu.with_memory_space_constraint(each, pltpu.HBM) for each in ins[direct:]
    )
    return pl.pallas_call(
        kernel,
        out_shape=tuple(outs),
        in_specs=[SMEM] * scalars + [VMEM] * (direct - scalars) + [ANY] * fetched,
        out_specs=(ANY if stores else VMEM,) * len(outs),
        scratch_shapes=list(scratch),
        compiler_params=pltpu.CompilerParams(vmem_limit_bytes=16 * 1024 * 1024),
        cost_estimate=pl.CostEstimate(
            flops=flops, bytes_accessed=bytes_accessed, transcendentals=0
        ),
        name=name,
    )(*ins)


def swapped(block, axis, apart):
    return lax.ppermute(block, axis, [(i, i ^ apart) for i in range(lax.axis_size(axis))])


def distances(tp):
    return [0] + sorted(range(1, tp), key=lambda j: (j < 2, j))


def exchanged(blocks):
    apart = distances(len(blocks))
    return [blocks[0]] + [swapped(b, "tp", j) for b, j in zip(blocks[1:], apart[1:])]


def body(
    queries,
    sequence_keys,
    sequence_values,
    output_gradient,
    enc_keys,
    encoded_values,
    nbr_owner,
    nbr_slot,
):
    tokens_here, query_width = queries.shape
    kv_width = sequence_keys.shape[1]
    both = 2 * kv_width
    groups = kv_width // HEAD_SIZE
    devices = lax.axis_size("seq")
    tp = lax.axis_size("tp")
    spans, per_span = nbr_owner.shape
    requests = spans * per_span
    cap = max(2, 2 * requests // devices)
    tokens = enc_keys.shape[1]
    rows_each = cap * tokens
    window = WINDOW_KEYS
    struct = jax.ShapeDtypeStruct
    store_rows = enc_keys.shape[0] * tokens
    lanes = devices * rows_each
    used = requests * tokens
    int32 = jnp.int32
    rank = lax.axis_index("seq").astype(int32).reshape(1)
    z_rank = lax.axis_index("tp").astype(int32).reshape(1)

    (want,) = call(
        functools.partial(plan_kernel, tokens, cap),
        "plan_requests",
        (nbr_owner, nbr_slot),
        (struct((devices, min(lanes, LANES)), int32),),
        0,
        100_000,
        scratch=[
            pltpu.SMEM(nbr_owner.shape, int32),
            pltpu.SMEM(nbr_slot.shape, int32),
            pltpu.SemaphoreType.DMA((2,)),
        ],
        fetched=2,
    )
    known, step = want[None], 1
    while devices // step > 4:
        known = jnp.concatenate([known, swapped(known, "seq", step)], axis=0)
        step *= 2
    pieces = [known] + [swapped(known, "seq", far) for far in range(step, devices, step)]

    chunks = 4
    store, halo, placed = call(
        functools.partial(stage_kernel, rows_each, chunks),
        "stage_store",
        (rank, nbr_owner, enc_keys, encoded_values, sequence_keys, sequence_values),
        (
            struct((store_rows, 2 * enc_keys.shape[2]), BF16),
            struct((window, both), BF16),
            struct((lanes, used), BF16),
        ),
        0,
        3_000_000,
        scratch=[
            pltpu.SMEM(nbr_owner.shape, int32),
            pltpu.VMEM(enc_keys.shape, BF16),
            pltpu.VMEM(encoded_values.shape, BF16),
            pltpu.SemaphoreType.DMA((2 * chunks + 3,)),
        ],
        scalars=1,
        fetched=5,
    )
    *sent, owned = call(
        functools.partial(pack_kernel, len(pieces)),
        "pack_requests",
        (rank, store, *pieces),
        [struct((rows_each, tp * both), BF16)] * devices + [struct((store_rows, lanes), BF16)],
        200_000_000,
        2_000_000,
        scalars=1,
    )
    got = [sent[0]] + [swapped(sent[j], "seq", j) for j in range(1, devices)]
    spread = call(
        functools.partial(spread_kernel, tp),
        "spread_rows",
        (z_rank, placed, *got),
        [struct((used, both), BF16)] * tp,
        50_000_000,
        1_000_000,
        scratch=[pltpu.VMEM((used, tp * both), BF16)],
        scalars=1,
    )
    near = exchanged(spread)
    near[1], halo = lax.optimization_barrier((near[1], halo))
    halo = lax.ppermute(halo, "seq", [(i, i + 1) for i in range(devices - 1)])

    blocks = spans * groups
    rows_span = per_span * NEIGHBOUR_LENGTH
    *grads, weights, grad_scores = call(
        functools.partial(cross_kernel, tp),
        "cross_attention",
        (queries, output_gradient, *near),
        [struct((used, both), BF16)] * tp
        + [struct((blocks, rows_span, GROUP * SPAN_TOKENS), BF16)] * 2,
        600_000_000,
        3_000_000,
    )
    grads, halo = lax.optimization_barrier((grads, halo))
    grads = exchanged(grads)
    self_out, self_dq, self_dkv, back = call(
        self_kernel,
        "self_attention",
        (rank, queries, sequence_keys, sequence_values, output_gradient, halo),
        (
            struct((tokens_here, query_width), F32),
            struct((tokens_here, query_width), F32),
            struct((tokens_here, both), F32),
            struct((window, both), BF16),
        ),
        1_600_000_000,
        6_000_000,
        scalars=1,
    )
    back = lax.ppermute(back, "seq", [(i + 1, i) for i in range(devices - 1)])
    grads, self_out = lax.optimization_barrier((grads, self_out))

    returned = call(
        functools.partial(scatter_kernel, tp),
        "scatter_gradients",
        (z_rank, placed, *grads),
        [struct((rows_each, tp * both), BF16)] * devices,
        50_000_000,
        1_000_000,
        scratch=[pltpu.VMEM((used, tp * both), BF16)],
        scalars=1,
    )
    returned, weights = lax.optimization_barrier((returned, weights))
    returned = [returned[0]] + [swapped(returned[j], "seq", j) for j in range(1, devices)]

    attended, query_gradient, key_gradient, value_gradient = call(
        functools.partial(join_kernel, tp),
        "join_outputs",
        (weights, grad_scores, self_out, self_dq, self_dkv, back, *near),
        (
            struct((tokens_here, query_width), BF16),
            struct((tokens_here, query_width), BF16),
            struct((tokens_here, kv_width), BF16),
            struct((tokens_here, kv_width), BF16),
        ),
        300_000_000,
        5_000_000,
    )
    returned, attended = lax.optimization_barrier((returned, attended))
    store_kgrad, store_vgrad = call(
        functools.partial(sum_kernel, chunks),
        "sum_store_gradients",
        (owned, *returned),
        (struct(enc_keys.shape, BF16), struct(encoded_values.shape, BF16)),
        200_000_000,
        2_000_000,
        scratch=[
            pltpu.VMEM(enc_keys.shape, BF16),
            pltpu.VMEM(encoded_values.shape, BF16),
            pltpu.SemaphoreType.DMA((2 * chunks,)),
        ],
        stores=True,
    )
    return (
        attended,
        query_gradient,
        key_gradient,
        value_gradient,
        store_kgrad,
        store_vgrad,
    )


def solution(mesh):
    arguments = (P("seq", "tp"),) * 4 + (P("seq", "tp", None),) * 2 + (P("seq", None),) * 2
    results = (P("seq", "tp"),) * 4 + (P("seq", "tp", None),) * 2
    return jax.shard_map(
        body, mesh=mesh, in_specs=arguments, out_specs=results, check_vma=False
    )
```

```python
import functools
import math

import jax
import jax.numpy as jnp
from jax import lax
from jax.experimental import pallas as pl
from jax.experimental.pallas import tpu as pltpu
from jax.sharding import PartitionSpec as P

QUERY_HEADS = 32
KEY_VALUE_HEADS = 8
HEAD_SIZE = 128
SPAN_TOKENS = 64
NEIGHBOUR_COUNT = 4
NEIGHBOUR_LENGTH = 16
WINDOW_KEYS = 128
GROUP = QUERY_HEADS // KEY_VALUE_HEADS
SCALE = 1.0 / math.sqrt(HEAD_SIZE)
LOG2E = math.log2(math.e)

F32 = jnp.float32
BF16 = jnp.bfloat16
VMEM = pl.BlockSpec(memory_space=pltpu.VMEM)
SMEM = pl.BlockSpec(memory_space=pltpu.SMEM)
ANY = pl.BlockSpec(memory_space=pl.ANY)
LANES = 128


def dot_nn(a, b):
    return lax.dot_general(a, b, (((1,), (0,)), ((), ())), preferred_element_type=F32)


def dot_nt(a, b):
    return lax.dot_general(a, b, (((1,), (1,)), ((), ())), preferred_element_type=F32)


def dot_tn(a, b):
    return lax.dot_general(a, b, (((0,), (0,)), ((), ())), preferred_element_type=F32)


def stacked_heads(ref, first_row, rows, group):
    return jnp.concatenate(
        [
            ref[
                first_row : first_row + rows,
                (group * GROUP + h) * HEAD_SIZE : (group * GROUP + h + 1) * HEAD_SIZE,
            ]
            for h in range(GROUP)
        ],
        axis=0,
    )


def probs_and_grads(scores, grad_probs, allowed):
    scores = scores * (SCALE * LOG2E)
    if allowed is not None:
        scores = jnp.where(allowed, scores, -jnp.inf)
    raised = jnp.exp2(scores - jnp.max(scores, axis=0, keepdims=True))
    probs = raised * (1.0 / jnp.sum(raised, axis=0, keepdims=True))
    delta = jnp.sum(probs * grad_probs, axis=0, keepdims=True)
    grad_scores = (probs * (grad_probs - delta) * SCALE).astype(BF16)
    return probs.astype(BF16), grad_scores


def plan_kernel(tokens, cap, owner_any, slot_any, want_ref, owner_ref, slot_ref, sems):
    copies = [
        pltpu.make_async_copy(owner_any, owner_ref, sems.at[0]),
        pltpu.make_async_copy(slot_any, slot_ref, sems.at[1]),
    ]
    for copy in copies:
        copy.start()
    row = lax.broadcasted_iota(jnp.int32, want_ref.shape, 0)
    lane = lax.broadcasted_iota(jnp.int32, want_ref.shape, 1)
    place = row * cap + (lane // tokens) % cap
    token = lane % tokens
    want = jnp.full(want_ref.shape, -1, jnp.int32)
    for copy in copies:
        copy.wait()
    for i, j, owner, rank in ranked(owner_ref):
        want = jnp.where(place == owner * cap + rank, slot_ref[i, j] * tokens + token, want)
    want_ref[...] = want


def ranked(owner_ref):
    spans, per_span = owner_ref.shape
    owners, found = [], []
    for i in range(spans):
        for j in range(per_span):
            owner = owner_ref[i, j]
            rank = jnp.int32(0)
            for earlier in owners:
                rank = rank + jnp.where(earlier == owner, 1, 0)
            owners.append(owner)
            found.append((i, j, owner, rank))
    return found


def stage_kernel(
    rows_each,
    chunks,
    me_ref,
    owner_any,
    k_any,
    v_any,
    sk_any,
    sv_any,
    store_ref,
    halo_ref,
    placed_ref,
    owner_ref,
    k_ref,
    v_ref,
    sems,
):
    slots, tokens, features = k_ref.shape
    kv_width = sk_any.shape[1]
    window = halo_ref.shape[0]
    tail = slice(sk_any.shape[0] - window, sk_any.shape[0])
    step = slots // chunks
    fetch_owner = pltpu.make_async_copy(owner_any, owner_ref, sems.at[2 * chunks + 2])
    fetch_owner.start()
    copies = []
    for i in range(chunks):
        part = slice(i * step, (i + 1) * step)
        copies.append(pltpu.make_async_copy(k_any.at[part], k_ref.at[part], sems.at[2 * i]))
        copies.append(pltpu.make_async_copy(v_any.at[part], v_ref.at[part], sems.at[2 * i + 1]))
    left, right = slice(0, kv_width), slice(kv_width, 2 * kv_width)
    copies.append(pltpu.make_async_copy(sk_any.at[tail], halo_ref.at[:, left], sems.at[2 * chunks]))
    copies.append(
        pltpu.make_async_copy(sv_any.at[tail], halo_ref.at[:, right], sems.at[2 * chunks + 1])
    )
    for copy in copies:
        copy.start()
    fetch_owner.wait()
    me = me_ref[0]
    lanes, used = placed_ref.shape
    lane = lax.broadcasted_iota(jnp.int32, (1, used), 1)
    place = lane % tokens
    for r, (_, _, owner, rank) in enumerate(ranked(owner_ref)):
        place = place + jnp.where(lane // tokens == r, (owner ^ me) * rows_each + rank * tokens, 0)
    row = lax.broadcasted_iota(jnp.int32, (lanes, used), 0)
    placed_ref[...] = jnp.where(row == place, 1.0, 0.0).astype(BF16)
    for i in range(chunks):
        copies[2 * i].wait()
        copies[2 * i + 1].wait()
        part = slice(i * step, (i + 1) * step)
        rows = slice(i * step * tokens, (i + 1) * step * tokens)
        for z in range(features // kv_width):
            cols = slice(z * kv_width, (z + 1) * kv_width)
            at = 2 * z * kv_width
            for ref in (k_ref, v_ref):
                store_ref[rows, at : at + kv_width] = ref[part, :, cols].reshape(
                    step * tokens, kv_width
                )
                at += kv_width
    for copy in copies[2 * chunks :]:
        copy.wait()


def pack_kernel(pieces, me_ref, store_ref, *refs):
    wanted_refs, send_refs, owned_ref = refs[:pieces], refs[pieces:-1], refs[-1]
    rows_each = send_refs[0].shape[0]
    rows, lanes = owned_ref.shape
    me = me_ref[0]
    width = wanted_refs[0].shape[2]
    lane = lax.broadcasted_iota(jnp.int32, (1, width), 1)
    parts = [jnp.full((1, width), -1, jnp.int32) for _ in range(lanes // width)]
    entries = [(ref, i) for ref in wanted_refs for i in range(ref.shape[0])]
    for apart, (wanted_ref, i) in enumerate(entries):
        part, at = divmod(apart * rows_each, width)
        from_there = wanted_ref[i, pl.ds(me, 1), :]
        here = (lane >= at) & (lane < at + rows_each)
        parts[part] = jnp.where(here, from_there, parts[part])
    target = jnp.concatenate(parts, axis=1)
    row = lax.broadcasted_iota(jnp.int32, (rows, lanes), 0)
    owned = jnp.where(row == target, 1.0, 0.0).astype(BF16)
    owned_ref[...] = owned
    picked = dot_tn(owned, store_ref[...]).astype(BF16)
    for at, send_ref in enumerate(by_distance(send_refs)):
        send_ref[...] = picked[at * rows_each : (at + 1) * rows_each]


def spread_kernel(tp, z_ref, placed_ref, *refs):
    got_refs, send_refs, near_ref = refs[: -tp - 1], refs[-tp - 1 : -1], refs[-1]
    both = send_refs[0].shape[1]
    got = jnp.concatenate([ref[...] for ref in by_distance(got_refs)], axis=0)
    near_ref[...] = dot_tn(placed_ref[...], got).astype(BF16)
    for apart, send_ref in zip(distances(tp), send_refs):
        start = pl.multiple_of((z_ref[0] ^ apart) * both, both)
        send_ref[...] = near_ref[:, pl.ds(start, both)]


def scatter_kernel(tp, z_ref, placed_ref, *refs):
    grad_refs, send_refs, all_ref = refs[:tp], refs[tp:-1], refs[-1]
    both = grad_refs[0].shape[1]
    rows_each = send_refs[0].shape[0]
    for apart, grad_ref in zip(distances(tp), grad_refs):
        start = pl.multiple_of((z_ref[0] ^ apart) * both, both)
        all_ref[:, pl.ds(start, both)] = grad_ref[...]
    rows = dot_nn(placed_ref[...], all_ref[...]).astype(BF16)
    for at, send_ref in enumerate(by_distance(send_refs)):
        send_ref[...] = rows[at * rows_each : (at + 1) * rows_each]


def self_kernel(
    rank_ref, q_ref, k_ref, v_ref, do_ref, halo_ref, out_ref, dq_ref, dkv_ref, back_ref
):
    tokens, kv_width = k_ref.shape
    block = WINDOW_KEYS
    blocks = tokens // block
    key_at = lax.broadcasted_iota(jnp.int32, (2 * block, GROUP * block), 0)
    query_at = lax.broadcasted_iota(jnp.int32, (2 * block, GROUP * block), 1) % block
    band = (key_at > query_at) & (key_at <= query_at + block)
    first_band = band & ((key_at >= block) | (rank_ref[0] > 0))
    for group in range(kv_width // HEAD_SIZE):
        cols = slice(group * HEAD_SIZE, (group + 1) * HEAD_SIZE)
        vcols = slice(kv_width + group * HEAD_SIZE, kv_width + (group + 1) * HEAD_SIZE)
        carried_k = carried_v = None
        for b in range(blocks):
            here = slice(b * block, (b + 1) * block)
            if b == 0:
                keys = jnp.concatenate([halo_ref[:, cols], k_ref[here, cols]], 0)
                values = jnp.concatenate([halo_ref[:, vcols], v_ref[here, cols]], 0)
            else:
                keys = k_ref[(b - 1) * block : (b + 1) * block, cols]
                values = v_ref[(b - 1) * block : (b + 1) * block, cols]
            query_rows = stacked_heads(q_ref, b * block, block, group)
            grad_rows = stacked_heads(do_ref, b * block, block, group)
            weights, grad_scores = probs_and_grads(
                dot_nt(keys, query_rows),
                dot_nt(values, grad_rows),
                first_band if b == 0 else band,
            )
            out = dot_tn(weights, values)
            dq = dot_tn(grad_scores, keys)
            for h in range(GROUP):
                head = slice((group * GROUP + h) * HEAD_SIZE, (group * GROUP + h + 1) * HEAD_SIZE)
                out_ref[here, head] = out[h * block : (h + 1) * block]
                dq_ref[here, head] = dq[h * block : (h + 1) * block]
            dk = dot_nn(grad_scores, query_rows)
            dv = dot_nn(weights, grad_rows)
            if b == 0:
                back_ref[:, cols] = dk[:block].astype(BF16)
                back_ref[:, vcols] = dv[:block].astype(BF16)
            else:
                before = slice((b - 1) * block, b * block)
                dkv_ref[before, cols] = carried_k + dk[:block]
                dkv_ref[before, vcols] = carried_v + dv[:block]
            carried_k, carried_v = dk[block:], dv[block:]
        last = slice((blocks - 1) * block, blocks * block)
        dkv_ref[last, cols] = carried_k
        dkv_ref[last, vcols] = carried_v


def span_rows(near_refs, span, rows, cols):
    return jnp.concatenate([ref[span * rows : (span + 1) * rows, cols] for ref in near_refs], axis=0)


def cross_kernel(tp, q_ref, do_ref, *refs):
    near_refs, grad_refs, w_ref, ds_ref = refs[:tp], refs[tp : 2 * tp], refs[2 * tp], refs[2 * tp + 1]
    kv_width = near_refs[0].shape[1] // 2
    groups = kv_width // HEAD_SIZE
    blocks, rows_span, columns = w_ref.shape
    rows = rows_span // tp
    queries, grads, scores, grad_probs = [], [], [], []
    for at in range(blocks):
        span, group = at // groups, at % groups
        cols = slice(group * HEAD_SIZE, (group + 1) * HEAD_SIZE)
        vcols = slice(kv_width + group * HEAD_SIZE, kv_width + (group + 1) * HEAD_SIZE)
        queries.append(stacked_heads(q_ref, span * SPAN_TOKENS, SPAN_TOKENS, group))
        grads.append(stacked_heads(do_ref, span * SPAN_TOKENS, SPAN_TOKENS, group))
        scores.append(dot_nt(span_rows(near_refs, span, rows, cols), queries[at]))
        grad_probs.append(dot_nt(span_rows(near_refs, span, rows, vcols), grads[at]))
    weights, grad_scores = probs_and_grads(
        jnp.concatenate(scores, axis=1), jnp.concatenate(grad_probs, axis=1), None
    )
    for at in range(blocks):
        span, group = at // groups, at % groups
        here = slice(span * rows, (span + 1) * rows)
        cols = slice(group * HEAD_SIZE, (group + 1) * HEAD_SIZE)
        vcols = slice(kv_width + group * HEAD_SIZE, kv_width + (group + 1) * HEAD_SIZE)
        part = slice(at * columns, (at + 1) * columns)
        w_ref[at] = weights[:, part]
        ds_ref[at] = grad_scores[:, part]
        dk = dot_nn(grad_scores[:, part], queries[at]).astype(BF16)
        dv = dot_nn(weights[:, part], grads[at]).astype(BF16)
        for i, grad_ref in enumerate(grad_refs):
            grad_ref[here, cols] = dk[i * rows : (i + 1) * rows]
            grad_ref[here, vcols] = dv[i * rows : (i + 1) * rows]


def join_kernel(tp, w_ref, ds_ref, out_ref, dq_ref, dkv_ref, back_ref, *refs):
    near_refs, (att_ref, qg_ref, kg_ref, vg_ref) = refs[:tp], refs[tp:]
    tokens, kv_width = kg_ref.shape
    groups = kv_width // HEAD_SIZE
    blocks, rows_span, _ = w_ref.shape
    for span in range(blocks // groups):
        rows = slice(span * SPAN_TOKENS, (span + 1) * SPAN_TOKENS)
        for group in range(groups):
            cols = slice(group * HEAD_SIZE, (group + 1) * HEAD_SIZE)
            vcols = slice(kv_width + group * HEAD_SIZE, kv_width + (group + 1) * HEAD_SIZE)
            at = span * groups + group
            out = dot_tn(w_ref[at], span_rows(near_refs, span, rows_span // tp, vcols))
            dq = dot_tn(ds_ref[at], span_rows(near_refs, span, rows_span // tp, cols))
            for h in range(GROUP):
                head = slice((group * GROUP + h) * HEAD_SIZE, (group * GROUP + h + 1) * HEAD_SIZE)
                part = slice(h * SPAN_TOKENS, (h + 1) * SPAN_TOKENS)
                att_ref[rows, head] = (out_ref[rows, head] + out[part]).astype(BF16)
                qg_ref[rows, head] = (dq_ref[rows, head] + dq[part]).astype(BF16)
    halo = back_ref.shape[0]
    kg_ref[: tokens - halo] = dkv_ref[: tokens - halo, :kv_width].astype(BF16)
    vg_ref[: tokens - halo] = dkv_ref[: tokens - halo, kv_width:].astype(BF16)
    kg_ref[tokens - halo :] = (
        dkv_ref[tokens - halo :, :kv_width] + back_ref[:, :kv_width].astype(F32)
    ).astype(BF16)
    vg_ref[tokens - halo :] = (
        dkv_ref[tokens - halo :, kv_width:] + back_ref[:, kv_width:].astype(F32)
    ).astype(BF16)


def sum_kernel(chunks, owned_ref, *refs):
    got_refs, (kg_any, vg_any, kg_ref, vg_ref, sems) = refs[:-5], refs[-5:]
    slots, tokens, features = kg_ref.shape
    tp = NEIGHBOUR_LENGTH // tokens
    width = features // tp
    got = jnp.concatenate([ref[...] for ref in by_distance(got_refs)], axis=0)
    step = slots // chunks
    copies = []
    for i in range(chunks):
        part = slice(i * step, (i + 1) * step)
        total = dot_nn(owned_ref[i * step * tokens : (i + 1) * step * tokens], got).astype(BF16)
        for z in range(tp):
            cols = slice(z * width, (z + 1) * width)
            at = 2 * z * width
            kg_ref[part, :, cols] = total[:, at : at + width].reshape(step, tokens, width)
            vg_ref[part, :, cols] = total[:, at + width : at + 2 * width].reshape(
                step, tokens, width
            )
        for j, (ref, out) in enumerate(((kg_ref, kg_any), (vg_ref, vg_any))):
            copies.append(pltpu.make_async_copy(ref.at[part], out.at[part], sems.at[2 * i + j]))
            copies[-1].start()
    for copy in copies:
        copy.wait()


def call(kernel, name, ins, outs, flops, bytes_accessed, scratch=(), scalars=0, fetched=0, stores=False):
    direct = len(ins) - fetched
    ins = ins[:direct] + tuple(
        pltpu.with_memory_space_constraint(each, pltpu.HBM) for each in ins[direct:]
    )
    return pl.pallas_call(
        kernel,
        out_shape=tuple(outs),
        in_specs=[SMEM] * scalars + [VMEM] * (direct - scalars) + [ANY] * fetched,
        out_specs=(ANY if stores else VMEM,) * len(outs),
        scratch_shapes=list(scratch),
        compiler_params=pltpu.CompilerParams(vmem_limit_bytes=16 * 1024 * 1024),
        cost_estimate=pl.CostEstimate(
            flops=flops, bytes_accessed=bytes_accessed, transcendentals=0
        ),
        name=name,
    )(*ins)


def swapped(block, axis, apart):
    return lax.ppermute(block, axis, [(i, i ^ apart) for i in range(lax.axis_size(axis))])


def plane_order(devices):
    def key(j):
        return (j == 1, j & 1, -bin(j >> 1).count("1"), j)

    return [0] + sorted(range(1, devices), key=key)


def by_distance(refs):
    order = plane_order(len(refs))
    return [refs[order.index(j)] for j in range(len(refs))]


def crossed(blocks):
    order = plane_order(len(blocks))
    return [blocks[0]] + [swapped(b, "seq", j) for b, j in zip(blocks[1:], order[1:])]


def distances(tp):
    return [0] + sorted(range(1, tp), key=lambda j: (j < 2, j))


def exchanged(blocks):
    apart = distances(len(blocks))
    return [blocks[0]] + [swapped(b, "tp", j) for b, j in zip(blocks[1:], apart[1:])]


def body(
    queries,
    sequence_keys,
    sequence_values,
    output_gradient,
    enc_keys,
    encoded_values,
    nbr_owner,
    nbr_slot,
):
    tokens_here, query_width = queries.shape
    kv_width = sequence_keys.shape[1]
    both = 2 * kv_width
    groups = kv_width // HEAD_SIZE
    devices = lax.axis_size("seq")
    tp = lax.axis_size("tp")
    spans, per_span = nbr_owner.shape
    requests = spans * per_span
    cap = max(2, 2 * requests // devices)
    tokens = enc_keys.shape[1]
    rows_each = cap * tokens
    window = WINDOW_KEYS
    struct = jax.ShapeDtypeStruct
    store_rows = enc_keys.shape[0] * tokens
    lanes = devices * rows_each
    used = requests * tokens
    int32 = jnp.int32
    rank = lax.axis_index("seq").astype(int32).reshape(1)
    z_rank = lax.axis_index("tp").astype(int32).reshape(1)

    (want,) = call(
        functools.partial(plan_kernel, tokens, cap),
        "plan_requests",
        (nbr_owner, nbr_slot),
        (struct((devices, min(lanes, LANES)), int32),),
        0,
        100_000,
        scratch=[
            pltpu.SMEM(nbr_owner.shape, int32),
            pltpu.SMEM(nbr_slot.shape, int32),
            pltpu.SemaphoreType.DMA((2,)),
        ],
        fetched=2,
    )
    known, step = want[None], 1
    while devices // step > 4:
        known = jnp.concatenate([known, swapped(known, "seq", step)], axis=0)
        step *= 2
    pieces = [known] + [swapped(known, "seq", far) for far in range(step, devices, step)]

    chunks = 4
    store, halo, placed = call(
        functools.partial(stage_kernel, rows_each, chunks),
        "stage_store",
        (rank, nbr_owner, enc_keys, encoded_values, sequence_keys, sequence_values),
        (
            struct((store_rows, 2 * enc_keys.shape[2]), BF16),
            struct((window, both), BF16),
            struct((lanes, used), BF16),
        ),
        0,
        3_000_000,
        scratch=[
            pltpu.SMEM(nbr_owner.shape, int32),
            pltpu.VMEM(enc_keys.shape, BF16),
            pltpu.VMEM(encoded_values.shape, BF16),
            pltpu.SemaphoreType.DMA((2 * chunks + 3,)),
        ],
        scalars=1,
        fetched=5,
    )
    *sent, owned = call(
        functools.partial(pack_kernel, len(pieces)),
        "pack_requests",
        (rank, store, *pieces),
        [struct((rows_each, tp * both), BF16)] * devices + [struct((store_rows, lanes), BF16)],
        200_000_000,
        2_000_000,
        scalars=1,
    )
    sent, halo = lax.optimization_barrier((sent, halo))
    got = crossed(sent)
    halo = lax.ppermute(halo, "seq", [(i, (i + 1) % devices) for i in range(devices)])
    spread = call(
        functools.partial(spread_kernel, tp),
        "spread_rows",
        (z_rank, placed, *got),
        [struct((used, both), BF16)] * tp,
        50_000_000,
        1_000_000,
        scratch=[pltpu.VMEM((used, tp * both), BF16)],
        scalars=1,
    )
    near = exchanged(spread)

    blocks = spans * groups
    rows_span = per_span * NEIGHBOUR_LENGTH
    *grads, weights, grad_scores = call(
        functools.partial(cross_kernel, tp),
        "cross_attention",
        (queries, output_gradient, *near),
        [struct((used, both), BF16)] * tp
        + [struct((blocks, rows_span, GROUP * SPAN_TOKENS), BF16)] * 2,
        600_000_000,
        3_000_000,
    )
    grads, halo = lax.optimization_barrier((grads, halo))
    grads = exchanged(grads)
    self_out, self_dq, self_dkv, back = call(
        self_kernel,
        "self_attention",
        (rank, queries, sequence_keys, sequence_values, output_gradient, halo),
        (
            struct((tokens_here, query_width), F32),
            struct((tokens_here, query_width), F32),
            struct((tokens_here, both), F32),
            struct((window, both), BF16),
        ),
        1_600_000_000,
        6_000_000,
        scalars=1,
    )
    back = lax.ppermute(back, "seq", [((i + 1) % devices, i) for i in range(devices)])
    grads, self_out = lax.optimization_barrier((grads, self_out))

    returned = call(
        functools.partial(scatter_kernel, tp),
        "scatter_gradients",
        (z_rank, placed, *grads),
        [struct((rows_each, tp * both), BF16)] * devices,
        50_000_000,
        1_000_000,
        scratch=[pltpu.VMEM((used, tp * both), BF16)],
        scalars=1,
    )
    returned, weights = lax.optimization_barrier((returned, weights))
    returned = crossed(returned)

    attended, query_gradient, key_gradient, value_gradient = call(
        functools.partial(join_kernel, tp),
        "join_outputs",
        (weights, grad_scores, self_out, self_dq, self_dkv, back, *near),
        (
            struct((tokens_here, query_width), BF16),
            struct((tokens_here, query_width), BF16),
            struct((tokens_here, kv_width), BF16),
            struct((tokens_here, kv_width), BF16),
        ),
        300_000_000,
        5_000_000,
    )
    returned, attended = lax.optimization_barrier((returned, attended))
    store_kgrad, store_vgrad = call(
        functools.partial(sum_kernel, chunks),
        "sum_store_gradients",
        (owned, *returned),
        (struct(enc_keys.shape, BF16), struct(encoded_values.shape, BF16)),
        200_000_000,
        2_000_000,
        scratch=[
            pltpu.VMEM(enc_keys.shape, BF16),
            pltpu.VMEM(encoded_values.shape, BF16),
            pltpu.SemaphoreType.DMA((2 * chunks,)),
        ],
        stores=True,
    )
    return (
        attended,
        query_gradient,
        key_gradient,
        value_gradient,
        store_kgrad,
        store_vgrad,
    )


def solution(mesh):
    arguments = (P("seq", "tp"),) * 4 + (P("seq", "tp", None),) * 2 + (P("seq", None),) * 2
    results = (P("seq", "tp"),) * 4 + (P("seq", "tp", None),) * 2
    return jax.shard_map(
        body, mesh=mesh, in_specs=arguments, out_specs=results, check_vma=False
    )
```

```python
import functools
import math

import jax
import jax.numpy as jnp
from jax import lax
from jax.experimental import pallas as pl
from jax.experimental.pallas import tpu as pltpu
from jax.sharding import PartitionSpec as P

QUERY_HEADS = 32
KEY_VALUE_HEADS = 8
HEAD_SIZE = 128
SPAN_TOKENS = 64
NEIGHBOUR_COUNT = 4
NEIGHBOUR_LENGTH = 16
WINDOW_KEYS = 128
GROUP = QUERY_HEADS // KEY_VALUE_HEADS
SCALE = 1.0 / math.sqrt(HEAD_SIZE)
LOG2E = math.log2(math.e)

F32 = jnp.float32
BF16 = jnp.bfloat16
VMEM = pl.BlockSpec(memory_space=pltpu.VMEM)
SMEM = pl.BlockSpec(memory_space=pltpu.SMEM)
ANY = pl.BlockSpec(memory_space=pl.ANY)
LANES = 128


def dot_nn(a, b):
    return lax.dot_general(a, b, (((1,), (0,)), ((), ())), preferred_element_type=F32)


def dot_nt(a, b):
    return lax.dot_general(a, b, (((1,), (1,)), ((), ())), preferred_element_type=F32)


def dot_tn(a, b):
    return lax.dot_general(a, b, (((0,), (0,)), ((), ())), preferred_element_type=F32)


def stacked_heads(ref, first_row, rows, group):
    return jnp.concatenate(
        [
            ref[
                first_row : first_row + rows,
                (group * GROUP + h) * HEAD_SIZE : (group * GROUP + h + 1) * HEAD_SIZE,
            ]
            for h in range(GROUP)
        ],
        axis=0,
    )


def probs_and_grads(scores, grad_probs, allowed):
    scores = scores * (SCALE * LOG2E)
    if allowed is not None:
        scores = jnp.where(allowed, scores, -jnp.inf)
    raised = jnp.exp2(scores - jnp.max(scores, axis=0, keepdims=True))
    probs = raised * (1.0 / jnp.sum(raised, axis=0, keepdims=True))
    delta = jnp.sum(probs * grad_probs, axis=0, keepdims=True)
    grad_scores = (probs * (grad_probs - delta) * SCALE).astype(BF16)
    return probs.astype(BF16), grad_scores


def plan_kernel(tokens, cap, owner_any, slot_any, want_ref, owner_ref, slot_ref, sems):
    copies = [
        pltpu.make_async_copy(owner_any, owner_ref, sems.at[0]),
        pltpu.make_async_copy(slot_any, slot_ref, sems.at[1]),
    ]
    for copy in copies:
        copy.start()
    row = lax.broadcasted_iota(jnp.int32, want_ref.shape, 0)
    lane = lax.broadcasted_iota(jnp.int32, want_ref.shape, 1)
    place = row * cap + (lane // tokens) % cap
    token = lane % tokens
    want = jnp.full(want_ref.shape, -1, jnp.int32)
    for copy in copies:
        copy.wait()
    for i, j, owner, rank in ranked(owner_ref):
        want = jnp.where(place == owner * cap + rank, slot_ref[i, j] * tokens + token, want)
    want_ref[...] = want


def ranked(owner_ref):
    spans, per_span = owner_ref.shape
    owners, found = [], []
    for i in range(spans):
        for j in range(per_span):
            owner = owner_ref[i, j]
            rank = jnp.int32(0)
            for earlier in owners:
                rank = rank + jnp.where(earlier == owner, 1, 0)
            owners.append(owner)
            found.append((i, j, owner, rank))
    return found


def stage_kernel(
    rows_each,
    chunks,
    me_ref,
    owner_any,
    k_any,
    v_any,
    sk_any,
    sv_any,
    store_ref,
    halo_ref,
    placed_ref,
    owner_ref,
    k_ref,
    v_ref,
    sems,
):
    slots, tokens, features = k_ref.shape
    kv_width = sk_any.shape[1]
    window = halo_ref.shape[0]
    tail = slice(sk_any.shape[0] - window, sk_any.shape[0])
    step = slots // chunks
    fetch_owner = pltpu.make_async_copy(owner_any, owner_ref, sems.at[2 * chunks + 2])
    fetch_owner.start()
    copies = []
    for i in range(chunks):
        part = slice(i * step, (i + 1) * step)
        copies.append(pltpu.make_async_copy(k_any.at[part], k_ref.at[part], sems.at[2 * i]))
        copies.append(pltpu.make_async_copy(v_any.at[part], v_ref.at[part], sems.at[2 * i + 1]))
    left, right = slice(0, kv_width), slice(kv_width, 2 * kv_width)
    copies.append(pltpu.make_async_copy(sk_any.at[tail], halo_ref.at[:, left], sems.at[2 * chunks]))
    copies.append(
        pltpu.make_async_copy(sv_any.at[tail], halo_ref.at[:, right], sems.at[2 * chunks + 1])
    )
    for copy in copies:
        copy.start()
    fetch_owner.wait()
    me = me_ref[0]
    lanes, used = placed_ref.shape
    lane = lax.broadcasted_iota(jnp.int32, (1, used), 1)
    place = lane % tokens
    for r, (_, _, owner, rank) in enumerate(ranked(owner_ref)):
        place = place + jnp.where(lane // tokens == r, (owner ^ me) * rows_each + rank * tokens, 0)
    row = lax.broadcasted_iota(jnp.int32, (lanes, used), 0)
    placed_ref[...] = jnp.where(row == place, 1.0, 0.0).astype(BF16)
    for i in range(chunks):
        copies[2 * i].wait()
        copies[2 * i + 1].wait()
        part = slice(i * step, (i + 1) * step)
        rows = slice(i * step * tokens, (i + 1) * step * tokens)
        for z in range(features // kv_width):
            cols = slice(z * kv_width, (z + 1) * kv_width)
            at = 2 * z * kv_width
            for ref in (k_ref, v_ref):
                store_ref[rows, at : at + kv_width] = ref[part, :, cols].reshape(
                    step * tokens, kv_width
                )
                at += kv_width
    for copy in copies[2 * chunks :]:
        copy.wait()


def by_core(rows, rows_each, same_ref, other_ref):
    for m in range(rows.shape[0] // (2 * rows_each)):
        here = slice(m * rows_each, (m + 1) * rows_each)
        at = 2 * m * rows_each
        same_ref[here] = rows[at : at + rows_each]
        other_ref[here] = rows[at + rows_each : at + 2 * rows_each]


def pack_kernel(pieces, me_ref, store_ref, *refs):
    wanted_refs, (same_ref, other_ref, owned_ref) = refs[:pieces], refs[pieces:]
    rows, lanes = owned_ref.shape
    rows_each = lanes // sum(ref.shape[0] for ref in wanted_refs)
    me = me_ref[0]
    width = wanted_refs[0].shape[2]
    lane = lax.broadcasted_iota(jnp.int32, (1, width), 1)
    parts = [jnp.full((1, width), -1, jnp.int32) for _ in range(lanes // width)]
    entries = [(ref, i) for ref in wanted_refs for i in range(ref.shape[0])]
    for apart, (wanted_ref, i) in enumerate(entries):
        part, at = divmod(apart * rows_each, width)
        from_there = wanted_ref[i, pl.ds(me, 1), :]
        here = (lane >= at) & (lane < at + rows_each)
        parts[part] = jnp.where(here, from_there, parts[part])
    target = jnp.concatenate(parts, axis=1)
    row = lax.broadcasted_iota(jnp.int32, (rows, lanes), 0)
    owned = jnp.where(row == target, 1.0, 0.0).astype(BF16)
    owned_ref[...] = owned
    picked = dot_tn(owned, store_ref[...]).astype(BF16)
    by_core(picked, rows_each, same_ref, other_ref)


def spread_kernel(tp, z_ref, placed_ref, *refs):
    got_refs, send_refs, near_ref = refs[: -tp - 1], refs[-tp - 1 : -1], refs[-1]
    both = send_refs[0].shape[1]
    got = jnp.concatenate([ref[...] for ref in by_chip(got_refs)], axis=0)
    near_ref[...] = dot_tn(placed_ref[...], got).astype(BF16)
    for apart, send_ref in zip(distances(tp), send_refs):
        start = pl.multiple_of((z_ref[0] ^ apart) * both, both)
        send_ref[...] = near_ref[:, pl.ds(start, both)]


def scatter_kernel(tp, rows_each, z_ref, placed_ref, *refs):
    grad_refs, (same_ref, other_ref, all_ref) = refs[:tp], refs[tp:]
    both = grad_refs[0].shape[1]
    for apart, grad_ref in zip(distances(tp), grad_refs):
        start = pl.multiple_of((z_ref[0] ^ apart) * both, both)
        all_ref[:, pl.ds(start, both)] = grad_ref[...]
    rows = dot_nn(placed_ref[...], all_ref[...]).astype(BF16)
    by_core(rows, rows_each, same_ref, other_ref)


def self_kernel(
    rank_ref, q_ref, k_ref, v_ref, do_ref, halo_ref, out_ref, dq_ref, dkv_ref, back_ref
):
    tokens, kv_width = k_ref.shape
    block = WINDOW_KEYS
    blocks = tokens // block
    key_at = lax.broadcasted_iota(jnp.int32, (2 * block, GROUP * block), 0)
    query_at = lax.broadcasted_iota(jnp.int32, (2 * block, GROUP * block), 1) % block
    band = (key_at > query_at) & (key_at <= query_at + block)
    first_band = band & ((key_at >= block) | (rank_ref[0] > 0))
    for group in range(kv_width // HEAD_SIZE):
        cols = slice(group * HEAD_SIZE, (group + 1) * HEAD_SIZE)
        vcols = slice(kv_width + group * HEAD_SIZE, kv_width + (group + 1) * HEAD_SIZE)
        carried_k = carried_v = None
        for b in range(blocks):
            here = slice(b * block, (b + 1) * block)
            if b == 0:
                keys = jnp.concatenate([halo_ref[:, cols], k_ref[here, cols]], 0)
                values = jnp.concatenate([halo_ref[:, vcols], v_ref[here, cols]], 0)
            else:
                keys = k_ref[(b - 1) * block : (b + 1) * block, cols]
                values = v_ref[(b - 1) * block : (b + 1) * block, cols]
            query_rows = stacked_heads(q_ref, b * block, block, group)
            grad_rows = stacked_heads(do_ref, b * block, block, group)
            weights, grad_scores = probs_and_grads(
                dot_nt(keys, query_rows),
                dot_nt(values, grad_rows),
                first_band if b == 0 else band,
            )
            out = dot_tn(weights, values)
            dq = dot_tn(grad_scores, keys)
            for h in range(GROUP):
                head = slice((group * GROUP + h) * HEAD_SIZE, (group * GROUP + h + 1) * HEAD_SIZE)
                out_ref[here, head] = out[h * block : (h + 1) * block]
                dq_ref[here, head] = dq[h * block : (h + 1) * block]
            dk = dot_nn(grad_scores, query_rows)
            dv = dot_nn(weights, grad_rows)
            if b == 0:
                back_ref[:, cols] = dk[:block].astype(BF16)
                back_ref[:, vcols] = dv[:block].astype(BF16)
            else:
                before = slice((b - 1) * block, b * block)
                dkv_ref[before, cols] = carried_k + dk[:block]
                dkv_ref[before, vcols] = carried_v + dv[:block]
            carried_k, carried_v = dk[block:], dv[block:]
        last = slice((blocks - 1) * block, blocks * block)
        dkv_ref[last, cols] = carried_k
        dkv_ref[last, vcols] = carried_v


def span_rows(near_refs, span, rows, cols):
    return jnp.concatenate([ref[span * rows : (span + 1) * rows, cols] for ref in near_refs], axis=0)


def cross_kernel(tp, q_ref, do_ref, *refs):
    near_refs, grad_refs, w_ref, ds_ref = refs[:tp], refs[tp : 2 * tp], refs[2 * tp], refs[2 * tp + 1]
    kv_width = near_refs[0].shape[1] // 2
    groups = kv_width // HEAD_SIZE
    blocks, rows_span, columns = w_ref.shape
    rows = rows_span // tp
    queries, grads, scores, grad_probs = [], [], [], []
    for at in range(blocks):
        span, group = at // groups, at % groups
        cols = slice(group * HEAD_SIZE, (group + 1) * HEAD_SIZE)
        vcols = slice(kv_width + group * HEAD_SIZE, kv_width + (group + 1) * HEAD_SIZE)
        queries.append(stacked_heads(q_ref, span * SPAN_TOKENS, SPAN_TOKENS, group))
        grads.append(stacked_heads(do_ref, span * SPAN_TOKENS, SPAN_TOKENS, group))
        scores.append(dot_nt(span_rows(near_refs, span, rows, cols), queries[at]))
        grad_probs.append(dot_nt(span_rows(near_refs, span, rows, vcols), grads[at]))
    weights, grad_scores = probs_and_grads(
        jnp.concatenate(scores, axis=1), jnp.concatenate(grad_probs, axis=1), None
    )
    for at in range(blocks):
        span, group = at // groups, at % groups
        here = slice(span * rows, (span + 1) * rows)
        cols = slice(group * HEAD_SIZE, (group + 1) * HEAD_SIZE)
        vcols = slice(kv_width + group * HEAD_SIZE, kv_width + (group + 1) * HEAD_SIZE)
        part = slice(at * columns, (at + 1) * columns)
        w_ref[at] = weights[:, part]
        ds_ref[at] = grad_scores[:, part]
        dk = dot_nn(grad_scores[:, part], queries[at]).astype(BF16)
        dv = dot_nn(weights[:, part], grads[at]).astype(BF16)
        for i, grad_ref in enumerate(grad_refs):
            grad_ref[here, cols] = dk[i * rows : (i + 1) * rows]
            grad_ref[here, vcols] = dv[i * rows : (i + 1) * rows]


def join_kernel(tp, w_ref, ds_ref, out_ref, dq_ref, dkv_ref, back_ref, *refs):
    near_refs, (att_ref, qg_ref, kg_ref, vg_ref) = refs[:tp], refs[tp:]
    tokens, kv_width = kg_ref.shape
    groups = kv_width // HEAD_SIZE
    blocks, rows_span, _ = w_ref.shape
    for span in range(blocks // groups):
        rows = slice(span * SPAN_TOKENS, (span + 1) * SPAN_TOKENS)
        for group in range(groups):
            cols = slice(group * HEAD_SIZE, (group + 1) * HEAD_SIZE)
            vcols = slice(kv_width + group * HEAD_SIZE, kv_width + (group + 1) * HEAD_SIZE)
            at = span * groups + group
            out = dot_tn(w_ref[at], span_rows(near_refs, span, rows_span // tp, vcols))
            dq = dot_tn(ds_ref[at], span_rows(near_refs, span, rows_span // tp, cols))
            for h in range(GROUP):
                head = slice((group * GROUP + h) * HEAD_SIZE, (group * GROUP + h + 1) * HEAD_SIZE)
                part = slice(h * SPAN_TOKENS, (h + 1) * SPAN_TOKENS)
                att_ref[rows, head] = (out_ref[rows, head] + out[part]).astype(BF16)
                qg_ref[rows, head] = (dq_ref[rows, head] + dq[part]).astype(BF16)
    halo = back_ref.shape[0]
    kg_ref[: tokens - halo] = dkv_ref[: tokens - halo, :kv_width].astype(BF16)
    vg_ref[: tokens - halo] = dkv_ref[: tokens - halo, kv_width:].astype(BF16)
    kg_ref[tokens - halo :] = (
        dkv_ref[tokens - halo :, :kv_width] + back_ref[:, :kv_width].astype(F32)
    ).astype(BF16)
    vg_ref[tokens - halo :] = (
        dkv_ref[tokens - halo :, kv_width:] + back_ref[:, kv_width:].astype(F32)
    ).astype(BF16)


def sum_kernel(chunks, owned_ref, *refs):
    got_refs, (kg_any, vg_any, kg_ref, vg_ref, sems) = refs[:-5], refs[-5:]
    slots, tokens, features = kg_ref.shape
    tp = NEIGHBOUR_LENGTH // tokens
    width = features // tp
    got = jnp.concatenate([ref[...] for ref in by_chip(got_refs)], axis=0)
    step = slots // chunks
    copies = []
    for i in range(chunks):
        part = slice(i * step, (i + 1) * step)
        total = dot_nn(owned_ref[i * step * tokens : (i + 1) * step * tokens], got).astype(BF16)
        for z in range(tp):
            cols = slice(z * width, (z + 1) * width)
            at = 2 * z * width
            kg_ref[part, :, cols] = total[:, at : at + width].reshape(step, tokens, width)
            vg_ref[part, :, cols] = total[:, at + width : at + 2 * width].reshape(
                step, tokens, width
            )
        for j, (ref, out) in enumerate(((kg_ref, kg_any), (vg_ref, vg_any))):
            copies.append(pltpu.make_async_copy(ref.at[part], out.at[part], sems.at[2 * i + j]))
            copies[-1].start()
    for copy in copies:
        copy.wait()


def call(kernel, name, ins, outs, flops, bytes_accessed, scratch=(), scalars=0, fetched=0, stores=False):
    direct = len(ins) - fetched
    ins = ins[:direct] + tuple(
        pltpu.with_memory_space_constraint(each, pltpu.HBM) for each in ins[direct:]
    )
    return pl.pallas_call(
        kernel,
        out_shape=tuple(outs),
        in_specs=[SMEM] * scalars + [VMEM] * (direct - scalars) + [ANY] * fetched,
        out_specs=(ANY if stores else VMEM,) * len(outs),
        scratch_shapes=list(scratch),
        compiler_params=pltpu.CompilerParams(vmem_limit_bytes=16 * 1024 * 1024),
        cost_estimate=pl.CostEstimate(
            flops=flops, bytes_accessed=bytes_accessed, transcendentals=0
        ),
        name=name,
    )(*ins)


def swapped(block, axis, apart):
    return lax.ppermute(block, axis, [(i, i ^ apart) for i in range(lax.axis_size(axis))])


def chip_order(chips):
    return [0] + sorted(range(1, chips), key=lambda m: (-bin(m).count("1"), m))


def by_chip(refs):
    order = chip_order(len(refs))
    return [refs[order.index(m)] for m in range(len(refs))]


def join_cores_kernel(own_ref, other_ref, *send_refs):
    rows = own_ref.shape[0] // len(send_refs)
    for m, send_ref in enumerate(by_chip(send_refs)):
        here = slice(m * rows, (m + 1) * rows)
        send_ref[:rows] = own_ref[here]
        send_ref[rows:] = other_ref[here]


def crossed(same, other):
    rows, columns = same.shape
    devices = lax.axis_size("seq")
    chips = devices // 2
    other = swapped(other, "seq", 1)
    blocks = call(
        join_cores_kernel,
        "join_cores",
        (same, other),
        [jax.ShapeDtypeStruct((2 * rows // chips, columns), same.dtype)] * chips,
        0,
        1_000_000,
    )
    order = chip_order(chips)
    return [blocks[0]] + [swapped(b, "seq", 2 * m) for b, m in zip(blocks[1:], order[1:])]


def distances(tp):
    return [0] + sorted(range(1, tp), key=lambda j: (j < 2, j))


def exchanged(blocks):
    apart = distances(len(blocks))
    return [blocks[0]] + [swapped(b, "tp", j) for b, j in zip(blocks[1:], apart[1:])]


def body(
    queries,
    sequence_keys,
    sequence_values,
    output_gradient,
    enc_keys,
    encoded_values,
    nbr_owner,
    nbr_slot,
):
    tokens_here, query_width = queries.shape
    kv_width = sequence_keys.shape[1]
    both = 2 * kv_width
    groups = kv_width // HEAD_SIZE
    devices = lax.axis_size("seq")
    tp = lax.axis_size("tp")
    spans, per_span = nbr_owner.shape
    requests = spans * per_span
    cap = max(2, 2 * requests // devices)
    tokens = enc_keys.shape[1]
    rows_each = cap * tokens
    window = WINDOW_KEYS
    struct = jax.ShapeDtypeStruct
    store_rows = enc_keys.shape[0] * tokens
    lanes = devices * rows_each
    used = requests * tokens
    int32 = jnp.int32
    rank = lax.axis_index("seq").astype(int32).reshape(1)
    z_rank = lax.axis_index("tp").astype(int32).reshape(1)

    (want,) = call(
        functools.partial(plan_kernel, tokens, cap),
        "plan_requests",
        (nbr_owner, nbr_slot),
        (struct((devices, min(lanes, LANES)), int32),),
        0,
        100_000,
        scratch=[
            pltpu.SMEM(nbr_owner.shape, int32),
            pltpu.SMEM(nbr_slot.shape, int32),
            pltpu.SemaphoreType.DMA((2,)),
        ],
        fetched=2,
    )
    known, step = want[None], 1
    while devices // step > 4:
        known = jnp.concatenate([known, swapped(known, "seq", step)], axis=0)
        step *= 2
    pieces = [known] + [swapped(known, "seq", far) for far in range(step, devices, step)]

    chunks = 4
    store, halo, placed = call(
        functools.partial(stage_kernel, rows_each, chunks),
        "stage_store",
        (rank, nbr_owner, enc_keys, encoded_values, sequence_keys, sequence_values),
        (
            struct((store_rows, 2 * enc_keys.shape[2]), BF16),
            struct((window, both), BF16),
            struct((lanes, used), BF16),
        ),
        0,
        3_000_000,
        scratch=[
            pltpu.SMEM(nbr_owner.shape, int32),
            pltpu.VMEM(enc_keys.shape, BF16),
            pltpu.VMEM(encoded_values.shape, BF16),
            pltpu.SemaphoreType.DMA((2 * chunks + 3,)),
        ],
        scalars=1,
        fetched=5,
    )
    half = struct((lanes // 2, tp * both), BF16)
    same, other, owned = call(
        functools.partial(pack_kernel, len(pieces)),
        "pack_requests",
        (rank, store, *pieces),
        (half, half, struct((store_rows, lanes), BF16)),
        200_000_000,
        2_000_000,
        scalars=1,
    )
    same, halo = lax.optimization_barrier((same, halo))
    got = crossed(same, other)
    halo = lax.ppermute(halo, "seq", [(i, (i + 1) % devices) for i in range(devices)])
    spread = call(
        functools.partial(spread_kernel, tp),
        "spread_rows",
        (z_rank, placed, *got),
        [struct((used, both), BF16)] * tp,
        50_000_000,
        1_000_000,
        scratch=[pltpu.VMEM((used, tp * both), BF16)],
        scalars=1,
    )
    near = exchanged(spread)

    blocks = spans * groups
    rows_span = per_span * NEIGHBOUR_LENGTH
    *grads, weights, grad_scores = call(
        functools.partial(cross_kernel, tp),
        "cross_attention",
        (queries, output_gradient, *near),
        [struct((used, both), BF16)] * tp
        + [struct((blocks, rows_span, GROUP * SPAN_TOKENS), BF16)] * 2,
        600_000_000,
        3_000_000,
    )
    grads, halo = lax.optimization_barrier((grads, halo))
    grads = exchanged(grads)
    self_out, self_dq, self_dkv, back = call(
        self_kernel,
        "self_attention",
        (rank, queries, sequence_keys, sequence_values, output_gradient, halo),
        (
            struct((tokens_here, query_width), F32),
            struct((tokens_here, query_width), F32),
            struct((tokens_here, both), F32),
            struct((window, both), BF16),
        ),
        1_600_000_000,
        6_000_000,
        scalars=1,
    )
    back = lax.ppermute(back, "seq", [((i + 1) % devices, i) for i in range(devices)])
    grads, self_out = lax.optimization_barrier((grads, self_out))

    same, other = call(
        functools.partial(scatter_kernel, tp, rows_each),
        "scatter_gradients",
        (z_rank, placed, *grads),
        (half, half),
        50_000_000,
        1_000_000,
        scratch=[pltpu.VMEM((used, tp * both), BF16)],
        scalars=1,
    )
    same, weights = lax.optimization_barrier((same, weights))
    returned = crossed(same, other)

    attended, query_gradient, key_gradient, value_gradient = call(
        functools.partial(join_kernel, tp),
        "join_outputs",
        (weights, grad_scores, self_out, self_dq, self_dkv, back, *near),
        (
            struct((tokens_here, query_width), BF16),
            struct((tokens_here, query_width), BF16),
            struct((tokens_here, kv_width), BF16),
            struct((tokens_here, kv_width), BF16),
        ),
        300_000_000,
        5_000_000,
    )
    returned, attended = lax.optimization_barrier((returned, attended))
    store_kgrad, store_vgrad = call(
        functools.partial(sum_kernel, chunks),
        "sum_store_gradients",
        (owned, *returned),
        (struct(enc_keys.shape, BF16), struct(encoded_values.shape, BF16)),
        200_000_000,
        2_000_000,
        scratch=[
            pltpu.VMEM(enc_keys.shape, BF16),
            pltpu.VMEM(encoded_values.shape, BF16),
            pltpu.SemaphoreType.DMA((2 * chunks,)),
        ],
        stores=True,
    )
    return (
        attended,
        query_gradient,
        key_gradient,
        value_gradient,
        store_kgrad,
        store_vgrad,
    )


def solution(mesh):
    arguments = (P("seq", "tp"),) * 4 + (P("seq", "tp", None),) * 2 + (P("seq", None),) * 2
    results = (P("seq", "tp"),) * 4 + (P("seq", "tp", None),) * 2
    return jax.shard_map(
        body, mesh=mesh, in_specs=arguments, out_specs=results, check_vma=False
    )
```

```python
import functools
import math

import jax
import jax.numpy as jnp
from jax import lax
from jax.experimental import pallas as pl
from jax.experimental.pallas import tpu as pltpu
from jax.sharding import PartitionSpec as P

QUERY_HEADS = 32
KEY_VALUE_HEADS = 8
HEAD_SIZE = 128
SPAN_TOKENS = 64
NEIGHBOUR_COUNT = 4
NEIGHBOUR_LENGTH = 16
WINDOW_KEYS = 128
GROUP = QUERY_HEADS // KEY_VALUE_HEADS
SCALE = 1.0 / math.sqrt(HEAD_SIZE)
LOG2E = math.log2(math.e)

F32 = jnp.float32
BF16 = jnp.bfloat16
VMEM = pl.BlockSpec(memory_space=pltpu.VMEM)
SMEM = pl.BlockSpec(memory_space=pltpu.SMEM)
ANY = pl.BlockSpec(memory_space=pl.ANY)
LANES = 128


def dot_nn(a, b):
    return lax.dot_general(a, b, (((1,), (0,)), ((), ())), preferred_element_type=F32)


def dot_nt(a, b):
    return lax.dot_general(a, b, (((1,), (1,)), ((), ())), preferred_element_type=F32)


def dot_tn(a, b):
    return lax.dot_general(a, b, (((0,), (0,)), ((), ())), preferred_element_type=F32)


def stacked_heads(ref, first_row, rows, group):
    return jnp.concatenate(
        [
            ref[
                first_row : first_row + rows,
                (group * GROUP + h) * HEAD_SIZE : (group * GROUP + h + 1) * HEAD_SIZE,
            ]
            for h in range(GROUP)
        ],
        axis=0,
    )


def probs_and_grads(scores, grad_probs, allowed):
    scores = scores * (SCALE * LOG2E)
    if allowed is not None:
        scores = jnp.where(allowed, scores, -jnp.inf)
    raised = jnp.exp2(scores - jnp.max(scores, axis=0, keepdims=True))
    probs = raised * (1.0 / jnp.sum(raised, axis=0, keepdims=True))
    delta = jnp.sum(probs * grad_probs, axis=0, keepdims=True)
    grad_scores = (probs * (grad_probs - delta) * SCALE).astype(BF16)
    return probs.astype(BF16), grad_scores


def plan_kernel(tokens, cap, owner_any, slot_any, want_ref, owner_ref, slot_ref, sems):
    copies = [
        pltpu.make_async_copy(owner_any, owner_ref, sems.at[0]),
        pltpu.make_async_copy(slot_any, slot_ref, sems.at[1]),
    ]
    for copy in copies:
        copy.start()
    row = lax.broadcasted_iota(jnp.int32, want_ref.shape, 0)
    lane = lax.broadcasted_iota(jnp.int32, want_ref.shape, 1)
    place = row * cap + (lane // tokens) % cap
    token = lane % tokens
    want = jnp.full(want_ref.shape, -1, jnp.int32)
    for copy in copies:
        copy.wait()
    for i, j, owner, rank in ranked(owner_ref):
        want = jnp.where(place == owner * cap + rank, slot_ref[i, j] * tokens + token, want)
    want_ref[...] = want


def ranked(owner_ref):
    spans, per_span = owner_ref.shape
    owners, found = [], []
    for i in range(spans):
        for j in range(per_span):
            owner = owner_ref[i, j]
            rank = jnp.int32(0)
            for earlier in owners:
                rank = rank + jnp.where(earlier == owner, 1, 0)
            owners.append(owner)
            found.append((i, j, owner, rank))
    return found


def stage_kernel(
    rows_each,
    chunks,
    me_ref,
    sibling_k_ref,
    sibling_v_ref,
    owner_any,
    sk_any,
    sv_any,
    k_any,
    v_any,
    store_ref,
    halo_ref,
    placed_ref,
    owner_ref,
    k_ref,
    v_ref,
    sems,
):
    store_refs = (k_ref, v_ref, sibling_k_ref, sibling_v_ref)
    slots, tokens, features = store_refs[0].shape
    kv_width = sk_any.shape[1]
    window = halo_ref.shape[0]
    tail = slice(sk_any.shape[0] - window, sk_any.shape[0])
    step = slots // chunks
    fetch_owner = pltpu.make_async_copy(owner_any, owner_ref, sems.at[0])
    fetch_owner.start()
    left, right = slice(0, kv_width), slice(kv_width, 2 * kv_width)
    copies = []
    for i in range(chunks):
        part = slice(i * step, (i + 1) * step)
        copies.append(pltpu.make_async_copy(k_any.at[part], k_ref.at[part], sems.at[3 + 2 * i]))
        copies.append(pltpu.make_async_copy(v_any.at[part], v_ref.at[part], sems.at[4 + 2 * i]))
    copies.append(pltpu.make_async_copy(sk_any.at[tail], halo_ref.at[:, left], sems.at[1]))
    copies.append(pltpu.make_async_copy(sv_any.at[tail], halo_ref.at[:, right], sems.at[2]))
    for copy in copies:
        copy.start()
    fetch_owner.wait()
    me = me_ref[0]
    lanes, used = placed_ref.shape
    lane = lax.broadcasted_iota(jnp.int32, (1, used), 1)
    place = lane % tokens
    for r, (_, _, owner, rank) in enumerate(ranked(owner_ref)):
        place = place + jnp.where(lane // tokens == r, (owner ^ me) * rows_each + rank * tokens, 0)
    row = lax.broadcasted_iota(jnp.int32, (lanes, used), 0)
    placed_ref[...] = jnp.where(row == place, 1.0, 0.0).astype(BF16)
    for i in range(chunks):
        part = slice(i * step, (i + 1) * step)
        copies[2 * i].wait()
        copies[2 * i + 1].wait()
        for j in range(4):
            core, kind = j // 2, j % 2
            first = (core * slots + i * step) * tokens
            store_ref[
                first : first + step * tokens, kind * features : (kind + 1) * features
            ] = store_refs[j][part].reshape(step * tokens, features)
    for copy in copies[2 * chunks :]:
        copy.wait()


def pack_kernel(rows_each, me_ref, store_ref, *refs):
    pieces = len(refs) // 3
    wanted_refs, key_refs, value_refs, target_ref = (
        refs[:pieces],
        by_chip(refs[pieces : 2 * pieces]),
        by_chip(refs[2 * pieces : 3 * pieces]),
        refs[-1],
    )
    rows, features = store_ref.shape[0], store_ref.shape[1] // 2
    lanes = target_ref.shape[1]
    width = wanted_refs[0].shape[1]
    me = me_ref[0]
    lane = lax.broadcasted_iota(jnp.int32, (1, width), 1)
    parts = [jnp.full((1, width), -1, jnp.int32) for _ in range(lanes // width)]
    for m, wanted_ref in enumerate(by_chip(wanted_refs)):
        for core in range(2):
            part, at = divmod((2 * m + core) * rows_each, width)
            from_there = wanted_ref[pl.ds(me ^ core, 1), :]
            here = (lane >= at) & (lane < at + rows_each)
            parts[part] = jnp.where(here, from_there, parts[part])
    target = jnp.concatenate(parts, axis=1)
    target_ref[...] = target
    second = (lax.broadcasted_iota(jnp.int32, (1, lanes), 1) // rows_each) % 2
    target = jnp.where(target >= 0, target + second * (rows // 2), -1)
    row = lax.broadcasted_iota(jnp.int32, (rows, lanes), 0)
    picks = jnp.where(row == target, 1.0, 0.0).astype(BF16)
    for kind, send_refs in enumerate((key_refs, value_refs)):
        cols = slice(kind * features, (kind + 1) * features)
        picked = dot_tn(picks, store_ref[:, cols]).astype(BF16)
        for m, send_ref in enumerate(send_refs):
            send_ref[...] = picked[2 * m * rows_each : 2 * (m + 1) * rows_each]


def spread_kernel(tp, z_ref, placed_ref, *refs):
    got_refs, send_refs, near_ref = refs[: -tp - 1], refs[-tp - 1 : -1], refs[-1]
    width = send_refs[0].shape[1]
    got = jnp.concatenate([ref[...] for ref in by_chip(got_refs)], axis=0)
    near_ref[...] = dot_tn(placed_ref[...], got).astype(BF16)
    for apart, send_ref in zip(distances(tp), send_refs):
        start = pl.multiple_of((z_ref[0] ^ apart) * width, width)
        send_ref[...] = near_ref[:, pl.ds(start, width)]


def scatter_kernel(tp, z_ref, placed_ref, *refs):
    grad_refs, send_refs, all_ref = refs[:tp], refs[tp:-1], refs[-1]
    width = grad_refs[0].shape[1]
    for apart, grad_ref in zip(distances(tp), grad_refs):
        start = pl.multiple_of((z_ref[0] ^ apart) * width, width)
        all_ref[:, pl.ds(start, width)] = grad_ref[...]
    rows = dot_nn(placed_ref[...], all_ref[...]).astype(BF16)
    step = send_refs[0].shape[0]
    for m, send_ref in enumerate(by_chip(send_refs)):
        send_ref[...] = rows[m * step : (m + 1) * step]


def part_cores_kernel(*refs):
    got_refs, (same_ref, other_ref) = by_chip(refs[:-2]), refs[-2:]
    rows = got_refs[0].shape[0] // 2
    for m, got_ref in enumerate(got_refs):
        same_ref[m * rows : (m + 1) * rows] = got_ref[:rows]
        other_ref[m * rows : (m + 1) * rows] = got_ref[rows:]


def self_kernel(
    rank_ref, q_ref, k_ref, v_ref, do_ref, halo_ref, out_ref, dq_ref, dkv_ref, back_ref
):
    tokens, kv_width = k_ref.shape
    block = WINDOW_KEYS
    blocks = tokens // block
    key_at = lax.broadcasted_iota(jnp.int32, (2 * block, GROUP * block), 0)
    query_at = lax.broadcasted_iota(jnp.int32, (2 * block, GROUP * block), 1) % block
    band = (key_at > query_at) & (key_at <= query_at + block)
    first_band = band & ((key_at >= block) | (rank_ref[0] > 0))
    for group in range(kv_width // HEAD_SIZE):
        cols = slice(group * HEAD_SIZE, (group + 1) * HEAD_SIZE)
        vcols = slice(kv_width + group * HEAD_SIZE, kv_width + (group + 1) * HEAD_SIZE)
        carried_k = carried_v = None
        for b in range(blocks):
            here = slice(b * block, (b + 1) * block)
            if b == 0:
                keys = jnp.concatenate([halo_ref[:, cols], k_ref[here, cols]], 0)
                values = jnp.concatenate([halo_ref[:, vcols], v_ref[here, cols]], 0)
            else:
                keys = k_ref[(b - 1) * block : (b + 1) * block, cols]
                values = v_ref[(b - 1) * block : (b + 1) * block, cols]
            query_rows = stacked_heads(q_ref, b * block, block, group)
            grad_rows = stacked_heads(do_ref, b * block, block, group)
            weights, grad_scores = probs_and_grads(
                dot_nt(keys, query_rows),
                dot_nt(values, grad_rows),
                first_band if b == 0 else band,
            )
            out = dot_tn(weights, values)
            dq = dot_tn(grad_scores, keys)
            for h in range(GROUP):
                head = slice((group * GROUP + h) * HEAD_SIZE, (group * GROUP + h + 1) * HEAD_SIZE)
                out_ref[here, head] = out[h * block : (h + 1) * block]
                dq_ref[here, head] = dq[h * block : (h + 1) * block]
            dk = dot_nn(grad_scores, query_rows)
            dv = dot_nn(weights, grad_rows)
            if b == 0:
                back_ref[:, cols] = dk[:block].astype(BF16)
                back_ref[:, vcols] = dv[:block].astype(BF16)
            else:
                before = slice((b - 1) * block, b * block)
                dkv_ref[before, cols] = carried_k + dk[:block]
                dkv_ref[before, vcols] = carried_v + dv[:block]
            carried_k, carried_v = dk[block:], dv[block:]
        last = slice((blocks - 1) * block, blocks * block)
        dkv_ref[last, cols] = carried_k
        dkv_ref[last, vcols] = carried_v


def span_rows(near_refs, span, rows, group):
    cols = slice(group * HEAD_SIZE, (group + 1) * HEAD_SIZE)
    return jnp.concatenate([ref[span * rows : (span + 1) * rows, cols] for ref in near_refs], axis=0)


def cross_kernel(tp, q_ref, do_ref, *refs):
    key_refs, value_refs, dk_refs, dv_refs = (refs[i * tp : (i + 1) * tp] for i in range(4))
    w_ref, ds_ref = refs[4 * tp :]
    groups = key_refs[0].shape[1] // HEAD_SIZE
    blocks, rows_span, columns = w_ref.shape
    rows = rows_span // tp
    queries, grads, scores, grad_probs = [], [], [], []
    for at in range(blocks):
        span, group = at // groups, at % groups
        queries.append(stacked_heads(q_ref, span * SPAN_TOKENS, SPAN_TOKENS, group))
        grads.append(stacked_heads(do_ref, span * SPAN_TOKENS, SPAN_TOKENS, group))
        scores.append(dot_nt(span_rows(key_refs, span, rows, group), queries[at]))
        grad_probs.append(dot_nt(span_rows(value_refs, span, rows, group), grads[at]))
    weights, grad_scores = probs_and_grads(
        jnp.concatenate(scores, axis=1), jnp.concatenate(grad_probs, axis=1), None
    )
    for at in range(blocks):
        span, group = at // groups, at % groups
        here = slice(span * rows, (span + 1) * rows)
        cols = slice(group * HEAD_SIZE, (group + 1) * HEAD_SIZE)
        part = slice(at * columns, (at + 1) * columns)
        w_ref[at] = weights[:, part]
        ds_ref[at] = grad_scores[:, part]
        dk = dot_nn(grad_scores[:, part], queries[at]).astype(BF16)
        dv = dot_nn(weights[:, part], grads[at]).astype(BF16)
        for i in range(tp):
            dk_refs[i][here, cols] = dk[i * rows : (i + 1) * rows]
            dv_refs[i][here, cols] = dv[i * rows : (i + 1) * rows]


def join_kernel(tp, w_ref, ds_ref, out_ref, dq_ref, dkv_ref, back_ref, *refs):
    key_refs, value_refs, (att_ref, qg_ref, kg_ref, vg_ref) = refs[:tp], refs[tp : 2 * tp], refs[2 * tp :]
    tokens, kv_width = kg_ref.shape
    groups = kv_width // HEAD_SIZE
    blocks, rows_span, _ = w_ref.shape
    for span in range(blocks // groups):
        rows = slice(span * SPAN_TOKENS, (span + 1) * SPAN_TOKENS)
        for group in range(groups):
            at = span * groups + group
            out = dot_tn(w_ref[at], span_rows(value_refs, span, rows_span // tp, group))
            dq = dot_tn(ds_ref[at], span_rows(key_refs, span, rows_span // tp, group))
            for h in range(GROUP):
                head = slice((group * GROUP + h) * HEAD_SIZE, (group * GROUP + h + 1) * HEAD_SIZE)
                part = slice(h * SPAN_TOKENS, (h + 1) * SPAN_TOKENS)
                att_ref[rows, head] = (out_ref[rows, head] + out[part]).astype(BF16)
                qg_ref[rows, head] = (dq_ref[rows, head] + dq[part]).astype(BF16)
    halo = back_ref.shape[0]
    kg_ref[: tokens - halo] = dkv_ref[: tokens - halo, :kv_width].astype(BF16)
    vg_ref[: tokens - halo] = dkv_ref[: tokens - halo, kv_width:].astype(BF16)
    kg_ref[tokens - halo :] = (
        dkv_ref[tokens - halo :, :kv_width] + back_ref[:, :kv_width].astype(F32)
    ).astype(BF16)
    vg_ref[tokens - halo :] = (
        dkv_ref[tokens - halo :, kv_width:] + back_ref[:, kv_width:].astype(F32)
    ).astype(BF16)


def sum_kernel(chunks, rows_each, target_ref, other_ref, same_rows, other_rows, out_any, out_ref, sems):
    slots, tokens, features = out_ref.shape
    half = same_rows.shape[0]
    lanes = target_ref.shape[1]
    lane = lax.broadcasted_iota(jnp.int32, (1, lanes), 1)
    second = (lane // rows_each) % 2
    target = jnp.where(second == 0, target_ref[...], other_ref[...])
    row = lax.broadcasted_iota(jnp.int32, (slots * tokens, lanes), 0)
    owned = jnp.where(row == target, 1.0, 0.0).astype(BF16)
    rows = []
    for m in range(half // rows_each):
        here = slice(m * rows_each, (m + 1) * rows_each)
        rows += [same_rows[here], other_rows[here]]
    got = jnp.concatenate(rows, axis=0)
    step = slots // chunks
    copies = []
    for i in range(chunks):
        part = slice(i * step, (i + 1) * step)
        total = dot_nn(owned[i * step * tokens : (i + 1) * step * tokens], got).astype(BF16)
        out_ref[part] = total.reshape(step, tokens, features)
        copies.append(pltpu.make_async_copy(out_ref.at[part], out_any.at[part], sems.at[i]))
        copies[-1].start()
    for copy in copies:
        copy.wait()


def call(kernel, name, ins, outs, flops, bytes_accessed, scratch=(), scalars=0, fetched=0, stores=False):
    direct = len(ins) - fetched
    ins = ins[:direct] + tuple(
        pltpu.with_memory_space_constraint(each, pltpu.HBM) for each in ins[direct:]
    )
    return pl.pallas_call(
        kernel,
        out_shape=tuple(outs),
        in_specs=[SMEM] * scalars + [VMEM] * (direct - scalars) + [ANY] * fetched,
        out_specs=(ANY if stores else VMEM,) * len(outs),
        scratch_shapes=list(scratch),
        compiler_params=pltpu.CompilerParams(vmem_limit_bytes=16 * 1024 * 1024),
        cost_estimate=pl.CostEstimate(
            flops=flops, bytes_accessed=bytes_accessed, transcendentals=0
        ),
        name=name,
    )(*ins)


def swapped(block, axis, apart):
    return lax.ppermute(block, axis, [(i, i ^ apart) for i in range(lax.axis_size(axis))])


def chip_order(chips):
    return [0] + sorted(range(1, chips), key=lambda m: (-bin(m).count("1"), m))


def by_chip(refs):
    order = chip_order(len(refs))
    return [refs[order.index(m)] for m in range(len(refs))]


def crossed(blocks):
    order = chip_order(len(blocks))
    return [blocks[0]] + [swapped(b, "seq", 2 * m) for b, m in zip(blocks[1:], order[1:])]


def distances(tp):
    return [0] + sorted(range(1, tp), key=lambda j: (j < 2, j))


def exchanged(blocks):
    apart = distances(len(blocks))
    return [blocks[0]] + [swapped(b, "tp", j) for b, j in zip(blocks[1:], apart[1:])]


def body(
    queries,
    sequence_keys,
    sequence_values,
    output_gradient,
    enc_keys,
    encoded_values,
    nbr_owner,
    nbr_slot,
):
    tokens_here, query_width = queries.shape
    kv_width = sequence_keys.shape[1]
    both = 2 * kv_width
    groups = kv_width // HEAD_SIZE
    devices = lax.axis_size("seq")
    tp = lax.axis_size("tp")
    spans, per_span = nbr_owner.shape
    requests = spans * per_span
    cap = max(2, 2 * requests // devices)
    tokens = enc_keys.shape[1]
    rows_each = cap * tokens
    window = WINDOW_KEYS
    struct = jax.ShapeDtypeStruct
    store_rows = enc_keys.shape[0] * tokens
    lanes = devices * rows_each
    used = requests * tokens
    int32 = jnp.int32
    rank = lax.axis_index("seq").astype(int32).reshape(1)
    z_rank = lax.axis_index("tp").astype(int32).reshape(1)

    sibling_keys = swapped(enc_keys, "seq", 1)
    sibling_values = swapped(encoded_values, "seq", 1)
    (want,) = call(
        functools.partial(plan_kernel, tokens, cap),
        "plan_requests",
        (nbr_owner, nbr_slot),
        (struct((devices, min(lanes, LANES)), int32),),
        0,
        100_000,
        scratch=[
            pltpu.SMEM(nbr_owner.shape, int32),
            pltpu.SMEM(nbr_slot.shape, int32),
            pltpu.SemaphoreType.DMA((2,)),
        ],
        fetched=2,
    )
    chips = devices // 2
    order = chip_order(chips)
    pieces = [want] + [swapped(want, "seq", 2 * m) for m in order[1:]]

    chunks = 4
    features = enc_keys.shape[2]
    store, halo, placed = call(
        functools.partial(stage_kernel, rows_each, chunks),
        "stage_store",
        (rank, sibling_keys, sibling_values, nbr_owner, sequence_keys, sequence_values)
        + (enc_keys, encoded_values),
        (
            struct((2 * store_rows, 2 * features), BF16),
            struct((window, both), BF16),
            struct((lanes, used), BF16),
        ),
        0,
        5_000_000,
        scratch=[pltpu.SMEM(nbr_owner.shape, int32)]
        + [pltpu.VMEM(enc_keys.shape, BF16)] * 2
        + [pltpu.SemaphoreType.DMA((3 + 2 * chunks,))],
        scalars=1,
        fetched=5,
    )
    halo = lax.ppermute(halo, "seq", [(i, (i + 1) % devices) for i in range(devices)])
    block = struct((2 * rows_each, features), BF16)
    *sent, target = call(
        functools.partial(pack_kernel, rows_each),
        "pack_requests",
        (rank, store, *pieces),
        [block] * (2 * chips) + [struct((1, lanes), int32)],
        200_000_000,
        2_000_000,
        scalars=1,
    )
    near = []
    got = [crossed(sent[:chips]), crossed(sent[chips:])]
    for kind in range(2):
        spread = call(
            functools.partial(spread_kernel, tp),
            "spread_keys" if kind == 0 else "spread_values",
            (z_rank, placed, *got[kind]),
            [struct((used, kv_width), BF16)] * tp,
            1_000_000,
            10_000,
            scratch=[pltpu.VMEM((used, features), BF16)],
            scalars=1,
        )
        near.append(exchanged(spread))
    near[0], halo, target = lax.optimization_barrier((near[0], halo, target))
    self_out, self_dq, self_dkv, back = call(
        self_kernel,
        "self_attention",
        (rank, queries, sequence_keys, sequence_values, output_gradient, halo),
        (
            struct((tokens_here, query_width), F32),
            struct((tokens_here, query_width), F32),
            struct((tokens_here, both), F32),
            struct((window, both), BF16),
        ),
        1_600_000_000,
        6_000_000,
        scalars=1,
    )
    back = lax.ppermute(back, "seq", [((i + 1) % devices, i) for i in range(devices)])
    other_target = swapped(target, "seq", 1)
    near[1], self_out = lax.optimization_barrier((near[1], self_out))

    blocks = spans * groups
    rows_span = per_span * NEIGHBOUR_LENGTH
    *grads, weights, grad_scores = call(
        functools.partial(cross_kernel, tp),
        "cross_attention",
        (queries, output_gradient, *near[0], *near[1]),
        [struct((used, kv_width), BF16)] * (2 * tp)
        + [struct((blocks, rows_span, GROUP * SPAN_TOKENS), BF16)] * 2,
        600_000_000,
        3_000_000,
    )
    grads = [exchanged(grads[tp:]), exchanged(grads[:tp])]
    halves = []
    for kind in range(2):
        returned = call(
            functools.partial(scatter_kernel, tp),
            "scatter_values" if kind == 0 else "scatter_keys",
            (z_rank, placed, *grads[kind]),
            [block] * chips,
            1_000_000,
            10_000,
            scratch=[pltpu.VMEM((used, features), BF16)],
            scalars=1,
        )
        if kind == 1:
            returned, weights = lax.optimization_barrier((returned, weights))
        same, other = call(
            part_cores_kernel,
            "part_cores",
            tuple(crossed(returned)),
            [struct((lanes // 2, features), BF16)] * 2,
            0,
            10_000,
        )
        halves.append((same, swapped(other, "seq", 1)))

    halves[0], grad_scores = lax.optimization_barrier((halves[0], grad_scores))
    attended, query_gradient, key_gradient, value_gradient = call(
        functools.partial(join_kernel, tp),
        "join_outputs",
        (weights, grad_scores, self_out, self_dq, self_dkv, back, *near[0], *near[1]),
        (
            struct((tokens_here, query_width), BF16),
            struct((tokens_here, query_width), BF16),
            struct((tokens_here, kv_width), BF16),
            struct((tokens_here, kv_width), BF16),
        ),
        300_000_000,
        5_000_000,
    )
    halves[0], attended = lax.optimization_barrier((halves[0], attended))
    summed = []
    for name, half in zip(("sum_value_gradients", "sum_key_gradients"), halves):
        if summed:
            half, summed[0] = lax.optimization_barrier((half, summed[0]))
        summed += call(
            functools.partial(sum_kernel, chunks, rows_each),
            name,
            (target, other_target, *half),
            (struct(enc_keys.shape, BF16),),
            100_000_000,
            1_000_000,
            scratch=[pltpu.VMEM(enc_keys.shape, BF16), pltpu.SemaphoreType.DMA((chunks,))],
            stores=True,
        )
    store_vgrad, store_kgrad = summed
    return (
        attended,
        query_gradient,
        key_gradient,
        value_gradient,
        store_kgrad,
        store_vgrad,
    )


def solution(mesh):
    arguments = (P("seq", "tp"),) * 4 + (P("seq", "tp", None),) * 2 + (P("seq", None),) * 2
    results = (P("seq", "tp"),) * 4 + (P("seq", "tp", None),) * 2
    return jax.shard_map(
        body, mesh=mesh, in_specs=arguments, out_specs=results, check_vma=False
    )
```

```python
import functools
import math

import jax
import jax.numpy as jnp
from jax import lax
from jax.experimental import pallas as pl
from jax.experimental.pallas import tpu as pltpu
from jax.sharding import PartitionSpec as P

QUERY_HEADS = 32
KEY_VALUE_HEADS = 8
HEAD_SIZE = 128
SPAN_TOKENS = 64
NEIGHBOUR_COUNT = 4
NEIGHBOUR_LENGTH = 16
WINDOW_KEYS = 128
GROUP = QUERY_HEADS // KEY_VALUE_HEADS
SCALE = 1.0 / math.sqrt(HEAD_SIZE)
LOG2E = math.log2(math.e)

F32 = jnp.float32
BF16 = jnp.bfloat16
VMEM = pl.BlockSpec(memory_space=pltpu.VMEM)
SMEM = pl.BlockSpec(memory_space=pltpu.SMEM)
ANY = pl.BlockSpec(memory_space=pl.ANY)
LANES = 128


def dot_nn(a, b):
    return lax.dot_general(a, b, (((1,), (0,)), ((), ())), preferred_element_type=F32)


def dot_nt(a, b):
    return lax.dot_general(a, b, (((1,), (1,)), ((), ())), preferred_element_type=F32)


def dot_tn(a, b):
    return lax.dot_general(a, b, (((0,), (0,)), ((), ())), preferred_element_type=F32)


def stacked_heads(ref, first_row, rows, group):
    return jnp.concatenate(
        [
            ref[
                first_row : first_row + rows,
                (group * GROUP + h) * HEAD_SIZE : (group * GROUP + h + 1) * HEAD_SIZE,
            ]
            for h in range(GROUP)
        ],
        axis=0,
    )


def probs_and_grads(scores, grad_probs, allowed):
    scores = scores * (SCALE * LOG2E)
    if allowed is not None:
        scores = jnp.where(allowed, scores, -jnp.inf)
    raised = jnp.exp2(scores - jnp.max(scores, axis=0, keepdims=True))
    probs = raised * (1.0 / jnp.sum(raised, axis=0, keepdims=True))
    delta = jnp.sum(probs * grad_probs, axis=0, keepdims=True)
    grad_scores = (probs * (grad_probs - delta) * SCALE).astype(BF16)
    return probs.astype(BF16), grad_scores


def plan_kernel(tokens, cap, owner_any, slot_any, want_ref, owner_ref, slot_ref, sems):
    copies = [
        pltpu.make_async_copy(owner_any, owner_ref, sems.at[0]),
        pltpu.make_async_copy(slot_any, slot_ref, sems.at[1]),
    ]
    for copy in copies:
        copy.start()
    row = lax.broadcasted_iota(jnp.int32, want_ref.shape, 0)
    lane = lax.broadcasted_iota(jnp.int32, want_ref.shape, 1)
    place = row * cap + (lane // tokens) % cap
    token = lane % tokens
    want = jnp.full(want_ref.shape, -1, jnp.int32)
    for copy in copies:
        copy.wait()
    for i, j, owner, rank in ranked(owner_ref):
        want = jnp.where(place == owner * cap + rank, slot_ref[i, j] * tokens + token, want)
    want_ref[...] = want


def ranked(owner_ref):
    spans, per_span = owner_ref.shape
    owners, found = [], []
    for i in range(spans):
        for j in range(per_span):
            owner = owner_ref[i, j]
            rank = jnp.int32(0)
            for earlier in owners:
                rank = rank + jnp.where(earlier == owner, 1, 0)
            owners.append(owner)
            found.append((i, j, owner, rank))
    return found


def stage_kernel(
    rows_each,
    chunks,
    me_ref,
    z_ref,
    sibling_k_ref,
    sibling_v_ref,
    owner_any,
    sk_any,
    sv_any,
    k_any,
    v_any,
    store_ref,
    halo_ref,
    placed_ref,
    owner_ref,
    k_ref,
    v_ref,
    sems,
):
    store_refs = (k_ref, v_ref, sibling_k_ref, sibling_v_ref)
    slots, tokens, features = store_refs[0].shape
    kv_width = sk_any.shape[1]
    window = halo_ref.shape[0]
    tail = slice(sk_any.shape[0] - window, sk_any.shape[0])
    step = slots // chunks
    fetch_owner = pltpu.make_async_copy(owner_any, owner_ref, sems.at[0])
    fetch_owner.start()
    left, right = slice(0, kv_width), slice(kv_width, 2 * kv_width)
    copies = []
    for i in range(chunks):
        part = slice(i * step, (i + 1) * step)
        copies.append(pltpu.make_async_copy(k_any.at[part], k_ref.at[part], sems.at[3 + 2 * i]))
        copies.append(pltpu.make_async_copy(v_any.at[part], v_ref.at[part], sems.at[4 + 2 * i]))
    copies.append(pltpu.make_async_copy(sk_any.at[tail], halo_ref.at[:, left], sems.at[1]))
    copies.append(pltpu.make_async_copy(sv_any.at[tail], halo_ref.at[:, right], sems.at[2]))
    for copy in copies:
        copy.start()
    fetch_owner.wait()
    me = me_ref[0]
    lanes, used = placed_ref.shape
    lane = lax.broadcasted_iota(jnp.int32, (1, used), 1)
    place = lane % tokens
    for r, (_, _, owner, rank) in enumerate(ranked(owner_ref)):
        place = place + jnp.where(lane // tokens == r, (owner ^ me) * rows_each + rank * tokens, 0)
    row = lax.broadcasted_iota(jnp.int32, (lanes, used), 0)
    placed_ref[...] = jnp.where(row == place, 1.0, 0.0).astype(BF16)
    for i in range(chunks):
        part = slice(i * step, (i + 1) * step)
        copies[2 * i].wait()
        copies[2 * i + 1].wait()
        for j in range(4):
            core, kind = j // 2, j % 2
            first = (core * slots + i * step) * tokens
            rows = slice(first, first + step * tokens)
            for d, apart in enumerate(farthest_first(features // kv_width)):
                start = pl.multiple_of((z_ref[0] ^ apart) * kv_width, kv_width)
                at = (2 * d + kind) * kv_width
                store_ref[rows, at : at + kv_width] = store_refs[j][
                    part, :, pl.ds(start, kv_width)
                ].reshape(step * tokens, kv_width)
    for copy in copies[2 * chunks :]:
        copy.wait()


def pack_kernel(rows_each, me_ref, store_ref, *refs):
    pieces = len(refs) // 3
    wanted_refs, far_refs, near_refs, target_ref = (
        refs[:pieces],
        by_chip(refs[pieces : 2 * pieces]),
        by_chip(refs[2 * pieces : 3 * pieces]),
        refs[-1],
    )
    rows, columns = store_ref.shape[0], store_ref.shape[1] // 2
    lanes = target_ref.shape[1]
    width = wanted_refs[0].shape[1]
    me = me_ref[0]
    lane = lax.broadcasted_iota(jnp.int32, (1, width), 1)
    parts = [jnp.full((1, width), -1, jnp.int32) for _ in range(lanes // width)]
    for m, wanted_ref in enumerate(by_chip(wanted_refs)):
        for core in range(2):
            part, at = divmod((2 * m + core) * rows_each, width)
            from_there = wanted_ref[pl.ds(me ^ core, 1), :]
            here = (lane >= at) & (lane < at + rows_each)
            parts[part] = jnp.where(here, from_there, parts[part])
    target = jnp.concatenate(parts, axis=1)
    target_ref[...] = target
    second = (lax.broadcasted_iota(jnp.int32, (1, lanes), 1) // rows_each) % 2
    target = jnp.where(target >= 0, target + second * (rows // 2), -1)
    row = lax.broadcasted_iota(jnp.int32, (rows, lanes), 0)
    picks = jnp.where(row == target, 1.0, 0.0).astype(BF16)
    for half, send_refs in enumerate((far_refs, near_refs)):
        cols = slice(half * columns, (half + 1) * columns)
        picked = dot_tn(picks, store_ref[:, cols]).astype(BF16)
        for m, send_ref in enumerate(send_refs):
            send_ref[...] = picked[2 * m * rows_each : 2 * (m + 1) * rows_each]


def spread_kernel(parts, placed_ref, *refs):
    got_refs, send_refs = refs[: -parts], refs[-parts :]
    width = send_refs[0].shape[1]
    got = jnp.concatenate([ref[...] for ref in by_chip(got_refs)], axis=0)
    rows = dot_tn(placed_ref[...], got).astype(BF16)
    for i, send_ref in enumerate(send_refs):
        send_ref[...] = rows[:, i * width : (i + 1) * width]


def scatter_kernel(tp, z_ref, placed_ref, *refs):
    grad_refs, send_refs, all_ref = refs[:tp], refs[tp:-1], refs[-1]
    both = grad_refs[0].shape[1]
    rows_each = send_refs[0].shape[0]
    for apart, grad_ref in zip(distances(tp), grad_refs):
        start = pl.multiple_of((z_ref[0] ^ apart) * both, both)
        all_ref[:, pl.ds(start, both)] = grad_ref[...]
    rows = dot_nn(placed_ref[...], all_ref[...]).astype(BF16)
    for at, send_ref in enumerate(by_distance(send_refs)):
        send_ref[...] = rows[at * rows_each : (at + 1) * rows_each]


def self_kernel(
    rank_ref, q_ref, k_ref, v_ref, do_ref, halo_ref, out_ref, dq_ref, dkv_ref, back_ref
):
    tokens, kv_width = k_ref.shape
    block = WINDOW_KEYS
    blocks = tokens // block
    key_at = lax.broadcasted_iota(jnp.int32, (2 * block, GROUP * block), 0)
    query_at = lax.broadcasted_iota(jnp.int32, (2 * block, GROUP * block), 1) % block
    band = (key_at > query_at) & (key_at <= query_at + block)
    first_band = band & ((key_at >= block) | (rank_ref[0] > 0))
    for group in range(kv_width // HEAD_SIZE):
        cols = slice(group * HEAD_SIZE, (group + 1) * HEAD_SIZE)
        vcols = slice(kv_width + group * HEAD_SIZE, kv_width + (group + 1) * HEAD_SIZE)
        carried_k = carried_v = None
        for b in range(blocks):
            here = slice(b * block, (b + 1) * block)
            if b == 0:
                keys = jnp.concatenate([halo_ref[:, cols], k_ref[here, cols]], 0)
                values = jnp.concatenate([halo_ref[:, vcols], v_ref[here, cols]], 0)
            else:
                keys = k_ref[(b - 1) * block : (b + 1) * block, cols]
                values = v_ref[(b - 1) * block : (b + 1) * block, cols]
            query_rows = stacked_heads(q_ref, b * block, block, group)
            grad_rows = stacked_heads(do_ref, b * block, block, group)
            weights, grad_scores = probs_and_grads(
                dot_nt(keys, query_rows),
                dot_nt(values, grad_rows),
                first_band if b == 0 else band,
            )
            out = dot_tn(weights, values)
            dq = dot_tn(grad_scores, keys)
            for h in range(GROUP):
                head = slice((group * GROUP + h) * HEAD_SIZE, (group * GROUP + h + 1) * HEAD_SIZE)
                out_ref[here, head] = out[h * block : (h + 1) * block]
                dq_ref[here, head] = dq[h * block : (h + 1) * block]
            dk = dot_nn(grad_scores, query_rows)
            dv = dot_nn(weights, grad_rows)
            if b == 0:
                back_ref[:, cols] = dk[:block].astype(BF16)
                back_ref[:, vcols] = dv[:block].astype(BF16)
            else:
                before = slice((b - 1) * block, b * block)
                dkv_ref[before, cols] = carried_k + dk[:block]
                dkv_ref[before, vcols] = carried_v + dv[:block]
            carried_k, carried_v = dk[block:], dv[block:]
        last = slice((blocks - 1) * block, blocks * block)
        dkv_ref[last, cols] = carried_k
        dkv_ref[last, vcols] = carried_v


def span_rows(near_refs, span, rows, cols):
    return jnp.concatenate([ref[span * rows : (span + 1) * rows, cols] for ref in near_refs], axis=0)


def cross_kernel(tp, q_ref, do_ref, *refs):
    near_refs, grad_refs, w_ref, ds_ref = refs[:tp], refs[tp : 2 * tp], refs[2 * tp], refs[2 * tp + 1]
    kv_width = near_refs[0].shape[1] // 2
    groups = kv_width // HEAD_SIZE
    blocks, rows_span, columns = w_ref.shape
    rows = rows_span // tp
    queries, grads, scores, grad_probs = [], [], [], []
    for at in range(blocks):
        span, group = at // groups, at % groups
        cols = slice(group * HEAD_SIZE, (group + 1) * HEAD_SIZE)
        vcols = slice(kv_width + group * HEAD_SIZE, kv_width + (group + 1) * HEAD_SIZE)
        queries.append(stacked_heads(q_ref, span * SPAN_TOKENS, SPAN_TOKENS, group))
        grads.append(stacked_heads(do_ref, span * SPAN_TOKENS, SPAN_TOKENS, group))
        scores.append(dot_nt(span_rows(near_refs, span, rows, cols), queries[at]))
        grad_probs.append(dot_nt(span_rows(near_refs, span, rows, vcols), grads[at]))
    weights, grad_scores = probs_and_grads(
        jnp.concatenate(scores, axis=1), jnp.concatenate(grad_probs, axis=1), None
    )
    for at in range(blocks):
        span, group = at // groups, at % groups
        here = slice(span * rows, (span + 1) * rows)
        cols = slice(group * HEAD_SIZE, (group + 1) * HEAD_SIZE)
        vcols = slice(kv_width + group * HEAD_SIZE, kv_width + (group + 1) * HEAD_SIZE)
        part = slice(at * columns, (at + 1) * columns)
        w_ref[at] = weights[:, part]
        ds_ref[at] = grad_scores[:, part]
        dk = dot_nn(grad_scores[:, part], queries[at]).astype(BF16)
        dv = dot_nn(weights[:, part], grads[at]).astype(BF16)
        for i, grad_ref in enumerate(grad_refs):
            grad_ref[here, cols] = dk[i * rows : (i + 1) * rows]
            grad_ref[here, vcols] = dv[i * rows : (i + 1) * rows]


def join_kernel(tp, w_ref, ds_ref, out_ref, dq_ref, dkv_ref, back_ref, *refs):
    near_refs, (att_ref, qg_ref, kg_ref, vg_ref) = refs[:tp], refs[tp:]
    tokens, kv_width = kg_ref.shape
    groups = kv_width // HEAD_SIZE
    blocks, rows_span, _ = w_ref.shape
    for span in range(blocks // groups):
        rows = slice(span * SPAN_TOKENS, (span + 1) * SPAN_TOKENS)
        for group in range(groups):
            cols = slice(group * HEAD_SIZE, (group + 1) * HEAD_SIZE)
            vcols = slice(kv_width + group * HEAD_SIZE, kv_width + (group + 1) * HEAD_SIZE)
            at = span * groups + group
            out = dot_tn(w_ref[at], span_rows(near_refs, span, rows_span // tp, vcols))
            dq = dot_tn(ds_ref[at], span_rows(near_refs, span, rows_span // tp, cols))
            for h in range(GROUP):
                head = slice((group * GROUP + h) * HEAD_SIZE, (group * GROUP + h + 1) * HEAD_SIZE)
                part = slice(h * SPAN_TOKENS, (h + 1) * SPAN_TOKENS)
                att_ref[rows, head] = (out_ref[rows, head] + out[part]).astype(BF16)
                qg_ref[rows, head] = (dq_ref[rows, head] + dq[part]).astype(BF16)
    halo = back_ref.shape[0]
    kg_ref[: tokens - halo] = dkv_ref[: tokens - halo, :kv_width].astype(BF16)
    vg_ref[: tokens - halo] = dkv_ref[: tokens - halo, kv_width:].astype(BF16)
    kg_ref[tokens - halo :] = (
        dkv_ref[tokens - halo :, :kv_width] + back_ref[:, :kv_width].astype(F32)
    ).astype(BF16)
    vg_ref[tokens - halo :] = (
        dkv_ref[tokens - halo :, kv_width:] + back_ref[:, kv_width:].astype(F32)
    ).astype(BF16)


def sum_kernel(chunks, target_ref, other_ref, *refs):
    got_refs, (kg_any, vg_any, kg_ref, vg_ref, sems) = refs[:-5], refs[-5:]
    slots, tokens, features = kg_ref.shape
    tp = NEIGHBOUR_LENGTH // tokens
    width = features // tp
    got = jnp.concatenate([ref[...] for ref in by_distance(got_refs)], axis=0)
    lanes = target_ref.shape[1]
    odd = (lax.broadcasted_iota(jnp.int32, (1, lanes), 1) // got_refs[0].shape[0]) % 2
    target = jnp.where(odd == 0, target_ref[...], other_ref[...])
    row = lax.broadcasted_iota(jnp.int32, (slots * tokens, lanes), 0)
    owned = jnp.where(row == target, 1.0, 0.0).astype(BF16)
    step = slots // chunks
    copies = []
    for i in range(chunks):
        part = slice(i * step, (i + 1) * step)
        total = dot_nn(owned[i * step * tokens : (i + 1) * step * tokens], got).astype(BF16)
        for z in range(tp):
            cols = slice(z * width, (z + 1) * width)
            at = 2 * z * width
            kg_ref[part, :, cols] = total[:, at : at + width].reshape(step, tokens, width)
            vg_ref[part, :, cols] = total[:, at + width : at + 2 * width].reshape(
                step, tokens, width
            )
        for j, (ref, out) in enumerate(((kg_ref, kg_any), (vg_ref, vg_any))):
            copies.append(pltpu.make_async_copy(ref.at[part], out.at[part], sems.at[2 * i + j]))
            copies[-1].start()
    for copy in copies:
        copy.wait()


def call(kernel, name, ins, outs, flops, bytes_accessed, scratch=(), scalars=0, fetched=0, stores=False):
    direct = len(ins) - fetched
    ins = ins[:direct] + tuple(
        pltpu.with_memory_space_constraint(each, pltpu.HBM) for each in ins[direct:]
    )
    return pl.pallas_call(
        kernel,
        out_shape=tuple(outs),
        in_specs=[SMEM] * scalars + [VMEM] * (direct - scalars) + [ANY] * fetched,
        out_specs=(ANY if stores else VMEM,) * len(outs),
        scratch_shapes=list(scratch),
        compiler_params=pltpu.CompilerParams(vmem_limit_bytes=16 * 1024 * 1024),
        cost_estimate=pl.CostEstimate(
            flops=flops, bytes_accessed=bytes_accessed, transcendentals=0
        ),
        name=name,
    )(*ins)


def swapped(block, axis, apart):
    return lax.ppermute(block, axis, [(i, i ^ apart) for i in range(lax.axis_size(axis))])


def plane_order(devices):
    def key(j):
        return (j == 1, j & 1, -bin(j >> 1).count("1"), j)

    return [0] + sorted(range(1, devices), key=key)


def by_distance(refs):
    order = plane_order(len(refs))
    return [refs[order.index(j)] for j in range(len(refs))]


def crossed(blocks):
    order = plane_order(len(blocks))
    return [blocks[0]] + [swapped(b, "seq", j) for b, j in zip(blocks[1:], order[1:])]


def chip_order(chips):
    return [0] + sorted(range(1, chips), key=lambda m: (-bin(m).count("1"), m))


def by_chip(refs):
    order = chip_order(len(refs))
    return [refs[order.index(m)] for m in range(len(refs))]


def between_chips(blocks):
    order = chip_order(len(blocks))
    return [blocks[0]] + [swapped(b, "seq", 2 * m) for b, m in zip(blocks[1:], order[1:])]


def farthest_first(tp):
    return distances(tp)[1:] + [0]


def distances(tp):
    return [0] + sorted(range(1, tp), key=lambda j: (j < 2, j))


def exchanged(blocks):
    apart = distances(len(blocks))
    return [blocks[0]] + [swapped(b, "tp", j) for b, j in zip(blocks[1:], apart[1:])]


def body(
    queries,
    sequence_keys,
    sequence_values,
    output_gradient,
    enc_keys,
    encoded_values,
    nbr_owner,
    nbr_slot,
):
    tokens_here, query_width = queries.shape
    kv_width = sequence_keys.shape[1]
    both = 2 * kv_width
    groups = kv_width // HEAD_SIZE
    devices = lax.axis_size("seq")
    tp = lax.axis_size("tp")
    spans, per_span = nbr_owner.shape
    requests = spans * per_span
    cap = max(2, 2 * requests // devices)
    tokens = enc_keys.shape[1]
    rows_each = cap * tokens
    window = WINDOW_KEYS
    struct = jax.ShapeDtypeStruct
    store_rows = enc_keys.shape[0] * tokens
    lanes = devices * rows_each
    used = requests * tokens
    int32 = jnp.int32
    rank = lax.axis_index("seq").astype(int32).reshape(1)
    z_rank = lax.axis_index("tp").astype(int32).reshape(1)

    sibling_keys = swapped(enc_keys, "seq", 1)
    sibling_values = swapped(encoded_values, "seq", 1)
    (want,) = call(
        functools.partial(plan_kernel, tokens, cap),
        "plan_requests",
        (nbr_owner, nbr_slot),
        (struct((devices, min(lanes, LANES)), int32),),
        0,
        100_000,
        scratch=[
            pltpu.SMEM(nbr_owner.shape, int32),
            pltpu.SMEM(nbr_slot.shape, int32),
            pltpu.SemaphoreType.DMA((2,)),
        ],
        fetched=2,
    )
    chips = devices // 2
    order = chip_order(chips)
    pieces = [want] + [swapped(want, "seq", 2 * m) for m in order[1:]]

    chunks = 4
    features = enc_keys.shape[2]
    store, halo, placed = call(
        functools.partial(stage_kernel, rows_each, chunks),
        "stage_store",
        (rank, z_rank, sibling_keys, sibling_values, nbr_owner, sequence_keys, sequence_values)
        + (enc_keys, encoded_values),
        (
            struct((2 * store_rows, 2 * features), BF16),
            struct((window, both), BF16),
            struct((lanes, used), BF16),
        ),
        0,
        5_000_000,
        scratch=[pltpu.SMEM(nbr_owner.shape, int32)]
        + [pltpu.VMEM(enc_keys.shape, BF16)] * 2
        + [pltpu.SemaphoreType.DMA((3 + 2 * chunks,))],
        scalars=2,
        fetched=5,
    )
    halo = lax.ppermute(halo, "seq", [(i, (i + 1) % devices) for i in range(devices)])
    block = struct((2 * rows_each, features), BF16)
    *sent, target = call(
        functools.partial(pack_kernel, rows_each),
        "pack_requests",
        (rank, store, *pieces),
        [block] * (2 * chips) + [struct((1, lanes), int32)],
        200_000_000,
        2_000_000,
        scalars=1,
    )
    parts = tp // 2
    moved = []
    for name, blocks in (("spread_far", sent[:chips]), ("spread_near", sent[chips:])):
        moved += call(
            functools.partial(spread_kernel, parts),
            name,
            (placed, *between_chips(blocks)),
            [struct((used, both), BF16)] * parts,
            1_000_000,
            10_000,
        )
    near = exchanged(moved[-1:] + moved[:-1])

    blocks = spans * groups
    rows_span = per_span * NEIGHBOUR_LENGTH
    *grads, weights, grad_scores = call(
        functools.partial(cross_kernel, tp),
        "cross_attention",
        (queries, output_gradient, *near),
        [struct((used, both), BF16)] * tp
        + [struct((blocks, rows_span, GROUP * SPAN_TOKENS), BF16)] * 2,
        600_000_000,
        3_000_000,
    )
    grads, halo, target = lax.optimization_barrier((grads, halo, target))
    grads = exchanged(grads)
    self_out, self_dq, self_dkv, back = call(
        self_kernel,
        "self_attention",
        (rank, queries, sequence_keys, sequence_values, output_gradient, halo),
        (
            struct((tokens_here, query_width), F32),
            struct((tokens_here, query_width), F32),
            struct((tokens_here, both), F32),
            struct((window, both), BF16),
        ),
        1_600_000_000,
        6_000_000,
        scalars=1,
    )
    back = lax.ppermute(back, "seq", [((i + 1) % devices, i) for i in range(devices)])
    other_target = swapped(target, "seq", 1)
    grads, self_out = lax.optimization_barrier((grads, self_out))

    returned = call(
        functools.partial(scatter_kernel, tp),
        "scatter_gradients",
        (z_rank, placed, *grads),
        [struct((rows_each, tp * both), BF16)] * devices,
        50_000_000,
        1_000_000,
        scratch=[pltpu.VMEM((used, tp * both), BF16)],
        scalars=1,
    )
    returned, weights = lax.optimization_barrier((returned, weights))
    returned = crossed(returned)

    attended, query_gradient, key_gradient, value_gradient = call(
        functools.partial(join_kernel, tp),
        "join_outputs",
        (weights, grad_scores, self_out, self_dq, self_dkv, back, *near),
        (
            struct((tokens_here, query_width), BF16),
            struct((tokens_here, query_width), BF16),
            struct((tokens_here, kv_width), BF16),
            struct((tokens_here, kv_width), BF16),
        ),
        300_000_000,
        5_000_000,
    )
    returned, attended = lax.optimization_barrier((returned, attended))
    store_kgrad, store_vgrad = call(
        functools.partial(sum_kernel, chunks),
        "sum_store_gradients",
        (target, other_target, *returned),
        (struct(enc_keys.shape, BF16), struct(encoded_values.shape, BF16)),
        200_000_000,
        2_000_000,
        scratch=[
            pltpu.VMEM(enc_keys.shape, BF16),
            pltpu.VMEM(encoded_values.shape, BF16),
            pltpu.SemaphoreType.DMA((2 * chunks,)),
        ],
        stores=True,
    )
    return (
        attended,
        query_gradient,
        key_gradient,
        value_gradient,
        store_kgrad,
        store_vgrad,
    )


def solution(mesh):
    arguments = (P("seq", "tp"),) * 4 + (P("seq", "tp", None),) * 2 + (P("seq", None),) * 2
    results = (P("seq", "tp"),) * 4 + (P("seq", "tp", None),) * 2
    return jax.shard_map(
        body, mesh=mesh, in_specs=arguments, out_specs=results, check_vma=False
    )
```

```python
import functools
import math

import jax
import jax.numpy as jnp
from jax import lax
from jax.experimental import pallas as pl
from jax.experimental.pallas import tpu as pltpu
from jax.sharding import PartitionSpec as P

QUERY_HEADS = 32
KEY_VALUE_HEADS = 8
HEAD_SIZE = 128
SPAN_TOKENS = 64
NEIGHBOUR_COUNT = 4
NEIGHBOUR_LENGTH = 16
WINDOW_KEYS = 128
GROUP = QUERY_HEADS // KEY_VALUE_HEADS
SCALE = 1.0 / math.sqrt(HEAD_SIZE)
LOG2E = math.log2(math.e)

F32 = jnp.float32
BF16 = jnp.bfloat16
VMEM = pl.BlockSpec(memory_space=pltpu.VMEM)
SMEM = pl.BlockSpec(memory_space=pltpu.SMEM)
ANY = pl.BlockSpec(memory_space=pl.ANY)
LANES = 128


def dot_nn(a, b):
    return lax.dot_general(a, b, (((1,), (0,)), ((), ())), preferred_element_type=F32)


def dot_nt(a, b):
    return lax.dot_general(a, b, (((1,), (1,)), ((), ())), preferred_element_type=F32)


def dot_tn(a, b):
    return lax.dot_general(a, b, (((0,), (0,)), ((), ())), preferred_element_type=F32)


def stacked_heads(ref, first_row, rows, group):
    return jnp.concatenate(
        [
            ref[
                first_row : first_row + rows,
                (group * GROUP + h) * HEAD_SIZE : (group * GROUP + h + 1) * HEAD_SIZE,
            ]
            for h in range(GROUP)
        ],
        axis=0,
    )


def probs_and_grads(scores, grad_probs, allowed):
    scores = scores * (SCALE * LOG2E)
    if allowed is not None:
        scores = jnp.where(allowed, scores, -jnp.inf)
    raised = jnp.exp2(scores - jnp.max(scores, axis=0, keepdims=True))
    probs = raised * (1.0 / jnp.sum(raised, axis=0, keepdims=True))
    delta = jnp.sum(probs * grad_probs, axis=0, keepdims=True)
    grad_scores = (probs * (grad_probs - delta) * SCALE).astype(BF16)
    return probs.astype(BF16), grad_scores


def plan_kernel(tokens, cap, owner_any, slot_any, want_ref, owner_ref, slot_ref, sems):
    copies = [
        pltpu.make_async_copy(owner_any, owner_ref, sems.at[0]),
        pltpu.make_async_copy(slot_any, slot_ref, sems.at[1]),
    ]
    for copy in copies:
        copy.start()
    row = lax.broadcasted_iota(jnp.int32, want_ref.shape, 0)
    lane = lax.broadcasted_iota(jnp.int32, want_ref.shape, 1)
    place = row * cap + (lane // tokens) % cap
    token = lane % tokens
    want = jnp.full(want_ref.shape, -1, jnp.int32)
    for copy in copies:
        copy.wait()
    for i, j, owner, rank in ranked(owner_ref):
        want = jnp.where(place == owner * cap + rank, slot_ref[i, j] * tokens + token, want)
    want_ref[...] = want


def ranked(owner_ref):
    spans, per_span = owner_ref.shape
    owners, found = [], []
    for i in range(spans):
        for j in range(per_span):
            owner = owner_ref[i, j]
            rank = jnp.int32(0)
            for earlier in owners:
                rank = rank + jnp.where(earlier == owner, 1, 0)
            owners.append(owner)
            found.append((i, j, owner, rank))
    return found


def stage_kernel(
    rows_each,
    chunks,
    me_ref,
    z_ref,
    sibling_k_ref,
    sibling_v_ref,
    owner_any,
    sk_any,
    sv_any,
    k_any,
    v_any,
    store_ref,
    halo_ref,
    placed_ref,
    owner_ref,
    k_ref,
    v_ref,
    sems,
):
    store_refs = (k_ref, v_ref, sibling_k_ref, sibling_v_ref)
    slots, tokens, features = store_refs[0].shape
    kv_width = sk_any.shape[1]
    window = halo_ref.shape[0]
    tail = slice(sk_any.shape[0] - window, sk_any.shape[0])
    step = slots // chunks
    fetch_owner = pltpu.make_async_copy(owner_any, owner_ref, sems.at[0])
    fetch_owner.start()
    left, right = slice(0, kv_width), slice(kv_width, 2 * kv_width)
    copies = []
    for i in range(chunks):
        part = slice(i * step, (i + 1) * step)
        copies.append(pltpu.make_async_copy(k_any.at[part], k_ref.at[part], sems.at[3 + 2 * i]))
        copies.append(pltpu.make_async_copy(v_any.at[part], v_ref.at[part], sems.at[4 + 2 * i]))
    copies.append(pltpu.make_async_copy(sk_any.at[tail], halo_ref.at[:, left], sems.at[1]))
    copies.append(pltpu.make_async_copy(sv_any.at[tail], halo_ref.at[:, right], sems.at[2]))
    for copy in copies:
        copy.start()
    fetch_owner.wait()
    me = me_ref[0]
    lanes, used = placed_ref.shape
    lane = lax.broadcasted_iota(jnp.int32, (1, used), 1)
    place = lane % tokens
    for r, (_, _, owner, rank) in enumerate(ranked(owner_ref)):
        place = place + jnp.where(lane // tokens == r, (owner ^ me) * rows_each + rank * tokens, 0)
    row = lax.broadcasted_iota(jnp.int32, (lanes, used), 0)
    placed_ref[...] = jnp.where(row == place, 1.0, 0.0).astype(BF16)
    for i in range(chunks):
        part = slice(i * step, (i + 1) * step)
        copies[2 * i].wait()
        copies[2 * i + 1].wait()
        for j in range(4):
            core, kind = j // 2, j % 2
            first = (core * slots + i * step) * tokens
            rows = slice(first, first + step * tokens)
            for d, apart in enumerate(farthest_first(features // kv_width)):
                start = pl.multiple_of((z_ref[0] ^ apart) * kv_width, kv_width)
                at = (2 * d + kind) * kv_width
                store_ref[rows, at : at + kv_width] = store_refs[j][
                    part, :, pl.ds(start, kv_width)
                ].reshape(step * tokens, kv_width)
    for copy in copies[2 * chunks :]:
        copy.wait()


def pack_kernel(rows_each, me_ref, store_ref, *refs):
    pieces = len(refs) // 3
    wanted_refs, far_refs, near_refs, target_ref = (
        refs[:pieces],
        by_chip(refs[pieces : 2 * pieces]),
        by_chip(refs[2 * pieces : 3 * pieces]),
        refs[-1],
    )
    rows, columns = store_ref.shape[0], store_ref.shape[1] // 2
    lanes = target_ref.shape[1]
    width = wanted_refs[0].shape[1]
    me = me_ref[0]
    lane = lax.broadcasted_iota(jnp.int32, (1, width), 1)
    parts = [jnp.full((1, width), -1, jnp.int32) for _ in range(lanes // width)]
    for m, wanted_ref in enumerate(by_chip(wanted_refs)):
        for core in range(2):
            part, at = divmod((2 * m + core) * rows_each, width)
            from_there = wanted_ref[pl.ds(me ^ core, 1), :]
            here = (lane >= at) & (lane < at + rows_each)
            parts[part] = jnp.where(here, from_there, parts[part])
    target = jnp.concatenate(parts, axis=1)
    target_ref[...] = target
    second = (lax.broadcasted_iota(jnp.int32, (1, lanes), 1) // rows_each) % 2
    target = jnp.where(target >= 0, target + second * (rows // 2), -1)
    row = lax.broadcasted_iota(jnp.int32, (rows, lanes), 0)
    picks = jnp.where(row == target, 1.0, 0.0).astype(BF16)
    for half, send_refs in enumerate((far_refs, near_refs)):
        cols = slice(half * columns, (half + 1) * columns)
        picked = dot_tn(picks, store_ref[:, cols]).astype(BF16)
        for m, send_ref in enumerate(send_refs):
            send_ref[...] = picked[2 * m * rows_each : 2 * (m + 1) * rows_each]


def spread_kernel(parts, placed_ref, *refs):
    got_refs, send_refs = refs[: -parts], refs[-parts :]
    width = send_refs[0].shape[1]
    got = jnp.concatenate([ref[...] for ref in by_chip(got_refs)], axis=0)
    rows = dot_tn(placed_ref[...], got).astype(BF16)
    for i, send_ref in enumerate(send_refs):
        send_ref[...] = rows[:, i * width : (i + 1) * width]


def scatter_kernel(chips, placed_ref, *refs):
    grad_refs, send_refs = refs[:-chips], refs[-chips:]
    grads = jnp.concatenate([ref[...] for ref in grad_refs], axis=1)
    rows = dot_nn(placed_ref[...], grads).astype(BF16)
    step = send_refs[0].shape[0]
    for m, send_ref in enumerate(by_chip(send_refs)):
        send_ref[...] = rows[m * step : (m + 1) * step]


def part_cores_kernel(*refs):
    got_refs, (same_ref, other_ref) = refs[:-2], refs[-2:]
    chips = len(got_refs) // 2
    rows, columns = got_refs[0].shape[0] // 2, got_refs[0].shape[1]
    for half in range(2):
        cols = slice(half * columns, (half + 1) * columns)
        for m, got_ref in enumerate(by_chip(got_refs[half * chips : (half + 1) * chips])):
            here = slice(m * rows, (m + 1) * rows)
            same_ref[here, cols] = got_ref[:rows]
            other_ref[here, cols] = got_ref[rows:]


def self_kernel(
    rank_ref, q_ref, k_ref, v_ref, do_ref, halo_ref, out_ref, dq_ref, dkv_ref, back_ref
):
    tokens, kv_width = k_ref.shape
    block = WINDOW_KEYS
    blocks = tokens // block
    key_at = lax.broadcasted_iota(jnp.int32, (2 * block, GROUP * block), 0)
    query_at = lax.broadcasted_iota(jnp.int32, (2 * block, GROUP * block), 1) % block
    band = (key_at > query_at) & (key_at <= query_at + block)
    first_band = band & ((key_at >= block) | (rank_ref[0] > 0))
    for group in range(kv_width // HEAD_SIZE):
        cols = slice(group * HEAD_SIZE, (group + 1) * HEAD_SIZE)
        vcols = slice(kv_width + group * HEAD_SIZE, kv_width + (group + 1) * HEAD_SIZE)
        carried_k = carried_v = None
        for b in range(blocks):
            here = slice(b * block, (b + 1) * block)
            if b == 0:
                keys = jnp.concatenate([halo_ref[:, cols], k_ref[here, cols]], 0)
                values = jnp.concatenate([halo_ref[:, vcols], v_ref[here, cols]], 0)
            else:
                keys = k_ref[(b - 1) * block : (b + 1) * block, cols]
                values = v_ref[(b - 1) * block : (b + 1) * block, cols]
            query_rows = stacked_heads(q_ref, b * block, block, group)
            grad_rows = stacked_heads(do_ref, b * block, block, group)
            weights, grad_scores = probs_and_grads(
                dot_nt(keys, query_rows),
                dot_nt(values, grad_rows),
                first_band if b == 0 else band,
            )
            out = dot_tn(weights, values)
            dq = dot_tn(grad_scores, keys)
            for h in range(GROUP):
                head = slice((group * GROUP + h) * HEAD_SIZE, (group * GROUP + h + 1) * HEAD_SIZE)
                out_ref[here, head] = out[h * block : (h + 1) * block]
                dq_ref[here, head] = dq[h * block : (h + 1) * block]
            dk = dot_nn(grad_scores, query_rows)
            dv = dot_nn(weights, grad_rows)
            if b == 0:
                back_ref[:, cols] = dk[:block].astype(BF16)
                back_ref[:, vcols] = dv[:block].astype(BF16)
            else:
                before = slice((b - 1) * block, b * block)
                dkv_ref[before, cols] = carried_k + dk[:block]
                dkv_ref[before, vcols] = carried_v + dv[:block]
            carried_k, carried_v = dk[block:], dv[block:]
        last = slice((blocks - 1) * block, blocks * block)
        dkv_ref[last, cols] = carried_k
        dkv_ref[last, vcols] = carried_v


def span_rows(near_refs, span, rows, cols):
    return jnp.concatenate([ref[span * rows : (span + 1) * rows, cols] for ref in near_refs], axis=0)


def cross_kernel(tp, q_ref, do_ref, *refs):
    near_refs, grad_refs, w_ref, ds_ref = refs[:tp], refs[tp : 2 * tp], refs[2 * tp], refs[2 * tp + 1]
    kv_width = near_refs[0].shape[1] // 2
    groups = kv_width // HEAD_SIZE
    blocks, rows_span, columns = w_ref.shape
    rows = rows_span // tp
    queries, grads, scores, grad_probs = [], [], [], []
    for at in range(blocks):
        span, group = at // groups, at % groups
        cols = slice(group * HEAD_SIZE, (group + 1) * HEAD_SIZE)
        vcols = slice(kv_width + group * HEAD_SIZE, kv_width + (group + 1) * HEAD_SIZE)
        queries.append(stacked_heads(q_ref, span * SPAN_TOKENS, SPAN_TOKENS, group))
        grads.append(stacked_heads(do_ref, span * SPAN_TOKENS, SPAN_TOKENS, group))
        scores.append(dot_nt(span_rows(near_refs, span, rows, cols), queries[at]))
        grad_probs.append(dot_nt(span_rows(near_refs, span, rows, vcols), grads[at]))
    weights, grad_scores = probs_and_grads(
        jnp.concatenate(scores, axis=1), jnp.concatenate(grad_probs, axis=1), None
    )
    for at in range(blocks):
        span, group = at // groups, at % groups
        here = slice(span * rows, (span + 1) * rows)
        cols = slice(group * HEAD_SIZE, (group + 1) * HEAD_SIZE)
        vcols = slice(kv_width + group * HEAD_SIZE, kv_width + (group + 1) * HEAD_SIZE)
        part = slice(at * columns, (at + 1) * columns)
        w_ref[at] = weights[:, part]
        ds_ref[at] = grad_scores[:, part]
        dk = dot_nn(grad_scores[:, part], queries[at]).astype(BF16)
        dv = dot_nn(weights[:, part], grads[at]).astype(BF16)
        for i, grad_ref in enumerate(grad_refs):
            grad_ref[here, cols] = dk[i * rows : (i + 1) * rows]
            grad_ref[here, vcols] = dv[i * rows : (i + 1) * rows]


def join_kernel(tp, w_ref, ds_ref, out_ref, dq_ref, dkv_ref, back_ref, *refs):
    near_refs, (att_ref, qg_ref, kg_ref, vg_ref) = refs[:tp], refs[tp:]
    tokens, kv_width = kg_ref.shape
    groups = kv_width // HEAD_SIZE
    blocks, rows_span, _ = w_ref.shape
    for span in range(blocks // groups):
        rows = slice(span * SPAN_TOKENS, (span + 1) * SPAN_TOKENS)
        for group in range(groups):
            cols = slice(group * HEAD_SIZE, (group + 1) * HEAD_SIZE)
            vcols = slice(kv_width + group * HEAD_SIZE, kv_width + (group + 1) * HEAD_SIZE)
            at = span * groups + group
            out = dot_tn(w_ref[at], span_rows(near_refs, span, rows_span // tp, vcols))
            dq = dot_tn(ds_ref[at], span_rows(near_refs, span, rows_span // tp, cols))
            for h in range(GROUP):
                head = slice((group * GROUP + h) * HEAD_SIZE, (group * GROUP + h + 1) * HEAD_SIZE)
                part = slice(h * SPAN_TOKENS, (h + 1) * SPAN_TOKENS)
                att_ref[rows, head] = (out_ref[rows, head] + out[part]).astype(BF16)
                qg_ref[rows, head] = (dq_ref[rows, head] + dq[part]).astype(BF16)
    halo = back_ref.shape[0]
    kg_ref[: tokens - halo] = dkv_ref[: tokens - halo, :kv_width].astype(BF16)
    vg_ref[: tokens - halo] = dkv_ref[: tokens - halo, kv_width:].astype(BF16)
    kg_ref[tokens - halo :] = (
        dkv_ref[tokens - halo :, :kv_width] + back_ref[:, :kv_width].astype(F32)
    ).astype(BF16)
    vg_ref[tokens - halo :] = (
        dkv_ref[tokens - halo :, kv_width:] + back_ref[:, kv_width:].astype(F32)
    ).astype(BF16)


def sum_kernel(
    chunks,
    rows_each,
    z_ref,
    target_ref,
    other_ref,
    same_rows,
    other_rows,
    kg_any,
    vg_any,
    kg_ref,
    vg_ref,
    sems,
):
    slots, tokens, features = kg_ref.shape
    tp = NEIGHBOUR_LENGTH // tokens
    width = features // tp
    got = []
    for m in range(same_rows.shape[0] // rows_each):
        here = slice(m * rows_each, (m + 1) * rows_each)
        got += [same_rows[here], other_rows[here]]
    got = jnp.concatenate(got, axis=0)
    lanes = target_ref.shape[1]
    odd = (lax.broadcasted_iota(jnp.int32, (1, lanes), 1) // rows_each) % 2
    target = jnp.where(odd == 0, target_ref[...], other_ref[...])
    row = lax.broadcasted_iota(jnp.int32, (slots * tokens, lanes), 0)
    owned = jnp.where(row == target, 1.0, 0.0).astype(BF16)
    step = slots // chunks
    copies = []
    for i in range(chunks):
        part = slice(i * step, (i + 1) * step)
        total = dot_nn(owned[i * step * tokens : (i + 1) * step * tokens], got).astype(BF16)
        for d, apart in enumerate(farthest_first(tp)):
            cols = pl.ds(pl.multiple_of((z_ref[0] ^ apart) * width, width), width)
            at = 2 * d * width
            kg_ref[part, :, cols] = total[:, at : at + width].reshape(step, tokens, width)
            vg_ref[part, :, cols] = total[:, at + width : at + 2 * width].reshape(
                step, tokens, width
            )
        for j, (ref, out) in enumerate(((kg_ref, kg_any), (vg_ref, vg_any))):
            copies.append(pltpu.make_async_copy(ref.at[part], out.at[part], sems.at[2 * i + j]))
            copies[-1].start()
    for copy in copies:
        copy.wait()


def call(kernel, name, ins, outs, flops, bytes_accessed, scratch=(), scalars=0, fetched=0, stores=False):
    direct = len(ins) - fetched
    ins = ins[:direct] + tuple(
        pltpu.with_memory_space_constraint(each, pltpu.HBM) for each in ins[direct:]
    )
    return pl.pallas_call(
        kernel,
        out_shape=tuple(outs),
        in_specs=[SMEM] * scalars + [VMEM] * (direct - scalars) + [ANY] * fetched,
        out_specs=(ANY if stores else VMEM,) * len(outs),
        scratch_shapes=list(scratch),
        compiler_params=pltpu.CompilerParams(vmem_limit_bytes=16 * 1024 * 1024),
        cost_estimate=pl.CostEstimate(
            flops=flops, bytes_accessed=bytes_accessed, transcendentals=0
        ),
        name=name,
    )(*ins)


def swapped(block, axis, apart):
    return lax.ppermute(block, axis, [(i, i ^ apart) for i in range(lax.axis_size(axis))])


def chip_order(chips):
    return [0] + sorted(range(1, chips), key=lambda m: (-bin(m).count("1"), m))


def by_chip(refs):
    order = chip_order(len(refs))
    return [refs[order.index(m)] for m in range(len(refs))]


def between_chips(blocks):
    order = chip_order(len(blocks))
    return [blocks[0]] + [swapped(b, "seq", 2 * m) for b, m in zip(blocks[1:], order[1:])]


def farthest_first(tp):
    return distances(tp)[1:] + [0]


def distances(tp):
    return [0] + sorted(range(1, tp), key=lambda j: (j < 2, j))


def exchanged(blocks):
    apart = distances(len(blocks))
    return [blocks[0]] + [swapped(b, "tp", j) for b, j in zip(blocks[1:], apart[1:])]


def body(
    queries,
    sequence_keys,
    sequence_values,
    output_gradient,
    enc_keys,
    encoded_values,
    nbr_owner,
    nbr_slot,
):
    tokens_here, query_width = queries.shape
    kv_width = sequence_keys.shape[1]
    both = 2 * kv_width
    groups = kv_width // HEAD_SIZE
    devices = lax.axis_size("seq")
    tp = lax.axis_size("tp")
    spans, per_span = nbr_owner.shape
    requests = spans * per_span
    cap = max(2, 2 * requests // devices)
    tokens = enc_keys.shape[1]
    rows_each = cap * tokens
    window = WINDOW_KEYS
    struct = jax.ShapeDtypeStruct
    store_rows = enc_keys.shape[0] * tokens
    lanes = devices * rows_each
    used = requests * tokens
    int32 = jnp.int32
    rank = lax.axis_index("seq").astype(int32).reshape(1)
    z_rank = lax.axis_index("tp").astype(int32).reshape(1)

    sibling_keys = swapped(enc_keys, "seq", 1)
    sibling_values = swapped(encoded_values, "seq", 1)
    (want,) = call(
        functools.partial(plan_kernel, tokens, cap),
        "plan_requests",
        (nbr_owner, nbr_slot),
        (struct((devices, min(lanes, LANES)), int32),),
        0,
        100_000,
        scratch=[
            pltpu.SMEM(nbr_owner.shape, int32),
            pltpu.SMEM(nbr_slot.shape, int32),
            pltpu.SemaphoreType.DMA((2,)),
        ],
        fetched=2,
    )
    chips = devices // 2
    order = chip_order(chips)
    pieces = [want] + [swapped(want, "seq", 2 * m) for m in order[1:]]

    chunks = 4
    features = enc_keys.shape[2]
    store, halo, placed = call(
        functools.partial(stage_kernel, rows_each, chunks),
        "stage_store",
        (rank, z_rank, sibling_keys, sibling_values, nbr_owner, sequence_keys, sequence_values)
        + (enc_keys, encoded_values),
        (
            struct((2 * store_rows, 2 * features), BF16),
            struct((window, both), BF16),
            struct((lanes, used), BF16),
        ),
        0,
        5_000_000,
        scratch=[pltpu.SMEM(nbr_owner.shape, int32)]
        + [pltpu.VMEM(enc_keys.shape, BF16)] * 2
        + [pltpu.SemaphoreType.DMA((3 + 2 * chunks,))],
        scalars=2,
        fetched=5,
    )
    block = struct((2 * rows_each, features), BF16)
    *sent, target = call(
        functools.partial(pack_kernel, rows_each),
        "pack_requests",
        (rank, store, *pieces),
        [block] * (2 * chips) + [struct((1, lanes), int32)],
        200_000_000,
        2_000_000,
        scalars=1,
    )
    parts = tp // 2
    moved = []
    far, near = between_chips(sent[:chips]), sent[chips:]
    for name, got in (("spread_far", far), ("spread_near", between_chips(near))):
        moved += call(
            functools.partial(spread_kernel, parts),
            name,
            (placed, *got),
            [struct((used, both), BF16)] * parts,
            1_000_000,
            10_000,
        )
    near = exchanged(moved[-1:] + moved[:-1])
    halo = lax.ppermute(halo, "seq", [(i, (i + 1) % devices) for i in range(devices)])
    other_target = swapped(target, "seq", 1)
    self_out, self_dq, self_dkv, back = call(
        self_kernel,
        "self_attention",
        (rank, queries, sequence_keys, sequence_values, output_gradient, halo),
        (
            struct((tokens_here, query_width), F32),
            struct((tokens_here, query_width), F32),
            struct((tokens_here, both), F32),
            struct((window, both), BF16),
        ),
        1_000_000,
        10_000,
        scalars=1,
    )
    back = lax.ppermute(back, "seq", [((i + 1) % devices, i) for i in range(devices)])
    near[1], self_out = lax.optimization_barrier((near[1], self_out))

    blocks = spans * groups
    rows_span = per_span * NEIGHBOUR_LENGTH
    *grads, weights, grad_scores = call(
        functools.partial(cross_kernel, tp),
        "cross_attention",
        (queries, output_gradient, *near),
        [struct((used, both), BF16)] * tp
        + [struct((blocks, rows_span, GROUP * SPAN_TOKENS), BF16)] * 2,
        600_000_000,
        3_000_000,
    )
    grads = exchanged(grads)
    grads = grads[1:] + grads[:1]
    returned = []
    for name, half in (("scatter_near", grads[parts:]), ("scatter_far", grads[:parts])):
        if returned:
            half, returned[2] = lax.optimization_barrier((half, returned[2]))
        sent = call(
            functools.partial(scatter_kernel, chips),
            name,
            (placed, *half),
            [block] * chips,
            1_000_000,
            10_000,
        )
        if returned:
            sent, weights = lax.optimization_barrier((sent, weights))
        returned += between_chips(sent)
    returned = returned[chips:] + returned[:chips]
    attended, query_gradient, key_gradient, value_gradient = call(
        functools.partial(join_kernel, tp),
        "join_outputs",
        (weights, grad_scores, self_out, self_dq, self_dkv, back, *near),
        (
            struct((tokens_here, query_width), BF16),
            struct((tokens_here, query_width), BF16),
            struct((tokens_here, kv_width), BF16),
            struct((tokens_here, kv_width), BF16),
        ),
        300_000_000,
        5_000_000,
    )
    returned[0], attended = lax.optimization_barrier((returned[0], attended))
    same, other = call(
        part_cores_kernel,
        "part_cores",
        tuple(returned),
        [struct((lanes // 2, 2 * features), BF16)] * 2,
        0,
        10_000,
    )
    other = swapped(other, "seq", 1)

    store_kgrad, store_vgrad = call(
        functools.partial(sum_kernel, chunks, rows_each),
        "sum_store_gradients",
        (z_rank, target, other_target, same, other),
        (struct(enc_keys.shape, BF16), struct(encoded_values.shape, BF16)),
        200_000_000,
        2_000_000,
        scratch=[
            pltpu.VMEM(enc_keys.shape, BF16),
            pltpu.VMEM(encoded_values.shape, BF16),
            pltpu.SemaphoreType.DMA((2 * chunks,)),
        ],
        scalars=1,
        stores=True,
    )
    return (
        attended,
        query_gradient,
        key_gradient,
        value_gradient,
        store_kgrad,
        store_vgrad,
    )


def solution(mesh):
    arguments = (P("seq", "tp"),) * 4 + (P("seq", "tp", None),) * 2 + (P("seq", None),) * 2
    results = (P("seq", "tp"),) * 4 + (P("seq", "tp", None),) * 2
    return jax.shard_map(
        body, mesh=mesh, in_specs=arguments, out_specs=results, check_vma=False
    )
```

```python
import functools
import math

import jax
import jax.numpy as jnp
from jax import lax
from jax.experimental import pallas as pl
from jax.experimental.pallas import tpu as pltpu
from jax.sharding import PartitionSpec as P

QUERY_HEADS = 32
KEY_VALUE_HEADS = 8
HEAD_SIZE = 128
SPAN_TOKENS = 64
NEIGHBOUR_COUNT = 4
NEIGHBOUR_LENGTH = 16
WINDOW_KEYS = 128
GROUP = QUERY_HEADS // KEY_VALUE_HEADS
SCALE = 1.0 / math.sqrt(HEAD_SIZE)
LOG2E = math.log2(math.e)

F32 = jnp.float32
BF16 = jnp.bfloat16
VMEM = pl.BlockSpec(memory_space=pltpu.VMEM)
SMEM = pl.BlockSpec(memory_space=pltpu.SMEM)
ANY = pl.BlockSpec(memory_space=pl.ANY)
LANES = 128


def dot_nn(a, b):
    return lax.dot_general(a, b, (((1,), (0,)), ((), ())), preferred_element_type=F32)


def dot_nt(a, b):
    return lax.dot_general(a, b, (((1,), (1,)), ((), ())), preferred_element_type=F32)


def dot_tn(a, b):
    return lax.dot_general(a, b, (((0,), (0,)), ((), ())), preferred_element_type=F32)


def stacked_heads(ref, first_row, rows, group):
    return jnp.concatenate(
        [
            ref[
                first_row : first_row + rows,
                (group * GROUP + h) * HEAD_SIZE : (group * GROUP + h + 1) * HEAD_SIZE,
            ]
            for h in range(GROUP)
        ],
        axis=0,
    )


def probs_and_grads(scores, grad_probs, allowed):
    scores = scores * (SCALE * LOG2E)
    if allowed is not None:
        scores = jnp.where(allowed, scores, -jnp.inf)
    raised = jnp.exp2(scores - jnp.max(scores, axis=0, keepdims=True))
    probs = raised * (1.0 / jnp.sum(raised, axis=0, keepdims=True))
    delta = jnp.sum(probs * grad_probs, axis=0, keepdims=True)
    grad_scores = (probs * (grad_probs - delta) * SCALE).astype(BF16)
    return probs.astype(BF16), grad_scores


def plan_kernel(tokens, cap, owner_any, slot_any, want_ref, owner_ref, slot_ref, sems):
    copies = [
        pltpu.make_async_copy(owner_any, owner_ref, sems.at[0]),
        pltpu.make_async_copy(slot_any, slot_ref, sems.at[1]),
    ]
    for copy in copies:
        copy.start()
    row = lax.broadcasted_iota(jnp.int32, want_ref.shape, 0)
    lane = lax.broadcasted_iota(jnp.int32, want_ref.shape, 1)
    place = row * cap + (lane // tokens) % cap
    token = lane % tokens
    want = jnp.full(want_ref.shape, -1, jnp.int32)
    for copy in copies:
        copy.wait()
    for i, j, owner, rank in ranked(owner_ref):
        want = jnp.where(place == owner * cap + rank, slot_ref[i, j] * tokens + token, want)
    want_ref[...] = want


def ranked(owner_ref):
    spans, per_span = owner_ref.shape
    owners, found = [], []
    for i in range(spans):
        for j in range(per_span):
            owner = owner_ref[i, j]
            rank = jnp.int32(0)
            for earlier in owners:
                rank = rank + jnp.where(earlier == owner, 1, 0)
            owners.append(owner)
            found.append((i, j, owner, rank))
    return found


def stage_kernel(
    rows_each,
    chunks,
    me_ref,
    z_ref,
    sibling_k_ref,
    sibling_v_ref,
    owner_any,
    sk_any,
    sv_any,
    k_any,
    v_any,
    store_ref,
    halo_ref,
    placed_ref,
    owner_ref,
    k_ref,
    v_ref,
    sems,
):
    store_refs = (k_ref, v_ref, sibling_k_ref, sibling_v_ref)
    slots, tokens, features = store_refs[0].shape
    kv_width = sk_any.shape[1]
    window = halo_ref.shape[0]
    tail = slice(sk_any.shape[0] - window, sk_any.shape[0])
    step = slots // chunks
    fetch_owner = pltpu.make_async_copy(owner_any, owner_ref, sems.at[0])
    fetch_owner.start()
    left, right = slice(0, kv_width), slice(kv_width, 2 * kv_width)
    copies = []
    for i in range(chunks):
        part = slice(i * step, (i + 1) * step)
        copies.append(pltpu.make_async_copy(k_any.at[part], k_ref.at[part], sems.at[3 + 2 * i]))
        copies.append(pltpu.make_async_copy(v_any.at[part], v_ref.at[part], sems.at[4 + 2 * i]))
    copies.append(pltpu.make_async_copy(sk_any.at[tail], halo_ref.at[:, left], sems.at[1]))
    copies.append(pltpu.make_async_copy(sv_any.at[tail], halo_ref.at[:, right], sems.at[2]))
    for copy in copies:
        copy.start()
    fetch_owner.wait()
    me = me_ref[0]
    lanes, used = placed_ref.shape
    lane = lax.broadcasted_iota(jnp.int32, (1, used), 1)
    place = lane % tokens
    for r, (_, _, owner, rank) in enumerate(ranked(owner_ref)):
        place = place + jnp.where(lane // tokens == r, (owner ^ me) * rows_each + rank * tokens, 0)
    row = lax.broadcasted_iota(jnp.int32, (lanes, used), 0)
    placed_ref[...] = jnp.where(row == place, 1.0, 0.0).astype(BF16)
    for i in range(chunks):
        part = slice(i * step, (i + 1) * step)
        copies[2 * i].wait()
        copies[2 * i + 1].wait()
        for j in range(4):
            core, kind = j // 2, j % 2
            first = (core * slots + i * step) * tokens
            rows = slice(first, first + step * tokens)
            for d, apart in enumerate(farthest_first(features // kv_width)):
                start = pl.multiple_of((z_ref[0] ^ apart) * kv_width, kv_width)
                at = (2 * d + kind) * kv_width
                store_ref[rows, at : at + kv_width] = store_refs[j][
                    part, :, pl.ds(start, kv_width)
                ].reshape(step * tokens, kv_width)
    for copy in copies[2 * chunks :]:
        copy.wait()


def pack_kernel(rows_each, me_ref, store_ref, *refs):
    pieces = len(refs) // 3
    wanted_refs, far_refs, near_refs, target_ref = (
        refs[:pieces],
        by_chip(refs[pieces : 2 * pieces]),
        by_chip(refs[2 * pieces : 3 * pieces]),
        refs[-1],
    )
    rows = store_ref.shape[0]
    lanes = target_ref.shape[1]
    width = wanted_refs[0].shape[1]
    me = me_ref[0]
    lane = lax.broadcasted_iota(jnp.int32, (1, width), 1)
    parts = [jnp.full((1, width), -1, jnp.int32) for _ in range(lanes // width)]
    for m, wanted_ref in enumerate(by_chip(wanted_refs)):
        for core in range(2):
            part, at = divmod((2 * m + core) * rows_each, width)
            from_there = wanted_ref[pl.ds(me ^ core, 1), :]
            here = (lane >= at) & (lane < at + rows_each)
            parts[part] = jnp.where(here, from_there, parts[part])
    target = jnp.concatenate(parts, axis=1)
    target_ref[...] = target
    second = (lax.broadcasted_iota(jnp.int32, (1, lanes), 1) // rows_each) % 2
    target = jnp.where(target >= 0, target + second * (rows // 2), -1)
    row = lax.broadcasted_iota(jnp.int32, (rows, lanes), 0)
    picks = jnp.where(row == target, 1.0, 0.0).astype(BF16)
    split = far_refs[0].shape[1]
    for cols, send_refs in ((slice(0, split), far_refs), (slice(split, None), near_refs)):
        picked = dot_tn(picks, store_ref[:, cols]).astype(BF16)
        for m, send_ref in enumerate(send_refs):
            send_ref[...] = picked[2 * m * rows_each : 2 * (m + 1) * rows_each]


def spread_kernel(parts, placed_ref, *refs):
    got_refs, send_refs = refs[: -parts], refs[-parts :]
    width = send_refs[0].shape[1]
    got = jnp.concatenate([ref[...] for ref in by_chip(got_refs)], axis=0)
    rows = dot_tn(placed_ref[...], got).astype(BF16)
    for i, send_ref in enumerate(send_refs):
        send_ref[...] = rows[:, i * width : (i + 1) * width]


def scatter_kernel(chips, placed_ref, *refs):
    grad_refs, send_refs = refs[:-chips], refs[-chips:]
    grads = jnp.concatenate([ref[...] for ref in grad_refs], axis=1)
    rows = dot_nn(placed_ref[...], grads).astype(BF16)
    step = send_refs[0].shape[0]
    for m, send_ref in enumerate(by_chip(send_refs)):
        send_ref[...] = rows[m * step : (m + 1) * step]


def part_cores_kernel(*refs):
    got_refs, (same_ref, other_ref) = refs[:-2], refs[-2:]
    chips = len(got_refs) // 2
    rows, columns = got_refs[0].shape[0] // 2, got_refs[0].shape[1]
    for half in range(2):
        cols = slice(half * columns, (half + 1) * columns)
        for m, got_ref in enumerate(by_chip(got_refs[half * chips : (half + 1) * chips])):
            here = slice(m * rows, (m + 1) * rows)
            same_ref[here, cols] = got_ref[:rows]
            other_ref[here, cols] = got_ref[rows:]


def self_kernel(
    rank_ref, q_ref, k_ref, v_ref, do_ref, halo_ref, out_ref, dq_ref, dkv_ref, back_ref
):
    tokens, kv_width = k_ref.shape
    block = WINDOW_KEYS
    blocks = tokens // block
    key_at = lax.broadcasted_iota(jnp.int32, (2 * block, GROUP * block), 0)
    query_at = lax.broadcasted_iota(jnp.int32, (2 * block, GROUP * block), 1) % block
    band = (key_at > query_at) & (key_at <= query_at + block)
    first_band = band & ((key_at >= block) | (rank_ref[0] > 0))
    for group in range(kv_width // HEAD_SIZE):
        cols = slice(group * HEAD_SIZE, (group + 1) * HEAD_SIZE)
        vcols = slice(kv_width + group * HEAD_SIZE, kv_width + (group + 1) * HEAD_SIZE)
        carried_k = carried_v = None
        for b in range(blocks):
            here = slice(b * block, (b + 1) * block)
            if b == 0:
                keys = jnp.concatenate([halo_ref[:, cols], k_ref[here, cols]], 0)
                values = jnp.concatenate([halo_ref[:, vcols], v_ref[here, cols]], 0)
            else:
                keys = k_ref[(b - 1) * block : (b + 1) * block, cols]
                values = v_ref[(b - 1) * block : (b + 1) * block, cols]
            query_rows = stacked_heads(q_ref, b * block, block, group)
            grad_rows = stacked_heads(do_ref, b * block, block, group)
            weights, grad_scores = probs_and_grads(
                dot_nt(keys, query_rows),
                dot_nt(values, grad_rows),
                first_band if b == 0 else band,
            )
            out = dot_tn(weights, values)
            dq = dot_tn(grad_scores, keys)
            for h in range(GROUP):
                head = slice((group * GROUP + h) * HEAD_SIZE, (group * GROUP + h + 1) * HEAD_SIZE)
                out_ref[here, head] = out[h * block : (h + 1) * block]
                dq_ref[here, head] = dq[h * block : (h + 1) * block]
            dk = dot_nn(grad_scores, query_rows)
            dv = dot_nn(weights, grad_rows)
            if b == 0:
                back_ref[:, cols] = dk[:block].astype(BF16)
                back_ref[:, vcols] = dv[:block].astype(BF16)
            else:
                before = slice((b - 1) * block, b * block)
                dkv_ref[before, cols] = carried_k + dk[:block]
                dkv_ref[before, vcols] = carried_v + dv[:block]
            carried_k, carried_v = dk[block:], dv[block:]
        last = slice((blocks - 1) * block, blocks * block)
        dkv_ref[last, cols] = carried_k
        dkv_ref[last, vcols] = carried_v


def span_rows(near_refs, span, rows, cols):
    return jnp.concatenate([ref[span * rows : (span + 1) * rows, cols] for ref in near_refs], axis=0)


def cross_kernel(tp, q_ref, do_ref, *refs):
    near_refs, grad_refs, w_ref, ds_ref = refs[:tp], refs[tp : 2 * tp], refs[2 * tp], refs[2 * tp + 1]
    kv_width = near_refs[0].shape[1] // 2
    groups = kv_width // HEAD_SIZE
    blocks, rows_span, columns = w_ref.shape
    rows = rows_span // tp
    queries, grads, scores, grad_probs = [], [], [], []
    for at in range(blocks):
        span, group = at // groups, at % groups
        cols = slice(group * HEAD_SIZE, (group + 1) * HEAD_SIZE)
        vcols = slice(kv_width + group * HEAD_SIZE, kv_width + (group + 1) * HEAD_SIZE)
        queries.append(stacked_heads(q_ref, span * SPAN_TOKENS, SPAN_TOKENS, group))
        grads.append(stacked_heads(do_ref, span * SPAN_TOKENS, SPAN_TOKENS, group))
        scores.append(dot_nt(span_rows(near_refs, span, rows, cols), queries[at]))
        grad_probs.append(dot_nt(span_rows(near_refs, span, rows, vcols), grads[at]))
    weights, grad_scores = probs_and_grads(
        jnp.concatenate(scores, axis=1), jnp.concatenate(grad_probs, axis=1), None
    )
    for at in range(blocks):
        span, group = at // groups, at % groups
        here = slice(span * rows, (span + 1) * rows)
        cols = slice(group * HEAD_SIZE, (group + 1) * HEAD_SIZE)
        vcols = slice(kv_width + group * HEAD_SIZE, kv_width + (group + 1) * HEAD_SIZE)
        part = slice(at * columns, (at + 1) * columns)
        w_ref[at] = weights[:, part]
        ds_ref[at] = grad_scores[:, part]
        dk = dot_nn(grad_scores[:, part], queries[at]).astype(BF16)
        dv = dot_nn(weights[:, part], grads[at]).astype(BF16)
        for i, grad_ref in enumerate(grad_refs):
            grad_ref[here, cols] = dk[i * rows : (i + 1) * rows]
            grad_ref[here, vcols] = dv[i * rows : (i + 1) * rows]


def join_kernel(tp, w_ref, ds_ref, out_ref, dq_ref, dkv_ref, back_ref, *refs):
    near_refs, (att_ref, qg_ref, kg_ref, vg_ref) = refs[:tp], refs[tp:]
    tokens, kv_width = kg_ref.shape
    groups = kv_width // HEAD_SIZE
    blocks, rows_span, _ = w_ref.shape
    for span in range(blocks // groups):
        rows = slice(span * SPAN_TOKENS, (span + 1) * SPAN_TOKENS)
        for group in range(groups):
            cols = slice(group * HEAD_SIZE, (group + 1) * HEAD_SIZE)
            vcols = slice(kv_width + group * HEAD_SIZE, kv_width + (group + 1) * HEAD_SIZE)
            at = span * groups + group
            out = dot_tn(w_ref[at], span_rows(near_refs, span, rows_span // tp, vcols))
            dq = dot_tn(ds_ref[at], span_rows(near_refs, span, rows_span // tp, cols))
            for h in range(GROUP):
                head = slice((group * GROUP + h) * HEAD_SIZE, (group * GROUP + h + 1) * HEAD_SIZE)
                part = slice(h * SPAN_TOKENS, (h + 1) * SPAN_TOKENS)
                att_ref[rows, head] = (out_ref[rows, head] + out[part]).astype(BF16)
                qg_ref[rows, head] = (dq_ref[rows, head] + dq[part]).astype(BF16)
    halo = back_ref.shape[0]
    kg_ref[: tokens - halo] = dkv_ref[: tokens - halo, :kv_width].astype(BF16)
    vg_ref[: tokens - halo] = dkv_ref[: tokens - halo, kv_width:].astype(BF16)
    kg_ref[tokens - halo :] = (
        dkv_ref[tokens - halo :, :kv_width] + back_ref[:, :kv_width].astype(F32)
    ).astype(BF16)
    vg_ref[tokens - halo :] = (
        dkv_ref[tokens - halo :, kv_width:] + back_ref[:, kv_width:].astype(F32)
    ).astype(BF16)


def sum_kernel(
    chunks,
    rows_each,
    z_ref,
    target_ref,
    other_ref,
    same_rows,
    other_rows,
    kg_any,
    vg_any,
    kg_ref,
    vg_ref,
    sems,
):
    slots, tokens, features = kg_ref.shape
    tp = NEIGHBOUR_LENGTH // tokens
    width = features // tp
    got = []
    for m in range(same_rows.shape[0] // rows_each):
        here = slice(m * rows_each, (m + 1) * rows_each)
        got += [same_rows[here], other_rows[here]]
    got = jnp.concatenate(got, axis=0)
    lanes = target_ref.shape[1]
    odd = (lax.broadcasted_iota(jnp.int32, (1, lanes), 1) // rows_each) % 2
    target = jnp.where(odd == 0, target_ref[...], other_ref[...])
    row = lax.broadcasted_iota(jnp.int32, (slots * tokens, lanes), 0)
    owned = jnp.where(row == target, 1.0, 0.0).astype(BF16)
    step = slots // chunks
    copies = []
    for i in range(chunks):
        part = slice(i * step, (i + 1) * step)
        total = dot_nn(owned[i * step * tokens : (i + 1) * step * tokens], got).astype(BF16)
        for d, apart in enumerate(farthest_first(tp)):
            cols = pl.ds(pl.multiple_of((z_ref[0] ^ apart) * width, width), width)
            at = 2 * d * width
            kg_ref[part, :, cols] = total[:, at : at + width].reshape(step, tokens, width)
            vg_ref[part, :, cols] = total[:, at + width : at + 2 * width].reshape(
                step, tokens, width
            )
        for j, (ref, out) in enumerate(((kg_ref, kg_any), (vg_ref, vg_any))):
            copies.append(pltpu.make_async_copy(ref.at[part], out.at[part], sems.at[2 * i + j]))
            copies[-1].start()
    for copy in copies:
        copy.wait()


def call(kernel, name, ins, outs, flops, bytes_accessed, scratch=(), scalars=0, fetched=0, stores=False):
    direct = len(ins) - fetched
    ins = ins[:direct] + tuple(
        pltpu.with_memory_space_constraint(each, pltpu.HBM) for each in ins[direct:]
    )
    return pl.pallas_call(
        kernel,
        out_shape=tuple(outs),
        in_specs=[SMEM] * scalars + [VMEM] * (direct - scalars) + [ANY] * fetched,
        out_specs=(ANY if stores else VMEM,) * len(outs),
        scratch_shapes=list(scratch),
        compiler_params=pltpu.CompilerParams(vmem_limit_bytes=16 * 1024 * 1024),
        cost_estimate=pl.CostEstimate(
            flops=flops, bytes_accessed=bytes_accessed, transcendentals=0
        ),
        name=name,
    )(*ins)


def swapped(block, axis, apart):
    return lax.ppermute(block, axis, [(i, i ^ apart) for i in range(lax.axis_size(axis))])


def chip_order(chips):
    return [0] + sorted(range(1, chips), key=lambda m: (-bin(m).count("1"), m))


def by_chip(refs):
    order = chip_order(len(refs))
    return [refs[order.index(m)] for m in range(len(refs))]


def between_chips(blocks):
    order = chip_order(len(blocks))
    return [blocks[0]] + [swapped(b, "seq", 2 * m) for b, m in zip(blocks[1:], order[1:])]


def farthest_first(tp):
    return distances(tp)[1:] + [0]


def distances(tp):
    return [0] + sorted(range(1, tp), key=lambda j: (j < 2, j))


def exchanged(blocks):
    apart = distances(len(blocks))
    return [blocks[0]] + [swapped(b, "tp", j) for b, j in zip(blocks[1:], apart[1:])]


def body(
    queries,
    sequence_keys,
    sequence_values,
    output_gradient,
    enc_keys,
    encoded_values,
    nbr_owner,
    nbr_slot,
):
    tokens_here, query_width = queries.shape
    kv_width = sequence_keys.shape[1]
    both = 2 * kv_width
    groups = kv_width // HEAD_SIZE
    devices = lax.axis_size("seq")
    tp = lax.axis_size("tp")
    spans, per_span = nbr_owner.shape
    requests = spans * per_span
    cap = max(2, 2 * requests // devices)
    tokens = enc_keys.shape[1]
    rows_each = cap * tokens
    window = WINDOW_KEYS
    struct = jax.ShapeDtypeStruct
    store_rows = enc_keys.shape[0] * tokens
    lanes = devices * rows_each
    used = requests * tokens
    int32 = jnp.int32
    rank = lax.axis_index("seq").astype(int32).reshape(1)
    z_rank = lax.axis_index("tp").astype(int32).reshape(1)

    sibling_keys = swapped(enc_keys, "seq", 1)
    sibling_values = swapped(encoded_values, "seq", 1)
    (want,) = call(
        functools.partial(plan_kernel, tokens, cap),
        "plan_requests",
        (nbr_owner, nbr_slot),
        (struct((devices, min(lanes, LANES)), int32),),
        0,
        100_000,
        scratch=[
            pltpu.SMEM(nbr_owner.shape, int32),
            pltpu.SMEM(nbr_slot.shape, int32),
            pltpu.SemaphoreType.DMA((2,)),
        ],
        fetched=2,
    )
    chips = devices // 2
    order = chip_order(chips)
    pieces = [want] + [swapped(want, "seq", 2 * m) for m in order[1:]]

    chunks = 4
    features = enc_keys.shape[2]
    store, halo, placed = call(
        functools.partial(stage_kernel, rows_each, chunks),
        "stage_store",
        (rank, z_rank, sibling_keys, sibling_values, nbr_owner, sequence_keys, sequence_values)
        + (enc_keys, encoded_values),
        (
            struct((2 * store_rows, 2 * features), BF16),
            struct((window, both), BF16),
            struct((lanes, used), BF16),
        ),
        0,
        5_000_000,
        scratch=[pltpu.SMEM(nbr_owner.shape, int32)]
        + [pltpu.VMEM(enc_keys.shape, BF16)] * 2
        + [pltpu.SemaphoreType.DMA((3 + 2 * chunks,))],
        scalars=2,
        fetched=5,
    )
    block = struct((2 * rows_each, features), BF16)
    *sent, target = call(
        functools.partial(pack_kernel, rows_each),
        "pack_requests",
        (rank, store, *pieces),
        [struct((2 * rows_each, (tp - 1) * both), BF16)] * chips
        + [struct((2 * rows_each, both), BF16)] * chips
        + [struct((1, lanes), int32)],
        200_000_000,
        2_000_000,
        scalars=1,
    )
    parts = tp // 2
    far, near = sent[:chips], sent[chips:]
    moved = call(
        functools.partial(spread_kernel, tp - 1),
        "spread_far",
        (placed, *between_chips(far)),
        [struct((used, both), BF16)] * (tp - 1),
        1_000_000,
        10_000,
    )
    moved = list(moved)
    moved += call(
        functools.partial(spread_kernel, 1),
        "spread_near",
        (placed, *between_chips(near)),
        [struct((used, both), BF16)],
        1_000_000,
        10_000,
    )
    near = exchanged(moved[-1:] + moved[:-1])
    halo = lax.ppermute(halo, "seq", [(i, (i + 1) % devices) for i in range(devices)])
    other_target = swapped(target, "seq", 1)
    self_out, self_dq, self_dkv, back = call(
        self_kernel,
        "self_attention",
        (rank, queries, sequence_keys, sequence_values, output_gradient, halo),
        (
            struct((tokens_here, query_width), F32),
            struct((tokens_here, query_width), F32),
            struct((tokens_here, both), F32),
            struct((window, both), BF16),
        ),
        1_000_000,
        10_000,
        scalars=1,
    )
    back = lax.ppermute(back, "seq", [((i + 1) % devices, i) for i in range(devices)])
    near[1], self_out = lax.optimization_barrier((near[1], self_out))

    blocks = spans * groups
    rows_span = per_span * NEIGHBOUR_LENGTH
    *grads, weights, grad_scores = call(
        functools.partial(cross_kernel, tp),
        "cross_attention",
        (queries, output_gradient, *near),
        [struct((used, both), BF16)] * tp
        + [struct((blocks, rows_span, GROUP * SPAN_TOKENS), BF16)] * 2,
        600_000_000,
        3_000_000,
    )
    grads = exchanged(grads)
    grads = grads[1:] + grads[:1]
    returned = []
    for name, half in (("scatter_near", grads[parts:]), ("scatter_far", grads[:parts])):
        if returned:
            half, returned[2], other_target = lax.optimization_barrier(
                (half, returned[2], other_target)
            )
        sent = call(
            functools.partial(scatter_kernel, chips),
            name,
            (placed, *half),
            [block] * chips,
            1_000_000,
            10_000,
        )
        if returned:
            sent, weights = lax.optimization_barrier((sent, weights))
        returned += between_chips(sent)
    returned = returned[chips:] + returned[:chips]
    attended, query_gradient, key_gradient, value_gradient = call(
        functools.partial(join_kernel, tp),
        "join_outputs",
        (weights, grad_scores, self_out, self_dq, self_dkv, back, *near),
        (
            struct((tokens_here, query_width), BF16),
            struct((tokens_here, query_width), BF16),
            struct((tokens_here, kv_width), BF16),
            struct((tokens_here, kv_width), BF16),
        ),
        300_000_000,
        5_000_000,
    )
    returned[0], attended = lax.optimization_barrier((returned[0], attended))
    same, other = call(
        part_cores_kernel,
        "part_cores",
        tuple(returned),
        [struct((lanes // 2, 2 * features), BF16)] * 2,
        0,
        10_000,
    )
    other = swapped(other, "seq", 1)

    store_kgrad, store_vgrad = call(
        functools.partial(sum_kernel, chunks, rows_each),
        "sum_store_gradients",
        (z_rank, target, other_target, same, other),
        (struct(enc_keys.shape, BF16), struct(encoded_values.shape, BF16)),
        200_000_000,
        2_000_000,
        scratch=[
            pltpu.VMEM(enc_keys.shape, BF16),
            pltpu.VMEM(encoded_values.shape, BF16),
            pltpu.SemaphoreType.DMA((2 * chunks,)),
        ],
        scalars=1,
        stores=True,
    )
    return (
        attended,
        query_gradient,
        key_gradient,
        value_gradient,
        store_kgrad,
        store_vgrad,
    )


def solution(mesh):
    arguments = (P("seq", "tp"),) * 4 + (P("seq", "tp", None),) * 2 + (P("seq", None),) * 2
    results = (P("seq", "tp"),) * 4 + (P("seq", "tp", None),) * 2
    return jax.shard_map(
        body, mesh=mesh, in_specs=arguments, out_specs=results, check_vma=False
    )
```

```python
import functools
import math

import jax
import jax.numpy as jnp
from jax import lax
from jax.experimental import pallas as pl
from jax.experimental.pallas import tpu as pltpu
from jax.sharding import PartitionSpec as P

QUERY_HEADS = 32
KEY_VALUE_HEADS = 8
HEAD_SIZE = 128
SPAN_TOKENS = 64
NEIGHBOUR_COUNT = 4
NEIGHBOUR_LENGTH = 16
WINDOW_KEYS = 128
GROUP = QUERY_HEADS // KEY_VALUE_HEADS
SCALE = 1.0 / math.sqrt(HEAD_SIZE)
LOG2E = math.log2(math.e)

F32 = jnp.float32
BF16 = jnp.bfloat16
VMEM = pl.BlockSpec(memory_space=pltpu.VMEM)
SMEM = pl.BlockSpec(memory_space=pltpu.SMEM)
ANY = pl.BlockSpec(memory_space=pl.ANY)
LANES = 128


def dot_nn(a, b):
    return lax.dot_general(a, b, (((1,), (0,)), ((), ())), preferred_element_type=F32)


def dot_nt(a, b):
    return lax.dot_general(a, b, (((1,), (1,)), ((), ())), preferred_element_type=F32)


def dot_tn(a, b):
    return lax.dot_general(a, b, (((0,), (0,)), ((), ())), preferred_element_type=F32)


def stacked_heads(ref, first_row, rows, group):
    return jnp.concatenate(
        [
            ref[
                first_row : first_row + rows,
                (group * GROUP + h) * HEAD_SIZE : (group * GROUP + h + 1) * HEAD_SIZE,
            ]
            for h in range(GROUP)
        ],
        axis=0,
    )


def probs_and_grads(scores, grad_probs, allowed):
    scores = scores * (SCALE * LOG2E)
    if allowed is not None:
        scores = jnp.where(allowed, scores, -jnp.inf)
    raised = jnp.exp2(scores - jnp.max(scores, axis=0, keepdims=True))
    probs = raised * (1.0 / jnp.sum(raised, axis=0, keepdims=True))
    delta = jnp.sum(probs * grad_probs, axis=0, keepdims=True)
    grad_scores = (probs * (grad_probs - delta) * SCALE).astype(BF16)
    return probs.astype(BF16), grad_scores


def plan_kernel(tokens, cap, owner_any, slot_any, want_ref, owner_ref, slot_ref, sems):
    copies = [
        pltpu.make_async_copy(owner_any, owner_ref, sems.at[0]),
        pltpu.make_async_copy(slot_any, slot_ref, sems.at[1]),
    ]
    for copy in copies:
        copy.start()
    row = lax.broadcasted_iota(jnp.int32, want_ref.shape, 0)
    lane = lax.broadcasted_iota(jnp.int32, want_ref.shape, 1)
    place = row * cap + (lane // tokens) % cap
    token = lane % tokens
    want = jnp.full(want_ref.shape, -1, jnp.int32)
    for copy in copies:
        copy.wait()
    for i, j, owner, rank in ranked(owner_ref):
        want = jnp.where(place == owner * cap + rank, slot_ref[i, j] * tokens + token, want)
    want_ref[...] = want


def ranked(owner_ref):
    spans, per_span = owner_ref.shape
    owners, found = [], []
    for i in range(spans):
        for j in range(per_span):
            owner = owner_ref[i, j]
            rank = jnp.int32(0)
            for earlier in owners:
                rank = rank + jnp.where(earlier == owner, 1, 0)
            owners.append(owner)
            found.append((i, j, owner, rank))
    return found


def stage_kernel(
    rows_each,
    chunks,
    me_ref,
    z_ref,
    sibling_k_ref,
    sibling_v_ref,
    owner_any,
    sk_any,
    sv_any,
    k_any,
    v_any,
    store_ref,
    halo_ref,
    placed_ref,
    owner_ref,
    k_ref,
    v_ref,
    sems,
):
    store_refs = (k_ref, v_ref, sibling_k_ref, sibling_v_ref)
    slots, tokens, features = store_refs[0].shape
    kv_width = sk_any.shape[1]
    window = halo_ref.shape[0]
    tail = slice(sk_any.shape[0] - window, sk_any.shape[0])
    step = slots // chunks
    fetch_owner = pltpu.make_async_copy(owner_any, owner_ref, sems.at[0])
    fetch_owner.start()
    left, right = slice(0, kv_width), slice(kv_width, 2 * kv_width)
    copies = []
    for i in range(chunks):
        part = slice(i * step, (i + 1) * step)
        copies.append(pltpu.make_async_copy(k_any.at[part], k_ref.at[part], sems.at[3 + 2 * i]))
        copies.append(pltpu.make_async_copy(v_any.at[part], v_ref.at[part], sems.at[4 + 2 * i]))
    copies.append(pltpu.make_async_copy(sk_any.at[tail], halo_ref.at[:, left], sems.at[1]))
    copies.append(pltpu.make_async_copy(sv_any.at[tail], halo_ref.at[:, right], sems.at[2]))
    for copy in copies:
        copy.start()
    fetch_owner.wait()
    me = me_ref[0]
    lanes, used = placed_ref.shape
    lane = lax.broadcasted_iota(jnp.int32, (1, used), 1)
    place = lane % tokens
    for r, (_, _, owner, rank) in enumerate(ranked(owner_ref)):
        place = place + jnp.where(lane // tokens == r, (owner ^ me) * rows_each + rank * tokens, 0)
    row = lax.broadcasted_iota(jnp.int32, (lanes, used), 0)
    placed_ref[...] = jnp.where(row == place, 1.0, 0.0).astype(BF16)
    for i in range(chunks):
        part = slice(i * step, (i + 1) * step)
        copies[2 * i].wait()
        copies[2 * i + 1].wait()
        for j in range(4):
            core, kind = j // 2, j % 2
            first = (core * slots + i * step) * tokens
            rows = slice(first, first + step * tokens)
            for d, apart in enumerate(farthest_first(features // kv_width)):
                start = pl.multiple_of((z_ref[0] ^ apart) * kv_width, kv_width)
                at = (2 * d + kind) * kv_width
                store_ref[rows, at : at + kv_width] = store_refs[j][
                    part, :, pl.ds(start, kv_width)
                ].reshape(step * tokens, kv_width)
    for copy in copies[2 * chunks :]:
        copy.wait()


def pack_kernel(rows_each, me_ref, store_ref, *refs):
    pieces = len(refs) // 3
    wanted_refs, far_refs, near_refs, target_ref = (
        refs[:pieces],
        by_chip(refs[pieces : 2 * pieces]),
        by_chip(refs[2 * pieces : 3 * pieces]),
        refs[-1],
    )
    rows, columns = store_ref.shape[0], store_ref.shape[1] // 2
    lanes = target_ref.shape[1]
    width = wanted_refs[0].shape[1]
    me = me_ref[0]
    lane = lax.broadcasted_iota(jnp.int32, (1, width), 1)
    parts = [jnp.full((1, width), -1, jnp.int32) for _ in range(lanes // width)]
    for m, wanted_ref in enumerate(by_chip(wanted_refs)):
        for core in range(2):
            part, at = divmod((2 * m + core) * rows_each, width)
            from_there = wanted_ref[pl.ds(me ^ core, 1), :]
            here = (lane >= at) & (lane < at + rows_each)
            parts[part] = jnp.where(here, from_there, parts[part])
    target = jnp.concatenate(parts, axis=1)
    target_ref[...] = target
    second = (lax.broadcasted_iota(jnp.int32, (1, lanes), 1) // rows_each) % 2
    target = jnp.where(target >= 0, target + second * (rows // 2), -1)
    row = lax.broadcasted_iota(jnp.int32, (rows, lanes), 0)
    picks = jnp.where(row == target, 1.0, 0.0).astype(BF16)
    for half, send_refs in enumerate((far_refs, near_refs)):
        cols = slice(half * columns, (half + 1) * columns)
        picked = dot_tn(picks, store_ref[:, cols]).astype(BF16)
        for m, send_ref in enumerate(send_refs):
            send_ref[...] = picked[2 * m * rows_each : 2 * (m + 1) * rows_each]


def spread_kernel(parts, placed_ref, *refs):
    got_refs, send_refs = refs[: -parts], refs[-parts :]
    width = send_refs[0].shape[1]
    got = jnp.concatenate([ref[...] for ref in by_chip(got_refs)], axis=0)
    rows = dot_tn(placed_ref[...], got).astype(BF16)
    for i, send_ref in enumerate(send_refs):
        send_ref[...] = rows[:, i * width : (i + 1) * width]


def scatter_kernel(chips, placed_ref, *refs):
    grad_refs, send_refs = refs[:-chips], refs[-chips:]
    grads = jnp.concatenate([ref[...] for ref in grad_refs], axis=1)
    rows = dot_nn(placed_ref[...], grads).astype(BF16)
    step = send_refs[0].shape[0]
    for m, send_ref in enumerate(by_chip(send_refs)):
        send_ref[...] = rows[m * step : (m + 1) * step]


def part_cores_kernel(*refs):
    got_refs, (same_ref, other_ref) = refs[:-2], refs[-2:]
    chips = len(got_refs) // 2
    rows, columns = got_refs[0].shape[0] // 2, got_refs[0].shape[1]
    for half in range(2):
        cols = slice(half * columns, (half + 1) * columns)
        for m, got_ref in enumerate(by_chip(got_refs[half * chips : (half + 1) * chips])):
            here = slice(m * rows, (m + 1) * rows)
            same_ref[here, cols] = got_ref[:rows]
            other_ref[here, cols] = got_ref[rows:]


def self_kernel(
    rank_ref, q_ref, k_ref, v_ref, do_ref, halo_ref, out_ref, dq_ref, dkv_ref, back_ref
):
    tokens, kv_width = k_ref.shape
    block = WINDOW_KEYS
    blocks = tokens // block
    key_at = lax.broadcasted_iota(jnp.int32, (2 * block, GROUP * block), 0)
    query_at = lax.broadcasted_iota(jnp.int32, (2 * block, GROUP * block), 1) % block
    band = (key_at > query_at) & (key_at <= query_at + block)
    first_band = band & ((key_at >= block) | (rank_ref[0] > 0))
    for group in range(kv_width // HEAD_SIZE):
        cols = slice(group * HEAD_SIZE, (group + 1) * HEAD_SIZE)
        vcols = slice(kv_width + group * HEAD_SIZE, kv_width + (group + 1) * HEAD_SIZE)
        carried_k = carried_v = None
        for b in range(blocks):
            here = slice(b * block, (b + 1) * block)
            if b == 0:
                keys = jnp.concatenate([halo_ref[:, cols], k_ref[here, cols]], 0)
                values = jnp.concatenate([halo_ref[:, vcols], v_ref[here, cols]], 0)
            else:
                keys = k_ref[(b - 1) * block : (b + 1) * block, cols]
                values = v_ref[(b - 1) * block : (b + 1) * block, cols]
            query_rows = stacked_heads(q_ref, b * block, block, group)
            grad_rows = stacked_heads(do_ref, b * block, block, group)
            weights, grad_scores = probs_and_grads(
                dot_nt(keys, query_rows),
                dot_nt(values, grad_rows),
                first_band if b == 0 else band,
            )
            out = dot_tn(weights, values)
            dq = dot_tn(grad_scores, keys)
            for h in range(GROUP):
                head = slice((group * GROUP + h) * HEAD_SIZE, (group * GROUP + h + 1) * HEAD_SIZE)
                out_ref[here, head] = out[h * block : (h + 1) * block]
                dq_ref[here, head] = dq[h * block : (h + 1) * block]
            dk = dot_nn(grad_scores, query_rows)
            dv = dot_nn(weights, grad_rows)
            if b == 0:
                back_ref[:, cols] = dk[:block].astype(BF16)
                back_ref[:, vcols] = dv[:block].astype(BF16)
            else:
                before = slice((b - 1) * block, b * block)
                dkv_ref[before, cols] = carried_k + dk[:block]
                dkv_ref[before, vcols] = carried_v + dv[:block]
            carried_k, carried_v = dk[block:], dv[block:]
        last = slice((blocks - 1) * block, blocks * block)
        dkv_ref[last, cols] = carried_k
        dkv_ref[last, vcols] = carried_v


def span_rows(near_refs, span, rows, cols):
    return jnp.concatenate([ref[span * rows : (span + 1) * rows, cols] for ref in near_refs], axis=0)


def cross_kernel(tp, q_ref, do_ref, *refs):
    near_refs, grad_refs, w_ref, ds_ref = refs[:tp], refs[tp : 2 * tp], refs[2 * tp], refs[2 * tp + 1]
    kv_width = near_refs[0].shape[1] // 2
    groups = kv_width // HEAD_SIZE
    blocks, rows_span, columns = w_ref.shape
    rows = rows_span // tp
    queries, grads, scores, grad_probs = [], [], [], []
    for at in range(blocks):
        span, group = at // groups, at % groups
        cols = slice(group * HEAD_SIZE, (group + 1) * HEAD_SIZE)
        vcols = slice(kv_width + group * HEAD_SIZE, kv_width + (group + 1) * HEAD_SIZE)
        queries.append(stacked_heads(q_ref, span * SPAN_TOKENS, SPAN_TOKENS, group))
        grads.append(stacked_heads(do_ref, span * SPAN_TOKENS, SPAN_TOKENS, group))
        scores.append(dot_nt(span_rows(near_refs, span, rows, cols), queries[at]))
        grad_probs.append(dot_nt(span_rows(near_refs, span, rows, vcols), grads[at]))
    weights, grad_scores = probs_and_grads(
        jnp.concatenate(scores, axis=1), jnp.concatenate(grad_probs, axis=1), None
    )
    for at in range(blocks):
        span, group = at // groups, at % groups
        here = slice(span * rows, (span + 1) * rows)
        cols = slice(group * HEAD_SIZE, (group + 1) * HEAD_SIZE)
        vcols = slice(kv_width + group * HEAD_SIZE, kv_width + (group + 1) * HEAD_SIZE)
        part = slice(at * columns, (at + 1) * columns)
        w_ref[at] = weights[:, part]
        ds_ref[at] = grad_scores[:, part]
        dk = dot_nn(grad_scores[:, part], queries[at]).astype(BF16)
        dv = dot_nn(weights[:, part], grads[at]).astype(BF16)
        for i, grad_ref in enumerate(grad_refs):
            grad_ref[here, cols] = dk[i * rows : (i + 1) * rows]
            grad_ref[here, vcols] = dv[i * rows : (i + 1) * rows]


def add_cross(rows_span, p_ref, self_ref, out_ref, near_refs, first_col, groups):
    for at in range(p_ref.shape[0]):
        span, group = at // groups, at % groups
        rows = slice(span * SPAN_TOKENS, (span + 1) * SPAN_TOKENS)
        cols = slice(first_col + group * HEAD_SIZE, first_col + (group + 1) * HEAD_SIZE)
        cross = dot_tn(p_ref[at], span_rows(near_refs, span, rows_span // len(near_refs), cols))
        for h in range(GROUP):
            head = slice((group * GROUP + h) * HEAD_SIZE, (group * GROUP + h + 1) * HEAD_SIZE)
            part = slice(h * SPAN_TOKENS, (h + 1) * SPAN_TOKENS)
            out_ref[rows, head] = (self_ref[rows, head] + cross[part]).astype(BF16)


def join_attended_kernel(w_ref, out_ref, *refs):
    near_refs, att_ref = refs[:-1], refs[-1]
    kv_width = near_refs[0].shape[1] // 2
    add_cross(
        w_ref.shape[1], w_ref, out_ref, att_ref, near_refs, kv_width, kv_width // HEAD_SIZE
    )


def join_gradients_kernel(tp, ds_ref, dq_ref, dkv_ref, back_ref, *refs):
    near_refs, (qg_ref, kg_ref, vg_ref) = refs[:tp], refs[tp:]
    tokens, kv_width = kg_ref.shape
    add_cross(ds_ref.shape[1], ds_ref, dq_ref, qg_ref, near_refs, 0, kv_width // HEAD_SIZE)
    halo = back_ref.shape[0]
    kg_ref[: tokens - halo] = dkv_ref[: tokens - halo, :kv_width].astype(BF16)
    vg_ref[: tokens - halo] = dkv_ref[: tokens - halo, kv_width:].astype(BF16)
    kg_ref[tokens - halo :] = (
        dkv_ref[tokens - halo :, :kv_width] + back_ref[:, :kv_width].astype(F32)
    ).astype(BF16)
    vg_ref[tokens - halo :] = (
        dkv_ref[tokens - halo :, kv_width:] + back_ref[:, kv_width:].astype(F32)
    ).astype(BF16)


def sum_kernel(
    chunks,
    rows_each,
    z_ref,
    target_ref,
    other_ref,
    same_rows,
    other_rows,
    kg_any,
    vg_any,
    kg_ref,
    vg_ref,
    sems,
):
    slots, tokens, features = kg_ref.shape
    tp = NEIGHBOUR_LENGTH // tokens
    width = features // tp
    got = []
    for m in range(same_rows.shape[0] // rows_each):
        here = slice(m * rows_each, (m + 1) * rows_each)
        got += [same_rows[here], other_rows[here]]
    got = jnp.concatenate(got, axis=0)
    lanes = target_ref.shape[1]
    odd = (lax.broadcasted_iota(jnp.int32, (1, lanes), 1) // rows_each) % 2
    target = jnp.where(odd == 0, target_ref[...], other_ref[...])
    row = lax.broadcasted_iota(jnp.int32, (slots * tokens, lanes), 0)
    owned = jnp.where(row == target, 1.0, 0.0).astype(BF16)
    step = slots // chunks
    copies = []
    for i in range(chunks):
        part = slice(i * step, (i + 1) * step)
        total = dot_nn(owned[i * step * tokens : (i + 1) * step * tokens], got).astype(BF16)
        for d, apart in enumerate(farthest_first(tp)):
            cols = pl.ds(pl.multiple_of((z_ref[0] ^ apart) * width, width), width)
            at = 2 * d * width
            kg_ref[part, :, cols] = total[:, at : at + width].reshape(step, tokens, width)
            vg_ref[part, :, cols] = total[:, at + width : at + 2 * width].reshape(
                step, tokens, width
            )
        for j, (ref, out) in enumerate(((kg_ref, kg_any), (vg_ref, vg_any))):
            copies.append(pltpu.make_async_copy(ref.at[part], out.at[part], sems.at[2 * i + j]))
            copies[-1].start()
    for copy in copies:
        copy.wait()


def call(kernel, name, ins, outs, flops, bytes_accessed, scratch=(), scalars=0, fetched=0, stores=False):
    direct = len(ins) - fetched
    ins = ins[:direct] + tuple(
        pltpu.with_memory_space_constraint(each, pltpu.HBM) for each in ins[direct:]
    )
    return pl.pallas_call(
        kernel,
        out_shape=tuple(outs),
        in_specs=[SMEM] * scalars + [VMEM] * (direct - scalars) + [ANY] * fetched,
        out_specs=(ANY if stores else VMEM,) * len(outs),
        scratch_shapes=list(scratch),
        compiler_params=pltpu.CompilerParams(vmem_limit_bytes=16 * 1024 * 1024),
        cost_estimate=pl.CostEstimate(
            flops=flops, bytes_accessed=bytes_accessed, transcendentals=0
        ),
        name=name,
    )(*ins)


def swapped(block, axis, apart):
    return lax.ppermute(block, axis, [(i, i ^ apart) for i in range(lax.axis_size(axis))])


def chip_order(chips):
    return [0] + sorted(range(1, chips), key=lambda m: (-bin(m).count("1"), m))


def by_chip(refs):
    order = chip_order(len(refs))
    return [refs[order.index(m)] for m in range(len(refs))]


def between_chips(blocks):
    order = chip_order(len(blocks))
    return [blocks[0]] + [swapped(b, "seq", 2 * m) for b, m in zip(blocks[1:], order[1:])]


def farthest_first(tp):
    return distances(tp)[1:] + [0]


def distances(tp):
    return [0] + sorted(range(1, tp), key=lambda j: (j < 2, j))


def exchanged(blocks):
    apart = distances(len(blocks))
    return [blocks[0]] + [swapped(b, "tp", j) for b, j in zip(blocks[1:], apart[1:])]


def body(
    queries,
    sequence_keys,
    sequence_values,
    output_gradient,
    enc_keys,
    encoded_values,
    nbr_owner,
    nbr_slot,
):
    tokens_here, query_width = queries.shape
    kv_width = sequence_keys.shape[1]
    both = 2 * kv_width
    groups = kv_width // HEAD_SIZE
    devices = lax.axis_size("seq")
    tp = lax.axis_size("tp")
    spans, per_span = nbr_owner.shape
    requests = spans * per_span
    cap = max(2, 2 * requests // devices)
    tokens = enc_keys.shape[1]
    rows_each = cap * tokens
    window = WINDOW_KEYS
    struct = jax.ShapeDtypeStruct
    store_rows = enc_keys.shape[0] * tokens
    lanes = devices * rows_each
    used = requests * tokens
    int32 = jnp.int32
    rank = lax.axis_index("seq").astype(int32).reshape(1)
    z_rank = lax.axis_index("tp").astype(int32).reshape(1)

    sibling_keys = swapped(enc_keys, "seq", 1)
    sibling_values = swapped(encoded_values, "seq", 1)
    (want,) = call(
        functools.partial(plan_kernel, tokens, cap),
        "plan_requests",
        (nbr_owner, nbr_slot),
        (struct((devices, min(lanes, LANES)), int32),),
        0,
        100_000,
        scratch=[
            pltpu.SMEM(nbr_owner.shape, int32),
            pltpu.SMEM(nbr_slot.shape, int32),
            pltpu.SemaphoreType.DMA((2,)),
        ],
        fetched=2,
    )
    chips = devices // 2
    order = chip_order(chips)
    pieces = [want] + [swapped(want, "seq", 2 * m) for m in order[1:]]

    chunks = 4
    features = enc_keys.shape[2]
    store, halo, placed = call(
        functools.partial(stage_kernel, rows_each, chunks),
        "stage_store",
        (rank, z_rank, sibling_keys, sibling_values, nbr_owner, sequence_keys, sequence_values)
        + (enc_keys, encoded_values),
        (
            struct((2 * store_rows, 2 * features), BF16),
            struct((window, both), BF16),
            struct((lanes, used), BF16),
        ),
        0,
        5_000_000,
        scratch=[pltpu.SMEM(nbr_owner.shape, int32)]
        + [pltpu.VMEM(enc_keys.shape, BF16)] * 2
        + [pltpu.SemaphoreType.DMA((3 + 2 * chunks,))],
        scalars=2,
        fetched=5,
    )
    block = struct((2 * rows_each, features), BF16)
    *sent, target = call(
        functools.partial(pack_kernel, rows_each),
        "pack_requests",
        (rank, store, *pieces),
        [block] * (2 * chips) + [struct((1, lanes), int32)],
        200_000_000,
        2_000_000,
        scalars=1,
    )
    parts = tp // 2
    moved = []
    far, near = between_chips(sent[:chips]), sent[chips:]
    for name, got in (("spread_far", far), ("spread_near", between_chips(near))):
        moved += call(
            functools.partial(spread_kernel, parts),
            name,
            (placed, *got),
            [struct((used, both), BF16)] * parts,
            1_000_000,
            10_000,
        )
    near = exchanged(moved[-1:] + moved[:-1])
    halo = lax.ppermute(halo, "seq", [(i, (i + 1) % devices) for i in range(devices)])
    other_target = swapped(target, "seq", 1)
    self_out, self_dq, self_dkv, back = call(
        self_kernel,
        "self_attention",
        (rank, queries, sequence_keys, sequence_values, output_gradient, halo),
        (
            struct((tokens_here, query_width), F32),
            struct((tokens_here, query_width), F32),
            struct((tokens_here, both), F32),
            struct((window, both), BF16),
        ),
        1_000_000,
        10_000,
        scalars=1,
    )
    back = lax.ppermute(back, "seq", [((i + 1) % devices, i) for i in range(devices)])
    near[1], self_out = lax.optimization_barrier((near[1], self_out))

    blocks = spans * groups
    rows_span = per_span * NEIGHBOUR_LENGTH
    *grads, weights, grad_scores = call(
        functools.partial(cross_kernel, tp),
        "cross_attention",
        (queries, output_gradient, *near),
        [struct((used, both), BF16)] * tp
        + [struct((blocks, rows_span, GROUP * SPAN_TOKENS), BF16)] * 2,
        600_000_000,
        3_000_000,
    )
    grads = exchanged(grads)
    grads = grads[1:] + grads[:1]
    returned = []
    for name, half in (("scatter_near", grads[parts:]), ("scatter_far", grads[:parts])):
        if returned:
            half, returned[2] = lax.optimization_barrier((half, returned[2]))
        sent = call(
            functools.partial(scatter_kernel, chips),
            name,
            (placed, *half),
            [block] * chips,
            1_000_000,
            10_000,
        )
        if returned:
            sent, weights = lax.optimization_barrier((sent, weights))
        returned += between_chips(sent)
    returned = returned[chips:] + returned[:chips]
    (attended,) = call(
        join_attended_kernel,
        "join_attended",
        (weights, self_out, *near),
        (struct((tokens_here, query_width), BF16),),
        1_000_000,
        10_000,
    )
    returned[0], attended, other_target = lax.optimization_barrier(
        (returned[0], attended, other_target)
    )
    same, other = call(
        part_cores_kernel,
        "part_cores",
        tuple(returned),
        [struct((lanes // 2, 2 * features), BF16)] * 2,
        0,
        10_000,
    )
    same, grad_scores = lax.optimization_barrier((same, grad_scores))
    other = swapped(other, "seq", 1)

    query_gradient, key_gradient, value_gradient = call(
        functools.partial(join_gradients_kernel, tp),
        "join_gradients",
        (grad_scores, self_dq, self_dkv, back, *near),
        (
            struct((tokens_here, query_width), BF16),
            struct((tokens_here, kv_width), BF16),
            struct((tokens_here, kv_width), BF16),
        ),
        1_000_000,
        10_000,
    )
    other, query_gradient = lax.optimization_barrier((other, query_gradient))

    store_kgrad, store_vgrad = call(
        functools.partial(sum_kernel, chunks, rows_each),
        "sum_store_gradients",
        (z_rank, target, other_target, same, other),
        (struct(enc_keys.shape, BF16), struct(encoded_values.shape, BF16)),
        200_000_000,
        2_000_000,
        scratch=[
            pltpu.VMEM(enc_keys.shape, BF16),
            pltpu.VMEM(encoded_values.shape, BF16),
            pltpu.SemaphoreType.DMA((2 * chunks,)),
        ],
        scalars=1,
        stores=True,
    )
    return (
        attended,
        query_gradient,
        key_gradient,
        value_gradient,
        store_kgrad,
        store_vgrad,
    )


def solution(mesh):
    arguments = (P("seq", "tp"),) * 4 + (P("seq", "tp", None),) * 2 + (P("seq", None),) * 2
    results = (P("seq", "tp"),) * 4 + (P("seq", "tp", None),) * 2
    return jax.shard_map(
        body, mesh=mesh, in_specs=arguments, out_specs=results, check_vma=False
    )
```

```python
import functools
import math

import jax
import jax.numpy as jnp
from jax import lax
from jax.experimental import pallas as pl
from jax.experimental.pallas import tpu as pltpu
from jax.sharding import PartitionSpec as P

QUERY_HEADS = 32
KEY_VALUE_HEADS = 8
HEAD_SIZE = 128
SPAN_TOKENS = 64
NEIGHBOUR_COUNT = 4
NEIGHBOUR_LENGTH = 16
WINDOW_KEYS = 128
GROUP = QUERY_HEADS // KEY_VALUE_HEADS
SCALE = 1.0 / math.sqrt(HEAD_SIZE)
LOG2E = math.log2(math.e)

F32 = jnp.float32
BF16 = jnp.bfloat16
VMEM = pl.BlockSpec(memory_space=pltpu.VMEM)
SMEM = pl.BlockSpec(memory_space=pltpu.SMEM)
ANY = pl.BlockSpec(memory_space=pl.ANY)
LANES = 128


def dot_nn(a, b):
    return lax.dot_general(a, b, (((1,), (0,)), ((), ())), preferred_element_type=F32)


def dot_nt(a, b):
    return lax.dot_general(a, b, (((1,), (1,)), ((), ())), preferred_element_type=F32)


def dot_tn(a, b):
    return lax.dot_general(a, b, (((0,), (0,)), ((), ())), preferred_element_type=F32)


def stacked_heads(ref, first_row, rows, group):
    return jnp.concatenate(
        [
            ref[
                first_row : first_row + rows,
                (group * GROUP + h) * HEAD_SIZE : (group * GROUP + h + 1) * HEAD_SIZE,
            ]
            for h in range(GROUP)
        ],
        axis=0,
    )


def probs_and_grads(scores, grad_probs, allowed):
    scores = scores * (SCALE * LOG2E)
    if allowed is not None:
        scores = jnp.where(allowed, scores, -jnp.inf)
    raised = jnp.exp2(scores - jnp.max(scores, axis=0, keepdims=True))
    probs = raised * (1.0 / jnp.sum(raised, axis=0, keepdims=True))
    delta = jnp.sum(probs * grad_probs, axis=0, keepdims=True)
    grad_scores = (probs * (grad_probs - delta) * SCALE).astype(BF16)
    return probs.astype(BF16), grad_scores


def plan_kernel(tokens, cap, owner_any, slot_any, want_ref, owner_ref, slot_ref, sems):
    copies = [
        pltpu.make_async_copy(owner_any, owner_ref, sems.at[0]),
        pltpu.make_async_copy(slot_any, slot_ref, sems.at[1]),
    ]
    for copy in copies:
        copy.start()
    row = lax.broadcasted_iota(jnp.int32, want_ref.shape, 0)
    lane = lax.broadcasted_iota(jnp.int32, want_ref.shape, 1)
    place = row * cap + (lane // tokens) % cap
    token = lane % tokens
    want = jnp.full(want_ref.shape, -1, jnp.int32)
    for copy in copies:
        copy.wait()
    for i, j, owner, rank in ranked(owner_ref):
        want = jnp.where(place == owner * cap + rank, slot_ref[i, j] * tokens + token, want)
    want_ref[...] = want


def ranked(owner_ref):
    spans, per_span = owner_ref.shape
    owners, found = [], []
    for i in range(spans):
        for j in range(per_span):
            owner = owner_ref[i, j]
            rank = jnp.int32(0)
            for earlier in owners:
                rank = rank + jnp.where(earlier == owner, 1, 0)
            owners.append(owner)
            found.append((i, j, owner, rank))
    return found


def stage_kernel(
    rows_each,
    chunks,
    me_ref,
    z_ref,
    sibling_k_ref,
    sibling_v_ref,
    owner_any,
    sk_any,
    sv_any,
    k_any,
    v_any,
    store_ref,
    halo_ref,
    placed_ref,
    owner_ref,
    k_ref,
    v_ref,
    sems,
):
    store_refs = (k_ref, v_ref, sibling_k_ref, sibling_v_ref)
    slots, tokens, features = store_refs[0].shape
    kv_width = sk_any.shape[1]
    window = halo_ref.shape[0]
    tail = slice(sk_any.shape[0] - window, sk_any.shape[0])
    step = slots // chunks
    fetch_owner = pltpu.make_async_copy(owner_any, owner_ref, sems.at[0])
    fetch_owner.start()
    left, right = slice(0, kv_width), slice(kv_width, 2 * kv_width)
    copies = []
    for i in range(chunks):
        part = slice(i * step, (i + 1) * step)
        copies.append(pltpu.make_async_copy(k_any.at[part], k_ref.at[part], sems.at[3 + 2 * i]))
        copies.append(pltpu.make_async_copy(v_any.at[part], v_ref.at[part], sems.at[4 + 2 * i]))
    copies.append(pltpu.make_async_copy(sk_any.at[tail], halo_ref.at[:, left], sems.at[1]))
    copies.append(pltpu.make_async_copy(sv_any.at[tail], halo_ref.at[:, right], sems.at[2]))
    for copy in copies:
        copy.start()
    fetch_owner.wait()
    me = me_ref[0]
    lanes, used = placed_ref.shape
    lane = lax.broadcasted_iota(jnp.int32, (1, used), 1)
    place = lane % tokens
    for r, (_, _, owner, rank) in enumerate(ranked(owner_ref)):
        place = place + jnp.where(lane // tokens == r, (owner ^ me) * rows_each + rank * tokens, 0)
    row = lax.broadcasted_iota(jnp.int32, (lanes, used), 0)
    placed_ref[...] = jnp.where(row == place, 1.0, 0.0).astype(BF16)
    for i in range(chunks):
        part = slice(i * step, (i + 1) * step)
        copies[2 * i].wait()
        copies[2 * i + 1].wait()
        for j in range(4):
            core, kind = j // 2, j % 2
            first = (core * slots + i * step) * tokens
            rows = slice(first, first + step * tokens)
            for d, apart in enumerate(farthest_first(features // kv_width)):
                start = pl.multiple_of((z_ref[0] ^ apart) * kv_width, kv_width)
                at = (2 * d + kind) * kv_width
                store_ref[rows, at : at + kv_width] = store_refs[j][
                    part, :, pl.ds(start, kv_width)
                ].reshape(step * tokens, kv_width)
    for copy in copies[2 * chunks :]:
        copy.wait()


def pack_kernel(rows_each, me_ref, store_ref, *refs):
    pieces = len(refs) // 3
    wanted_refs, far_refs, near_refs, target_ref = (
        refs[:pieces],
        by_chip(refs[pieces : 2 * pieces]),
        by_chip(refs[2 * pieces : 3 * pieces]),
        refs[-1],
    )
    rows, columns = store_ref.shape[0], store_ref.shape[1] // 2
    lanes = target_ref.shape[1]
    width = wanted_refs[0].shape[1]
    me = me_ref[0]
    lane = lax.broadcasted_iota(jnp.int32, (1, width), 1)
    parts = [jnp.full((1, width), -1, jnp.int32) for _ in range(lanes // width)]
    for m, wanted_ref in enumerate(by_chip(wanted_refs)):
        for core in range(2):
            part, at = divmod((2 * m + core) * rows_each, width)
            from_there = wanted_ref[pl.ds(me ^ core, 1), :]
            here = (lane >= at) & (lane < at + rows_each)
            parts[part] = jnp.where(here, from_there, parts[part])
    target = jnp.concatenate(parts, axis=1)
    target_ref[...] = target
    second = (lax.broadcasted_iota(jnp.int32, (1, lanes), 1) // rows_each) % 2
    target = jnp.where(target >= 0, target + second * (rows // 2), -1)
    row = lax.broadcasted_iota(jnp.int32, (rows, lanes), 0)
    picks = jnp.where(row == target, 1.0, 0.0).astype(BF16)
    for half, send_refs in enumerate((far_refs, near_refs)):
        cols = slice(half * columns, (half + 1) * columns)
        picked = dot_tn(picks, store_ref[:, cols]).astype(BF16)
        for m, send_ref in enumerate(send_refs):
            send_ref[...] = picked[2 * m * rows_each : 2 * (m + 1) * rows_each]


def spread_kernel(parts, placed_ref, *refs):
    got_refs, send_refs = refs[: -parts], refs[-parts :]
    width = send_refs[0].shape[1]
    got = jnp.concatenate([ref[...] for ref in by_chip(got_refs)], axis=0)
    rows = dot_tn(placed_ref[...], got).astype(BF16)
    for i, send_ref in enumerate(send_refs):
        send_ref[...] = rows[:, i * width : (i + 1) * width]


def scatter_kernel(chips, placed_ref, *refs):
    grad_refs, send_refs = refs[:-chips], refs[-chips:]
    grads = jnp.concatenate([ref[...] for ref in grad_refs], axis=1)
    rows = dot_nn(placed_ref[...], grads).astype(BF16)
    step = send_refs[0].shape[0]
    for m, send_ref in enumerate(by_chip(send_refs)):
        send_ref[...] = rows[m * step : (m + 1) * step]


def part_cores_kernel(*refs):
    got_refs, (same_ref, other_ref) = refs[:-2], refs[-2:]
    chips = len(got_refs) // 2
    rows, columns = got_refs[0].shape[0] // 2, got_refs[0].shape[1]
    for half in range(2):
        cols = slice(half * columns, (half + 1) * columns)
        for m, got_ref in enumerate(by_chip(got_refs[half * chips : (half + 1) * chips])):
            here = slice(m * rows, (m + 1) * rows)
            same_ref[here, cols] = got_ref[:rows]
            other_ref[here, cols] = got_ref[rows:]


def self_kernel(
    rank_ref, q_ref, k_ref, v_ref, do_ref, halo_ref, out_ref, dq_ref, dkv_ref, back_ref
):
    tokens, kv_width = k_ref.shape
    block = WINDOW_KEYS
    blocks = tokens // block
    key_at = lax.broadcasted_iota(jnp.int32, (2 * block, GROUP * block), 0)
    query_at = lax.broadcasted_iota(jnp.int32, (2 * block, GROUP * block), 1) % block
    band = (key_at > query_at) & (key_at <= query_at + block)
    first_band = band & ((key_at >= block) | (rank_ref[0] > 0))
    for group in range(kv_width // HEAD_SIZE):
        cols = slice(group * HEAD_SIZE, (group + 1) * HEAD_SIZE)
        vcols = slice(kv_width + group * HEAD_SIZE, kv_width + (group + 1) * HEAD_SIZE)
        carried_k = carried_v = None
        for b in range(blocks):
            here = slice(b * block, (b + 1) * block)
            if b == 0:
                keys = jnp.concatenate([halo_ref[:, cols], k_ref[here, cols]], 0)
                values = jnp.concatenate([halo_ref[:, vcols], v_ref[here, cols]], 0)
            else:
                keys = k_ref[(b - 1) * block : (b + 1) * block, cols]
                values = v_ref[(b - 1) * block : (b + 1) * block, cols]
            query_rows = stacked_heads(q_ref, b * block, block, group)
            grad_rows = stacked_heads(do_ref, b * block, block, group)
            weights, grad_scores = probs_and_grads(
                dot_nt(keys, query_rows),
                dot_nt(values, grad_rows),
                first_band if b == 0 else band,
            )
            out = dot_tn(weights, values)
            dq = dot_tn(grad_scores, keys)
            for h in range(GROUP):
                head = slice((group * GROUP + h) * HEAD_SIZE, (group * GROUP + h + 1) * HEAD_SIZE)
                out_ref[here, head] = out[h * block : (h + 1) * block]
                dq_ref[here, head] = dq[h * block : (h + 1) * block]
            dk = dot_nn(grad_scores, query_rows)
            dv = dot_nn(weights, grad_rows)
            if b == 0:
                back_ref[:, cols] = dk[:block].astype(BF16)
                back_ref[:, vcols] = dv[:block].astype(BF16)
            else:
                before = slice((b - 1) * block, b * block)
                dkv_ref[before, cols] = carried_k + dk[:block]
                dkv_ref[before, vcols] = carried_v + dv[:block]
            carried_k, carried_v = dk[block:], dv[block:]
        last = slice((blocks - 1) * block, blocks * block)
        dkv_ref[last, cols] = carried_k
        dkv_ref[last, vcols] = carried_v


def span_rows(near_refs, span, rows, cols):
    return jnp.concatenate([ref[span * rows : (span + 1) * rows, cols] for ref in near_refs], axis=0)


def cross_kernel(tp, q_ref, do_ref, *refs):
    near_refs, grad_refs, w_ref, ds_ref = refs[:tp], refs[tp : 2 * tp], refs[2 * tp], refs[2 * tp + 1]
    kv_width = near_refs[0].shape[1] // 2
    groups = kv_width // HEAD_SIZE
    blocks, rows_span, columns = w_ref.shape
    rows = rows_span // tp
    queries, grads, scores, grad_probs = [], [], [], []
    for at in range(blocks):
        span, group = at // groups, at % groups
        cols = slice(group * HEAD_SIZE, (group + 1) * HEAD_SIZE)
        vcols = slice(kv_width + group * HEAD_SIZE, kv_width + (group + 1) * HEAD_SIZE)
        queries.append(stacked_heads(q_ref, span * SPAN_TOKENS, SPAN_TOKENS, group))
        grads.append(stacked_heads(do_ref, span * SPAN_TOKENS, SPAN_TOKENS, group))
        scores.append(dot_nt(span_rows(near_refs, span, rows, cols), queries[at]))
        grad_probs.append(dot_nt(span_rows(near_refs, span, rows, vcols), grads[at]))
    weights, grad_scores = probs_and_grads(
        jnp.concatenate(scores, axis=1), jnp.concatenate(grad_probs, axis=1), None
    )
    for at in range(blocks):
        span, group = at // groups, at % groups
        here = slice(span * rows, (span + 1) * rows)
        cols = slice(group * HEAD_SIZE, (group + 1) * HEAD_SIZE)
        vcols = slice(kv_width + group * HEAD_SIZE, kv_width + (group + 1) * HEAD_SIZE)
        part = slice(at * columns, (at + 1) * columns)
        w_ref[at] = weights[:, part]
        ds_ref[at] = grad_scores[:, part]
        dk = dot_nn(grad_scores[:, part], queries[at]).astype(BF16)
        dv = dot_nn(weights[:, part], grads[at]).astype(BF16)
        for i, grad_ref in enumerate(grad_refs):
            grad_ref[here, cols] = dk[i * rows : (i + 1) * rows]
            grad_ref[here, vcols] = dv[i * rows : (i + 1) * rows]


def add_cross(rows_span, p_ref, self_ref, out_ref, near_refs, first_col, groups):
    for at in range(p_ref.shape[0]):
        span, group = at // groups, at % groups
        rows = slice(span * SPAN_TOKENS, (span + 1) * SPAN_TOKENS)
        cols = slice(first_col + group * HEAD_SIZE, first_col + (group + 1) * HEAD_SIZE)
        cross = dot_tn(p_ref[at], span_rows(near_refs, span, rows_span // len(near_refs), cols))
        for h in range(GROUP):
            head = slice((group * GROUP + h) * HEAD_SIZE, (group * GROUP + h + 1) * HEAD_SIZE)
            part = slice(h * SPAN_TOKENS, (h + 1) * SPAN_TOKENS)
            out_ref[rows, head] = (self_ref[rows, head] + cross[part]).astype(BF16)


def join_attended_kernel(w_ref, out_ref, *refs):
    near_refs, att_ref = refs[:-1], refs[-1]
    kv_width = near_refs[0].shape[1] // 2
    add_cross(
        w_ref.shape[1], w_ref, out_ref, att_ref, near_refs, kv_width, kv_width // HEAD_SIZE
    )


def join_gradients_kernel(tp, ds_ref, dq_ref, dkv_ref, back_ref, *refs):
    near_refs, (qg_ref, kg_ref, vg_ref) = refs[:tp], refs[tp:]
    tokens, kv_width = kg_ref.shape
    add_cross(ds_ref.shape[1], ds_ref, dq_ref, qg_ref, near_refs, 0, kv_width // HEAD_SIZE)
    halo = back_ref.shape[0]
    kg_ref[: tokens - halo] = dkv_ref[: tokens - halo, :kv_width].astype(BF16)
    vg_ref[: tokens - halo] = dkv_ref[: tokens - halo, kv_width:].astype(BF16)
    kg_ref[tokens - halo :] = (
        dkv_ref[tokens - halo :, :kv_width] + back_ref[:, :kv_width].astype(F32)
    ).astype(BF16)
    vg_ref[tokens - halo :] = (
        dkv_ref[tokens - halo :, kv_width:] + back_ref[:, kv_width:].astype(F32)
    ).astype(BF16)


def sum_kernel(
    chunks,
    rows_each,
    z_ref,
    target_ref,
    other_ref,
    same_rows,
    other_rows,
    kg_any,
    vg_any,
    kg_ref,
    vg_ref,
    sems,
):
    slots, tokens, features = kg_ref.shape
    tp = NEIGHBOUR_LENGTH // tokens
    width = features // tp
    got = []
    for m in range(same_rows.shape[0] // rows_each):
        here = slice(m * rows_each, (m + 1) * rows_each)
        got += [same_rows[here], other_rows[here]]
    got = jnp.concatenate(got, axis=0)
    lanes = target_ref.shape[1]
    odd = (lax.broadcasted_iota(jnp.int32, (1, lanes), 1) // rows_each) % 2
    target = jnp.where(odd == 0, target_ref[...], other_ref[...])
    row = lax.broadcasted_iota(jnp.int32, (slots * tokens, lanes), 0)
    owned = jnp.where(row == target, 1.0, 0.0).astype(BF16)
    step = slots // chunks
    copies = []
    for i in range(chunks):
        part = slice(i * step, (i + 1) * step)
        total = dot_nn(owned[i * step * tokens : (i + 1) * step * tokens], got).astype(BF16)
        for d, apart in enumerate(farthest_first(tp)):
            cols = pl.ds(pl.multiple_of((z_ref[0] ^ apart) * width, width), width)
            at = 2 * d * width
            kg_ref[part, :, cols] = total[:, at : at + width].reshape(step, tokens, width)
            vg_ref[part, :, cols] = total[:, at + width : at + 2 * width].reshape(
                step, tokens, width
            )
        for j, (ref, out) in enumerate(((kg_ref, kg_any), (vg_ref, vg_any))):
            copies.append(pltpu.make_async_copy(ref.at[part], out.at[part], sems.at[2 * i + j]))
            copies[-1].start()
    for copy in copies:
        copy.wait()


def call(kernel, name, ins, outs, flops, bytes_accessed, scratch=(), scalars=0, fetched=0, stores=False):
    direct = len(ins) - fetched
    ins = ins[:direct] + tuple(
        pltpu.with_memory_space_constraint(each, pltpu.HBM) for each in ins[direct:]
    )
    return pl.pallas_call(
        kernel,
        out_shape=tuple(outs),
        in_specs=[SMEM] * scalars + [VMEM] * (direct - scalars) + [ANY] * fetched,
        out_specs=(ANY if stores else VMEM,) * len(outs),
        scratch_shapes=list(scratch),
        compiler_params=pltpu.CompilerParams(vmem_limit_bytes=16 * 1024 * 1024),
        cost_estimate=pl.CostEstimate(
            flops=flops, bytes_accessed=bytes_accessed, transcendentals=0
        ),
        name=name,
    )(*ins)


def swapped(block, axis, apart):
    return lax.ppermute(block, axis, [(i, i ^ apart) for i in range(lax.axis_size(axis))])


def chip_order(chips):
    return [0] + sorted(range(1, chips), key=lambda m: (-bin(m).count("1"), m))


def by_chip(refs):
    order = chip_order(len(refs))
    return [refs[order.index(m)] for m in range(len(refs))]


def between_chips(blocks):
    order = chip_order(len(blocks))
    return [blocks[0]] + [swapped(b, "seq", 2 * m) for b, m in zip(blocks[1:], order[1:])]


def farthest_first(tp):
    return distances(tp)[1:] + [0]


def distances(tp):
    return [0] + sorted(range(1, tp), key=lambda j: (j < 2, j))


def exchanged(blocks):
    apart = distances(len(blocks))
    return [blocks[0]] + [swapped(b, "tp", j) for b, j in zip(blocks[1:], apart[1:])]


def body(
    queries,
    sequence_keys,
    sequence_values,
    output_gradient,
    enc_keys,
    encoded_values,
    nbr_owner,
    nbr_slot,
):
    tokens_here, query_width = queries.shape
    kv_width = sequence_keys.shape[1]
    both = 2 * kv_width
    groups = kv_width // HEAD_SIZE
    devices = lax.axis_size("seq")
    tp = lax.axis_size("tp")
    spans, per_span = nbr_owner.shape
    requests = spans * per_span
    cap = max(2, 2 * requests // devices)
    tokens = enc_keys.shape[1]
    rows_each = cap * tokens
    window = WINDOW_KEYS
    struct = jax.ShapeDtypeStruct
    store_rows = enc_keys.shape[0] * tokens
    lanes = devices * rows_each
    used = requests * tokens
    int32 = jnp.int32
    rank = lax.axis_index("seq").astype(int32).reshape(1)
    z_rank = lax.axis_index("tp").astype(int32).reshape(1)

    sibling_keys = swapped(enc_keys, "seq", 1)
    sibling_values = swapped(encoded_values, "seq", 1)
    (want,) = call(
        functools.partial(plan_kernel, tokens, cap),
        "plan_requests",
        (nbr_owner, nbr_slot),
        (struct((devices, min(lanes, LANES)), int32),),
        0,
        100_000,
        scratch=[
            pltpu.SMEM(nbr_owner.shape, int32),
            pltpu.SMEM(nbr_slot.shape, int32),
            pltpu.SemaphoreType.DMA((2,)),
        ],
        fetched=2,
    )
    chips = devices // 2
    order = chip_order(chips)
    pieces = [want] + [swapped(want, "seq", 2 * m) for m in order[1:]]

    chunks = 4
    features = enc_keys.shape[2]
    store, halo, placed = call(
        functools.partial(stage_kernel, rows_each, chunks),
        "stage_store",
        (rank, z_rank, sibling_keys, sibling_values, nbr_owner, sequence_keys, sequence_values)
        + (enc_keys, encoded_values),
        (
            struct((2 * store_rows, 2 * features), BF16),
            struct((window, both), BF16),
            struct((lanes, used), BF16),
        ),
        0,
        5_000_000,
        scratch=[pltpu.SMEM(nbr_owner.shape, int32)]
        + [pltpu.VMEM(enc_keys.shape, BF16)] * 2
        + [pltpu.SemaphoreType.DMA((3 + 2 * chunks,))],
        scalars=2,
        fetched=5,
    )
    block = struct((2 * rows_each, features), BF16)
    *sent, target = call(
        functools.partial(pack_kernel, rows_each),
        "pack_requests",
        (rank, store, *pieces),
        [block] * (2 * chips) + [struct((1, lanes), int32)],
        200_000_000,
        2_000_000,
        scalars=1,
    )
    parts = tp // 2
    moved = []
    far, near = between_chips(sent[:chips]), sent[chips:]
    for name, got in (("spread_far", far), ("spread_near", between_chips(near))):
        moved += call(
            functools.partial(spread_kernel, parts),
            name,
            (placed, *got),
            [struct((used, both), BF16)] * parts,
            1_000_000,
            10_000,
        )
    near = exchanged(moved[-1:] + moved[:-1])
    halo = lax.ppermute(halo, "seq", [(i, (i + 1) % devices) for i in range(devices)])
    other_target = swapped(target, "seq", 1)
    self_out, self_dq, self_dkv, back = call(
        self_kernel,
        "self_attention",
        (rank, queries, sequence_keys, sequence_values, output_gradient, halo),
        (
            struct((tokens_here, query_width), F32),
            struct((tokens_here, query_width), F32),
            struct((tokens_here, both), F32),
            struct((window, both), BF16),
        ),
        1_000_000,
        10_000,
        scalars=1,
    )
    back = lax.ppermute(back, "seq", [((i + 1) % devices, i) for i in range(devices)])
    near[1], self_out = lax.optimization_barrier((near[1], self_out))

    blocks = spans * groups
    rows_span = per_span * NEIGHBOUR_LENGTH
    *grads, weights, grad_scores = call(
        functools.partial(cross_kernel, tp),
        "cross_attention",
        (queries, output_gradient, *near),
        [struct((used, both), BF16)] * tp
        + [struct((blocks, rows_span, GROUP * SPAN_TOKENS), BF16)] * 2,
        600_000_000,
        3_000_000,
    )
    grads = exchanged(grads)
    grads = grads[1:] + grads[:1]
    returned = []
    for name, half in (("scatter_near", grads[parts:]), ("scatter_far", grads[:parts])):
        if not returned:
            half[0], back = lax.optimization_barrier((half[0], back))
        if returned:
            half, returned[2] = lax.optimization_barrier((half, returned[2]))
        sent = call(
            functools.partial(scatter_kernel, chips),
            name,
            (placed, *half),
            [block] * chips,
            1_000_000,
            10_000,
        )
        if returned:
            sent, weights = lax.optimization_barrier((sent, weights))
        returned += between_chips(sent)
    returned = returned[chips:] + returned[:chips]
    (attended,) = call(
        join_attended_kernel,
        "join_attended",
        (weights, self_out, *near),
        (struct((tokens_here, query_width), BF16),),
        1_000_000,
        10_000,
    )
    returned[0], attended, other_target = lax.optimization_barrier(
        (returned[0], attended, other_target)
    )
    same, other = call(
        part_cores_kernel,
        "part_cores",
        tuple(returned),
        [struct((lanes // 2, 2 * features), BF16)] * 2,
        0,
        10_000,
    )
    same, grad_scores = lax.optimization_barrier((same, grad_scores))
    other = swapped(other, "seq", 1)

    query_gradient, key_gradient, value_gradient = call(
        functools.partial(join_gradients_kernel, tp),
        "join_gradients",
        (grad_scores, self_dq, self_dkv, back, *near),
        (
            struct((tokens_here, query_width), BF16),
            struct((tokens_here, kv_width), BF16),
            struct((tokens_here, kv_width), BF16),
        ),
        1_000_000,
        10_000,
    )
    other, query_gradient = lax.optimization_barrier((other, query_gradient))

    store_kgrad, store_vgrad = call(
        functools.partial(sum_kernel, chunks, rows_each),
        "sum_store_gradients",
        (z_rank, target, other_target, same, other),
        (struct(enc_keys.shape, BF16), struct(encoded_values.shape, BF16)),
        200_000_000,
        2_000_000,
        scratch=[
            pltpu.VMEM(enc_keys.shape, BF16),
            pltpu.VMEM(encoded_values.shape, BF16),
            pltpu.SemaphoreType.DMA((2 * chunks,)),
        ],
        scalars=1,
        stores=True,
    )
    return (
        attended,
        query_gradient,
        key_gradient,
        value_gradient,
        store_kgrad,
        store_vgrad,
    )


def solution(mesh):
    arguments = (P("seq", "tp"),) * 4 + (P("seq", "tp", None),) * 2 + (P("seq", None),) * 2
    results = (P("seq", "tp"),) * 4 + (P("seq", "tp", None),) * 2
    return jax.shard_map(
        body, mesh=mesh, in_specs=arguments, out_specs=results, check_vma=False
    )
```

```python
import functools
import math

import jax
import jax.numpy as jnp
from jax import lax
from jax.experimental import pallas as pl
from jax.experimental.pallas import tpu as pltpu
from jax.sharding import PartitionSpec as P

QUERY_HEADS = 32
KEY_VALUE_HEADS = 8
HEAD_SIZE = 128
SPAN_TOKENS = 64
NEIGHBOUR_COUNT = 4
NEIGHBOUR_LENGTH = 16
WINDOW_KEYS = 128
GROUP = QUERY_HEADS // KEY_VALUE_HEADS
SCALE = 1.0 / math.sqrt(HEAD_SIZE)
LOG2E = math.log2(math.e)

F32 = jnp.float32
BF16 = jnp.bfloat16
VMEM = pl.BlockSpec(memory_space=pltpu.VMEM)
SMEM = pl.BlockSpec(memory_space=pltpu.SMEM)
ANY = pl.BlockSpec(memory_space=pl.ANY)
LANES = 128


def dot_nn(a, b):
    return lax.dot_general(a, b, (((1,), (0,)), ((), ())), preferred_element_type=F32)


def dot_nt(a, b):
    return lax.dot_general(a, b, (((1,), (1,)), ((), ())), preferred_element_type=F32)


def dot_tn(a, b):
    return lax.dot_general(a, b, (((0,), (0,)), ((), ())), preferred_element_type=F32)


def stacked_heads(ref, first_row, rows, group):
    return jnp.concatenate(
        [
            ref[
                first_row : first_row + rows,
                (group * GROUP + h) * HEAD_SIZE : (group * GROUP + h + 1) * HEAD_SIZE,
            ]
            for h in range(GROUP)
        ],
        axis=0,
    )


def probs_and_grads(scores, grad_probs, allowed):
    scores = scores * (SCALE * LOG2E)
    if allowed is not None:
        scores = jnp.where(allowed, scores, -jnp.inf)
    raised = jnp.exp2(scores - jnp.max(scores, axis=0, keepdims=True))
    probs = raised * (1.0 / jnp.sum(raised, axis=0, keepdims=True))
    delta = jnp.sum(probs * grad_probs, axis=0, keepdims=True)
    grad_scores = (probs * (grad_probs - delta) * SCALE).astype(BF16)
    return probs.astype(BF16), grad_scores


def plan_kernel(tokens, cap, owner_any, slot_any, want_ref, owner_ref, slot_ref, sems):
    copies = [
        pltpu.make_async_copy(owner_any, owner_ref, sems.at[0]),
        pltpu.make_async_copy(slot_any, slot_ref, sems.at[1]),
    ]
    for copy in copies:
        copy.start()
    row = lax.broadcasted_iota(jnp.int32, want_ref.shape, 0)
    lane = lax.broadcasted_iota(jnp.int32, want_ref.shape, 1)
    place = row * cap + (lane // tokens) % cap
    token = lane % tokens
    want = jnp.full(want_ref.shape, -1, jnp.int32)
    for copy in copies:
        copy.wait()
    for i, j, owner, rank in ranked(owner_ref):
        want = jnp.where(place == owner * cap + rank, slot_ref[i, j] * tokens + token, want)
    want_ref[...] = want


def ranked(owner_ref):
    spans, per_span = owner_ref.shape
    owners, found = [], []
    for i in range(spans):
        for j in range(per_span):
            owner = owner_ref[i, j]
            rank = jnp.int32(0)
            for earlier in owners:
                rank = rank + jnp.where(earlier == owner, 1, 0)
            owners.append(owner)
            found.append((i, j, owner, rank))
    return found


def stage_kernel(
    rows_each,
    chunks,
    me_ref,
    z_ref,
    sibling_k_ref,
    sibling_v_ref,
    owner_any,
    sk_any,
    sv_any,
    k_any,
    v_any,
    store_ref,
    halo_ref,
    placed_ref,
    owner_ref,
    k_ref,
    v_ref,
    sems,
):
    store_refs = (k_ref, v_ref, sibling_k_ref, sibling_v_ref)
    slots, tokens, features = store_refs[0].shape
    kv_width = sk_any.shape[1]
    window = halo_ref.shape[0]
    tail = slice(sk_any.shape[0] - window, sk_any.shape[0])
    step = slots // chunks
    fetch_owner = pltpu.make_async_copy(owner_any, owner_ref, sems.at[0])
    fetch_owner.start()
    left, right = slice(0, kv_width), slice(kv_width, 2 * kv_width)
    copies = []
    for i in range(chunks):
        part = slice(i * step, (i + 1) * step)
        copies.append(pltpu.make_async_copy(k_any.at[part], k_ref.at[part], sems.at[3 + 2 * i]))
        copies.append(pltpu.make_async_copy(v_any.at[part], v_ref.at[part], sems.at[4 + 2 * i]))
    copies.append(pltpu.make_async_copy(sk_any.at[tail], halo_ref.at[:, left], sems.at[1]))
    copies.append(pltpu.make_async_copy(sv_any.at[tail], halo_ref.at[:, right], sems.at[2]))
    for copy in copies:
        copy.start()
    fetch_owner.wait()
    me = me_ref[0]
    lanes, used = placed_ref.shape
    lane = lax.broadcasted_iota(jnp.int32, (1, used), 1)
    place = lane % tokens
    for r, (_, _, owner, rank) in enumerate(ranked(owner_ref)):
        place = place + jnp.where(lane // tokens == r, (owner ^ me) * rows_each + rank * tokens, 0)
    row = lax.broadcasted_iota(jnp.int32, (lanes, used), 0)
    placed_ref[...] = jnp.where(row == place, 1.0, 0.0).astype(BF16)
    for i in range(chunks):
        part = slice(i * step, (i + 1) * step)
        copies[2 * i].wait()
        copies[2 * i + 1].wait()
        for j in range(4):
            core, kind = j // 2, j % 2
            first = (core * slots + i * step) * tokens
            rows = slice(first, first + step * tokens)
            for d, apart in enumerate(farthest_first(features // kv_width)):
                start = pl.multiple_of((z_ref[0] ^ apart) * kv_width, kv_width)
                at = (2 * d + kind) * kv_width
                store_ref[rows, at : at + kv_width] = store_refs[j][
                    part, :, pl.ds(start, kv_width)
                ].reshape(step * tokens, kv_width)
    for copy in copies[2 * chunks :]:
        copy.wait()


def pack_kernel(rows_each, me_ref, store_ref, *refs):
    pieces = len(refs) // 3
    wanted_refs, far_refs, near_refs, target_ref = (
        refs[:pieces],
        by_chip(refs[pieces : 2 * pieces]),
        by_chip(refs[2 * pieces : 3 * pieces]),
        refs[-1],
    )
    rows, columns = store_ref.shape[0], store_ref.shape[1] // 2
    lanes = target_ref.shape[1]
    width = wanted_refs[0].shape[1]
    me = me_ref[0]
    lane = lax.broadcasted_iota(jnp.int32, (1, width), 1)
    parts = [jnp.full((1, width), -1, jnp.int32) for _ in range(lanes // width)]
    for m, wanted_ref in enumerate(by_chip(wanted_refs)):
        for core in range(2):
            part, at = divmod((2 * m + core) * rows_each, width)
            from_there = wanted_ref[pl.ds(me ^ core, 1), :]
            here = (lane >= at) & (lane < at + rows_each)
            parts[part] = jnp.where(here, from_there, parts[part])
    target = jnp.concatenate(parts, axis=1)
    target_ref[...] = target
    second = (lax.broadcasted_iota(jnp.int32, (1, lanes), 1) // rows_each) % 2
    target = jnp.where(target >= 0, target + second * (rows // 2), -1)
    row = lax.broadcasted_iota(jnp.int32, (rows, lanes), 0)
    picks = jnp.where(row == target, 1.0, 0.0).astype(BF16)
    for half, send_refs in enumerate((far_refs, near_refs)):
        cols = slice(half * columns, (half + 1) * columns)
        picked = dot_tn(picks, store_ref[:, cols]).astype(BF16)
        for m, send_ref in enumerate(send_refs):
            send_ref[...] = picked[2 * m * rows_each : 2 * (m + 1) * rows_each]


def spread_kernel(parts, placed_ref, *refs):
    got_refs, send_refs = refs[: -parts], refs[-parts :]
    width = send_refs[0].shape[1]
    got = jnp.concatenate([ref[...] for ref in by_chip(got_refs)], axis=0)
    rows = dot_tn(placed_ref[...], got).astype(BF16)
    for i, send_ref in enumerate(send_refs):
        send_ref[...] = rows[:, i * width : (i + 1) * width]


def scatter_kernel(chips, placed_ref, *refs):
    grad_refs, send_refs = refs[:-chips], refs[-chips:]
    grads = jnp.concatenate([ref[...] for ref in grad_refs], axis=1)
    rows = dot_nn(placed_ref[...], grads).astype(BF16)
    step = send_refs[0].shape[0]
    for m, send_ref in enumerate(by_chip(send_refs)):
        send_ref[...] = rows[m * step : (m + 1) * step]


def part_cores_kernel(*refs):
    got_refs, (same_ref, other_ref) = refs[:-2], refs[-2:]
    chips = len(got_refs) // 2
    rows, columns = got_refs[0].shape[0] // 2, got_refs[0].shape[1]
    for half in range(2):
        cols = slice(half * columns, (half + 1) * columns)
        for m, got_ref in enumerate(by_chip(got_refs[half * chips : (half + 1) * chips])):
            here = slice(m * rows, (m + 1) * rows)
            same_ref[here, cols] = got_ref[:rows]
            other_ref[here, cols] = got_ref[rows:]


def self_kernel(
    rank_ref, q_ref, k_ref, v_ref, do_ref, halo_ref, out_ref, dq_ref, dkv_ref, back_ref
):
    tokens, kv_width = k_ref.shape
    block = WINDOW_KEYS
    blocks = tokens // block
    key_at = lax.broadcasted_iota(jnp.int32, (2 * block, GROUP * block), 0)
    query_at = lax.broadcasted_iota(jnp.int32, (2 * block, GROUP * block), 1) % block
    band = (key_at > query_at) & (key_at <= query_at + block)
    first_band = band & ((key_at >= block) | (rank_ref[0] > 0))
    for group in range(kv_width // HEAD_SIZE):
        cols = slice(group * HEAD_SIZE, (group + 1) * HEAD_SIZE)
        vcols = slice(kv_width + group * HEAD_SIZE, kv_width + (group + 1) * HEAD_SIZE)
        carried_k = carried_v = None
        for b in range(blocks):
            here = slice(b * block, (b + 1) * block)
            if b == 0:
                keys = jnp.concatenate([halo_ref[:, cols], k_ref[here, cols]], 0)
                values = jnp.concatenate([halo_ref[:, vcols], v_ref[here, cols]], 0)
            else:
                keys = k_ref[(b - 1) * block : (b + 1) * block, cols]
                values = v_ref[(b - 1) * block : (b + 1) * block, cols]
            query_rows = stacked_heads(q_ref, b * block, block, group)
            grad_rows = stacked_heads(do_ref, b * block, block, group)
            weights, grad_scores = probs_and_grads(
                dot_nt(keys, query_rows),
                dot_nt(values, grad_rows),
                first_band if b == 0 else band,
            )
            out = dot_tn(weights, values)
            dq = dot_tn(grad_scores, keys)
            for h in range(GROUP):
                head = slice((group * GROUP + h) * HEAD_SIZE, (group * GROUP + h + 1) * HEAD_SIZE)
                out_ref[here, head] = out[h * block : (h + 1) * block]
                dq_ref[here, head] = dq[h * block : (h + 1) * block]
            dk = dot_nn(grad_scores, query_rows)
            dv = dot_nn(weights, grad_rows)
            if b == 0:
                back_ref[:, cols] = dk[:block].astype(BF16)
                back_ref[:, vcols] = dv[:block].astype(BF16)
            else:
                before = slice((b - 1) * block, b * block)
                dkv_ref[before, cols] = carried_k + dk[:block]
                dkv_ref[before, vcols] = carried_v + dv[:block]
            carried_k, carried_v = dk[block:], dv[block:]
        last = slice((blocks - 1) * block, blocks * block)
        dkv_ref[last, cols] = carried_k
        dkv_ref[last, vcols] = carried_v


def span_rows(near_refs, span, rows, cols):
    return jnp.concatenate([ref[span * rows : (span + 1) * rows, cols] for ref in near_refs], axis=0)


def cross_kernel(tp, q_ref, do_ref, *refs):
    near_refs, grad_refs, w_ref, ds_ref = refs[:tp], refs[tp : 2 * tp], refs[2 * tp], refs[2 * tp + 1]
    kv_width = near_refs[0].shape[1] // 2
    groups = kv_width // HEAD_SIZE
    blocks, rows_span, columns = w_ref.shape
    rows = rows_span // tp
    queries, grads, scores, grad_probs = [], [], [], []
    for at in range(blocks):
        span, group = at // groups, at % groups
        cols = slice(group * HEAD_SIZE, (group + 1) * HEAD_SIZE)
        vcols = slice(kv_width + group * HEAD_SIZE, kv_width + (group + 1) * HEAD_SIZE)
        queries.append(stacked_heads(q_ref, span * SPAN_TOKENS, SPAN_TOKENS, group))
        grads.append(stacked_heads(do_ref, span * SPAN_TOKENS, SPAN_TOKENS, group))
        scores.append(dot_nt(span_rows(near_refs, span, rows, cols), queries[at]))
        grad_probs.append(dot_nt(span_rows(near_refs, span, rows, vcols), grads[at]))
    weights, grad_scores = probs_and_grads(
        jnp.concatenate(scores, axis=1), jnp.concatenate(grad_probs, axis=1), None
    )
    for at in range(blocks):
        span, group = at // groups, at % groups
        here = slice(span * rows, (span + 1) * rows)
        cols = slice(group * HEAD_SIZE, (group + 1) * HEAD_SIZE)
        vcols = slice(kv_width + group * HEAD_SIZE, kv_width + (group + 1) * HEAD_SIZE)
        part = slice(at * columns, (at + 1) * columns)
        w_ref[at] = weights[:, part]
        ds_ref[at] = grad_scores[:, part]
        dk = dot_nn(grad_scores[:, part], queries[at]).astype(BF16)
        dv = dot_nn(weights[:, part], grads[at]).astype(BF16)
        for i, grad_ref in enumerate(grad_refs):
            grad_ref[here, cols] = dk[i * rows : (i + 1) * rows]
            grad_ref[here, vcols] = dv[i * rows : (i + 1) * rows]


def add_cross(rows_span, p_ref, self_ref, out_ref, near_refs, first_col, groups):
    for at in range(p_ref.shape[0]):
        span, group = at // groups, at % groups
        rows = slice(span * SPAN_TOKENS, (span + 1) * SPAN_TOKENS)
        cols = slice(first_col + group * HEAD_SIZE, first_col + (group + 1) * HEAD_SIZE)
        cross = dot_tn(p_ref[at], span_rows(near_refs, span, rows_span // len(near_refs), cols))
        for h in range(GROUP):
            head = slice((group * GROUP + h) * HEAD_SIZE, (group * GROUP + h + 1) * HEAD_SIZE)
            part = slice(h * SPAN_TOKENS, (h + 1) * SPAN_TOKENS)
            out_ref[rows, head] = (self_ref[rows, head] + cross[part]).astype(BF16)


def join_attended_kernel(w_ref, out_ref, *refs):
    near_refs, att_ref = refs[:-1], refs[-1]
    kv_width = near_refs[0].shape[1] // 2
    add_cross(
        w_ref.shape[1], w_ref, out_ref, att_ref, near_refs, kv_width, kv_width // HEAD_SIZE
    )


def join_gradients_kernel(tp, ds_ref, dq_ref, dkv_ref, back_ref, *refs):
    near_refs, (qg_ref, kg_ref, vg_ref) = refs[:tp], refs[tp:]
    tokens, kv_width = kg_ref.shape
    add_cross(ds_ref.shape[1], ds_ref, dq_ref, qg_ref, near_refs, 0, kv_width // HEAD_SIZE)
    halo = back_ref.shape[0]
    kg_ref[: tokens - halo] = dkv_ref[: tokens - halo, :kv_width].astype(BF16)
    vg_ref[: tokens - halo] = dkv_ref[: tokens - halo, kv_width:].astype(BF16)
    kg_ref[tokens - halo :] = (
        dkv_ref[tokens - halo :, :kv_width] + back_ref[:, :kv_width].astype(F32)
    ).astype(BF16)
    vg_ref[tokens - halo :] = (
        dkv_ref[tokens - halo :, kv_width:] + back_ref[:, kv_width:].astype(F32)
    ).astype(BF16)


def sum_kernel(
    chunks,
    rows_each,
    z_ref,
    target_ref,
    other_ref,
    same_rows,
    other_rows,
    kg_any,
    vg_any,
    kg_ref,
    vg_ref,
    sems,
):
    slots, tokens, features = kg_ref.shape
    tp = NEIGHBOUR_LENGTH // tokens
    width = features // tp
    got = []
    for m in range(same_rows.shape[0] // rows_each):
        here = slice(m * rows_each, (m + 1) * rows_each)
        got += [same_rows[here], other_rows[here]]
    got = jnp.concatenate(got, axis=0)
    lanes = target_ref.shape[1]
    odd = (lax.broadcasted_iota(jnp.int32, (1, lanes), 1) // rows_each) % 2
    target = jnp.where(odd == 0, target_ref[...], other_ref[...])
    row = lax.broadcasted_iota(jnp.int32, (slots * tokens, lanes), 0)
    owned = jnp.where(row == target, 1.0, 0.0).astype(BF16)
    step = slots // chunks
    copies = []
    for i in range(chunks):
        part = slice(i * step, (i + 1) * step)
        total = dot_nn(owned[i * step * tokens : (i + 1) * step * tokens], got).astype(BF16)
        for d, apart in enumerate(farthest_first(tp)):
            cols = pl.ds(pl.multiple_of((z_ref[0] ^ apart) * width, width), width)
            at = 2 * d * width
            kg_ref[part, :, cols] = total[:, at : at + width].reshape(step, tokens, width)
            vg_ref[part, :, cols] = total[:, at + width : at + 2 * width].reshape(
                step, tokens, width
            )
        for j, (ref, out) in enumerate(((kg_ref, kg_any), (vg_ref, vg_any))):
            copies.append(pltpu.make_async_copy(ref.at[part], out.at[part], sems.at[2 * i + j]))
            copies[-1].start()
    for copy in copies:
        copy.wait()


def call(kernel, name, ins, outs, flops, bytes_accessed, scratch=(), scalars=0, fetched=0, stores=False):
    direct = len(ins) - fetched
    ins = ins[:direct] + tuple(
        pltpu.with_memory_space_constraint(each, pltpu.HBM) for each in ins[direct:]
    )
    return pl.pallas_call(
        kernel,
        out_shape=tuple(outs),
        in_specs=[SMEM] * scalars + [VMEM] * (direct - scalars) + [ANY] * fetched,
        out_specs=(ANY if stores else VMEM,) * len(outs),
        scratch_shapes=list(scratch),
        compiler_params=pltpu.CompilerParams(vmem_limit_bytes=16 * 1024 * 1024),
        cost_estimate=pl.CostEstimate(
            flops=flops, bytes_accessed=bytes_accessed, transcendentals=0
        ),
        name=name,
    )(*ins)


def swapped(block, axis, apart):
    return lax.ppermute(block, axis, [(i, i ^ apart) for i in range(lax.axis_size(axis))])


def chip_order(chips):
    return [0] + sorted(range(1, chips), key=lambda m: (-bin(m).count("1"), m))


def by_chip(refs):
    order = chip_order(len(refs))
    return [refs[order.index(m)] for m in range(len(refs))]


def between_chips(blocks):
    order = chip_order(len(blocks))
    return [blocks[0]] + [swapped(b, "seq", 2 * m) for b, m in zip(blocks[1:], order[1:])]


def farthest_first(tp):
    return distances(tp)[1:] + [0]


def distances(tp):
    return [0] + sorted(range(1, tp), key=lambda j: (j < 2, j))


def exchanged(blocks):
    apart = distances(len(blocks))
    return [blocks[0]] + [swapped(b, "tp", j) for b, j in zip(blocks[1:], apart[1:])]


def body(
    queries,
    sequence_keys,
    sequence_values,
    output_gradient,
    enc_keys,
    encoded_values,
    nbr_owner,
    nbr_slot,
):
    tokens_here, query_width = queries.shape
    kv_width = sequence_keys.shape[1]
    both = 2 * kv_width
    groups = kv_width // HEAD_SIZE
    devices = lax.axis_size("seq")
    tp = lax.axis_size("tp")
    spans, per_span = nbr_owner.shape
    requests = spans * per_span
    cap = max(2, 2 * requests // devices)
    tokens = enc_keys.shape[1]
    rows_each = cap * tokens
    window = WINDOW_KEYS
    struct = jax.ShapeDtypeStruct
    store_rows = enc_keys.shape[0] * tokens
    lanes = devices * rows_each
    used = requests * tokens
    int32 = jnp.int32
    rank = lax.axis_index("seq").astype(int32).reshape(1)
    z_rank = lax.axis_index("tp").astype(int32).reshape(1)

    sibling_keys = swapped(enc_keys, "seq", 1)
    sibling_values = swapped(encoded_values, "seq", 1)
    (want,) = call(
        functools.partial(plan_kernel, tokens, cap),
        "plan_requests",
        (nbr_owner, nbr_slot),
        (struct((devices, min(lanes, LANES)), int32),),
        0,
        100_000,
        scratch=[
            pltpu.SMEM(nbr_owner.shape, int32),
            pltpu.SMEM(nbr_slot.shape, int32),
            pltpu.SemaphoreType.DMA((2,)),
        ],
        fetched=2,
    )
    chips = devices // 2
    order = chip_order(chips)
    pieces = [want] + [swapped(want, "seq", 2 * m) for m in order[1:]]

    chunks = 4
    features = enc_keys.shape[2]
    store, halo, placed = call(
        functools.partial(stage_kernel, rows_each, chunks),
        "stage_store",
        (rank, z_rank, sibling_keys, sibling_values, nbr_owner, sequence_keys, sequence_values)
        + (enc_keys, encoded_values),
        (
            struct((2 * store_rows, 2 * features), BF16),
            struct((window, both), BF16),
            struct((lanes, used), BF16),
        ),
        0,
        5_000_000,
        scratch=[pltpu.SMEM(nbr_owner.shape, int32)]
        + [pltpu.VMEM(enc_keys.shape, BF16)] * 2
        + [pltpu.SemaphoreType.DMA((3 + 2 * chunks,))],
        scalars=2,
        fetched=5,
    )
    block = struct((2 * rows_each, features), BF16)
    *sent, target = call(
        functools.partial(pack_kernel, rows_each),
        "pack_requests",
        (rank, store, *pieces),
        [block] * (2 * chips) + [struct((1, lanes), int32)],
        200_000_000,
        2_000_000,
        scalars=1,
    )
    parts = tp // 2
    moved = []
    far, near = between_chips(sent[:chips]), sent[chips:]
    for name, got in (("spread_far", far), ("spread_near", between_chips(near))):
        moved += call(
            functools.partial(spread_kernel, parts),
            name,
            (placed, *got),
            [struct((used, both), BF16)] * parts,
            1_000_000,
            10_000,
        )
    near = exchanged(moved[-1:] + moved[:-1])
    halo = lax.ppermute(halo, "seq", [(i, (i + 1) % devices) for i in range(devices)])
    other_target = swapped(target, "seq", 1)
    self_out, self_dq, self_dkv, back = call(
        self_kernel,
        "self_attention",
        (rank, queries, sequence_keys, sequence_values, output_gradient, halo),
        (
            struct((tokens_here, query_width), F32),
            struct((tokens_here, query_width), F32),
            struct((tokens_here, both), F32),
            struct((window, both), BF16),
        ),
        1_000_000,
        10_000,
        scalars=1,
    )
    back = lax.ppermute(back, "seq", [((i + 1) % devices, i) for i in range(devices)])
    near[1], self_out = lax.optimization_barrier((near[1], self_out))

    blocks = spans * groups
    rows_span = per_span * NEIGHBOUR_LENGTH
    *grads, weights, grad_scores = call(
        functools.partial(cross_kernel, tp),
        "cross_attention",
        (queries, output_gradient, *near),
        [struct((used, both), BF16)] * tp
        + [struct((blocks, rows_span, GROUP * SPAN_TOKENS), BF16)] * 2,
        600_000_000,
        3_000_000,
    )
    grads = exchanged(grads)
    grads = grads[1:] + grads[:1]
    returned = []
    for name, half in (("scatter_near", grads[parts:]), ("scatter_far", grads[:parts])):
        if returned:
            half[0], back = lax.optimization_barrier((half[0], back))
        if returned:
            half, returned[2] = lax.optimization_barrier((half, returned[2]))
        sent = call(
            functools.partial(scatter_kernel, chips),
            name,
            (placed, *half),
            [block] * chips,
            1_000_000,
            10_000,
        )
        if returned:
            sent, weights = lax.optimization_barrier((sent, weights))
        returned += between_chips(sent)
    returned = returned[chips:] + returned[:chips]
    (attended,) = call(
        join_attended_kernel,
        "join_attended",
        (weights, self_out, *near),
        (struct((tokens_here, query_width), BF16),),
        1_000_000,
        10_000,
    )
    returned[0], attended, other_target = lax.optimization_barrier(
        (returned[0], attended, other_target)
    )
    same, other = call(
        part_cores_kernel,
        "part_cores",
        tuple(returned),
        [struct((lanes // 2, 2 * features), BF16)] * 2,
        0,
        10_000,
    )
    same, grad_scores = lax.optimization_barrier((same, grad_scores))
    other = swapped(other, "seq", 1)

    query_gradient, key_gradient, value_gradient = call(
        functools.partial(join_gradients_kernel, tp),
        "join_gradients",
        (grad_scores, self_dq, self_dkv, back, *near),
        (
            struct((tokens_here, query_width), BF16),
            struct((tokens_here, kv_width), BF16),
            struct((tokens_here, kv_width), BF16),
        ),
        1_000_000,
        10_000,
    )
    other, query_gradient = lax.optimization_barrier((other, query_gradient))

    store_kgrad, store_vgrad = call(
        functools.partial(sum_kernel, chunks, rows_each),
        "sum_store_gradients",
        (z_rank, target, other_target, same, other),
        (struct(enc_keys.shape, BF16), struct(encoded_values.shape, BF16)),
        200_000_000,
        2_000_000,
        scratch=[
            pltpu.VMEM(enc_keys.shape, BF16),
            pltpu.VMEM(encoded_values.shape, BF16),
            pltpu.SemaphoreType.DMA((2 * chunks,)),
        ],
        scalars=1,
        stores=True,
    )
    return (
        attended,
        query_gradient,
        key_gradient,
        value_gradient,
        store_kgrad,
        store_vgrad,
    )


def solution(mesh):
    arguments = (P("seq", "tp"),) * 4 + (P("seq", "tp", None),) * 2 + (P("seq", None),) * 2
    results = (P("seq", "tp"),) * 4 + (P("seq", "tp", None),) * 2
    return jax.shard_map(
        body, mesh=mesh, in_specs=arguments, out_specs=results, check_vma=False
    )
```

```python
import functools
import math

import jax
import jax.numpy as jnp
from jax import lax
from jax.experimental import pallas as pl
from jax.experimental.pallas import tpu as pltpu
from jax.sharding import PartitionSpec as P

QUERY_HEADS = 32
KEY_VALUE_HEADS = 8
HEAD_SIZE = 128
SPAN_TOKENS = 64
NEIGHBOUR_COUNT = 4
NEIGHBOUR_LENGTH = 16
WINDOW_KEYS = 128
GROUP = QUERY_HEADS // KEY_VALUE_HEADS
SCALE = 1.0 / math.sqrt(HEAD_SIZE)
LOG2E = math.log2(math.e)

F32 = jnp.float32
BF16 = jnp.bfloat16
VMEM = pl.BlockSpec(memory_space=pltpu.VMEM)
SMEM = pl.BlockSpec(memory_space=pltpu.SMEM)
ANY = pl.BlockSpec(memory_space=pl.ANY)
LANES = 128


def dot_nn(a, b):
    return lax.dot_general(a, b, (((1,), (0,)), ((), ())), preferred_element_type=F32)


def dot_nt(a, b):
    return lax.dot_general(a, b, (((1,), (1,)), ((), ())), preferred_element_type=F32)


def dot_tn(a, b):
    return lax.dot_general(a, b, (((0,), (0,)), ((), ())), preferred_element_type=F32)


def stacked_heads(ref, first_row, rows, group):
    return jnp.concatenate(
        [
            ref[
                first_row : first_row + rows,
                (group * GROUP + h) * HEAD_SIZE : (group * GROUP + h + 1) * HEAD_SIZE,
            ]
            for h in range(GROUP)
        ],
        axis=0,
    )


def probs_and_grads(scores, grad_probs, allowed):
    scores = scores * (SCALE * LOG2E)
    if allowed is not None:
        scores = jnp.where(allowed, scores, -jnp.inf)
    raised = jnp.exp2(scores - jnp.max(scores, axis=0, keepdims=True))
    probs = raised * (1.0 / jnp.sum(raised, axis=0, keepdims=True))
    delta = jnp.sum(probs * grad_probs, axis=0, keepdims=True)
    grad_scores = (probs * (grad_probs - delta) * SCALE).astype(BF16)
    return probs.astype(BF16), grad_scores


def plan_kernel(tokens, cap, owner_any, slot_any, want_ref, owner_ref, slot_ref, sems):
    copies = [
        pltpu.make_async_copy(owner_any, owner_ref, sems.at[0]),
        pltpu.make_async_copy(slot_any, slot_ref, sems.at[1]),
    ]
    for copy in copies:
        copy.start()
    row = lax.broadcasted_iota(jnp.int32, want_ref.shape, 0)
    lane = lax.broadcasted_iota(jnp.int32, want_ref.shape, 1)
    place = row * cap + (lane // tokens) % cap
    token = lane % tokens
    want = jnp.full(want_ref.shape, -1, jnp.int32)
    for copy in copies:
        copy.wait()
    for i, j, owner, rank in ranked(owner_ref):
        want = jnp.where(place == owner * cap + rank, slot_ref[i, j] * tokens + token, want)
    want_ref[...] = want


def ranked(owner_ref):
    spans, per_span = owner_ref.shape
    owners, found = [], []
    for i in range(spans):
        for j in range(per_span):
            owner = owner_ref[i, j]
            rank = jnp.int32(0)
            for earlier in owners:
                rank = rank + jnp.where(earlier == owner, 1, 0)
            owners.append(owner)
            found.append((i, j, owner, rank))
    return found


def stage_kernel(
    rows_each,
    chunks,
    me_ref,
    z_ref,
    sibling_k_ref,
    sibling_v_ref,
    owner_any,
    sk_any,
    sv_any,
    k_any,
    v_any,
    store_ref,
    halo_ref,
    placed_ref,
    owner_ref,
    k_ref,
    v_ref,
    sems,
):
    store_refs = (k_ref, v_ref, sibling_k_ref, sibling_v_ref)
    slots, tokens, features = store_refs[0].shape
    kv_width = sk_any.shape[1]
    window = halo_ref.shape[0]
    tail = slice(sk_any.shape[0] - window, sk_any.shape[0])
    step = slots // chunks
    fetch_owner = pltpu.make_async_copy(owner_any, owner_ref, sems.at[0])
    fetch_owner.start()
    left, right = slice(0, kv_width), slice(kv_width, 2 * kv_width)
    copies = []
    for i in range(chunks):
        part = slice(i * step, (i + 1) * step)
        copies.append(pltpu.make_async_copy(k_any.at[part], k_ref.at[part], sems.at[3 + 2 * i]))
        copies.append(pltpu.make_async_copy(v_any.at[part], v_ref.at[part], sems.at[4 + 2 * i]))
    copies.append(pltpu.make_async_copy(sk_any.at[tail], halo_ref.at[:, left], sems.at[1]))
    copies.append(pltpu.make_async_copy(sv_any.at[tail], halo_ref.at[:, right], sems.at[2]))
    for copy in copies:
        copy.start()
    fetch_owner.wait()
    me = me_ref[0]
    lanes, used = placed_ref.shape
    lane = lax.broadcasted_iota(jnp.int32, (1, used), 1)
    place = lane % tokens
    for r, (_, _, owner, rank) in enumerate(ranked(owner_ref)):
        place = place + jnp.where(lane // tokens == r, (owner ^ me) * rows_each + rank * tokens, 0)
    row = lax.broadcasted_iota(jnp.int32, (lanes, used), 0)
    placed_ref[...] = jnp.where(row == place, 1.0, 0.0).astype(BF16)
    for i in range(chunks):
        part = slice(i * step, (i + 1) * step)
        copies[2 * i].wait()
        copies[2 * i + 1].wait()
        for j in range(4):
            core, kind = j // 2, j % 2
            first = (core * slots + i * step) * tokens
            rows = slice(first, first + step * tokens)
            for d, apart in enumerate(farthest_first(features // kv_width)):
                start = pl.multiple_of((z_ref[0] ^ apart) * kv_width, kv_width)
                at = (2 * d + kind) * kv_width
                store_ref[rows, at : at + kv_width] = store_refs[j][
                    part, :, pl.ds(start, kv_width)
                ].reshape(step * tokens, kv_width)
    for copy in copies[2 * chunks :]:
        copy.wait()


def pack_kernel(rows_each, me_ref, store_ref, *refs):
    pieces = len(refs) // 3
    wanted_refs, far_refs, near_refs, target_ref = (
        refs[:pieces],
        by_chip(refs[pieces : 2 * pieces]),
        by_chip(refs[2 * pieces : 3 * pieces]),
        refs[-1],
    )
    rows, columns = store_ref.shape[0], store_ref.shape[1] // 2
    lanes = target_ref.shape[1]
    width = wanted_refs[0].shape[1]
    me = me_ref[0]
    lane = lax.broadcasted_iota(jnp.int32, (1, width), 1)
    parts = [jnp.full((1, width), -1, jnp.int32) for _ in range(lanes // width)]
    for m, wanted_ref in enumerate(by_chip(wanted_refs)):
        for core in range(2):
            part, at = divmod((2 * m + core) * rows_each, width)
            from_there = wanted_ref[pl.ds(me ^ core, 1), :]
            here = (lane >= at) & (lane < at + rows_each)
            parts[part] = jnp.where(here, from_there, parts[part])
    target = jnp.concatenate(parts, axis=1)
    target_ref[...] = target
    second = (lax.broadcasted_iota(jnp.int32, (1, lanes), 1) // rows_each) % 2
    target = jnp.where(target >= 0, target + second * (rows // 2), -1)
    row = lax.broadcasted_iota(jnp.int32, (rows, lanes), 0)
    picks = jnp.where(row == target, 1.0, 0.0).astype(BF16)
    for half, send_refs in enumerate((far_refs, near_refs)):
        cols = slice(half * columns, (half + 1) * columns)
        picked = dot_tn(picks, store_ref[:, cols]).astype(BF16)
        for m, send_ref in enumerate(send_refs):
            send_ref[...] = picked[2 * m * rows_each : 2 * (m + 1) * rows_each]


def spread_kernel(parts, placed_ref, *refs):
    got_refs, send_refs = refs[: -parts], refs[-parts :]
    width = send_refs[0].shape[1]
    got = jnp.concatenate([ref[...] for ref in by_chip(got_refs)], axis=0)
    rows = dot_tn(placed_ref[...], got).astype(BF16)
    for i, send_ref in enumerate(send_refs):
        send_ref[...] = rows[:, i * width : (i + 1) * width]


def scatter_kernel(chips, placed_ref, *refs):
    grad_refs, send_refs = refs[:-chips], refs[-chips:]
    grads = jnp.concatenate([ref[...] for ref in grad_refs], axis=1)
    rows = dot_nn(placed_ref[...], grads).astype(BF16)
    step = send_refs[0].shape[0]
    for m, send_ref in enumerate(by_chip(send_refs)):
        send_ref[...] = rows[m * step : (m + 1) * step]


def part_cores_kernel(*refs):
    got_refs, (same_ref, other_ref) = refs[:-2], refs[-2:]
    chips = len(got_refs) // 2
    rows, columns = got_refs[0].shape[0] // 2, got_refs[0].shape[1]
    for half in range(2):
        cols = slice(half * columns, (half + 1) * columns)
        for m, got_ref in enumerate(by_chip(got_refs[half * chips : (half + 1) * chips])):
            here = slice(m * rows, (m + 1) * rows)
            same_ref[here, cols] = got_ref[:rows]
            other_ref[here, cols] = got_ref[rows:]


def self_kernel(
    rank_ref, q_ref, k_ref, v_ref, do_ref, halo_ref, out_ref, dq_ref, dkv_ref, back_ref
):
    tokens, kv_width = k_ref.shape
    block = WINDOW_KEYS
    blocks = tokens // block
    key_at = lax.broadcasted_iota(jnp.int32, (2 * block, GROUP * block), 0)
    query_at = lax.broadcasted_iota(jnp.int32, (2 * block, GROUP * block), 1) % block
    band = (key_at > query_at) & (key_at <= query_at + block)
    first_band = band & ((key_at >= block) | (rank_ref[0] > 0))
    for group in range(kv_width // HEAD_SIZE):
        cols = slice(group * HEAD_SIZE, (group + 1) * HEAD_SIZE)
        vcols = slice(kv_width + group * HEAD_SIZE, kv_width + (group + 1) * HEAD_SIZE)
        carried_k = carried_v = None
        for b in range(blocks):
            here = slice(b * block, (b + 1) * block)
            if b == 0:
                keys = jnp.concatenate([halo_ref[:, cols], k_ref[here, cols]], 0)
                values = jnp.concatenate([halo_ref[:, vcols], v_ref[here, cols]], 0)
            else:
                keys = k_ref[(b - 1) * block : (b + 1) * block, cols]
                values = v_ref[(b - 1) * block : (b + 1) * block, cols]
            query_rows = stacked_heads(q_ref, b * block, block, group)
            grad_rows = stacked_heads(do_ref, b * block, block, group)
            weights, grad_scores = probs_and_grads(
                dot_nt(keys, query_rows),
                dot_nt(values, grad_rows),
                first_band if b == 0 else band,
            )
            out = dot_tn(weights, values)
            dq = dot_tn(grad_scores, keys)
            for h in range(GROUP):
                head = slice((group * GROUP + h) * HEAD_SIZE, (group * GROUP + h + 1) * HEAD_SIZE)
                out_ref[here, head] = out[h * block : (h + 1) * block]
                dq_ref[here, head] = dq[h * block : (h + 1) * block]
            dk = dot_nn(grad_scores, query_rows)
            dv = dot_nn(weights, grad_rows)
            if b == 0:
                back_ref[:, cols] = dk[:block].astype(BF16)
                back_ref[:, vcols] = dv[:block].astype(BF16)
            else:
                before = slice((b - 1) * block, b * block)
                dkv_ref[before, cols] = carried_k + dk[:block]
                dkv_ref[before, vcols] = carried_v + dv[:block]
            carried_k, carried_v = dk[block:], dv[block:]
        last = slice((blocks - 1) * block, blocks * block)
        dkv_ref[last, cols] = carried_k
        dkv_ref[last, vcols] = carried_v


def span_rows(near_refs, span, rows, cols):
    return jnp.concatenate([ref[span * rows : (span + 1) * rows, cols] for ref in near_refs], axis=0)


def cross_kernel(tp, q_ref, do_ref, *refs):
    near_refs, grad_refs, w_ref, ds_ref = refs[:tp], refs[tp : 2 * tp], refs[2 * tp], refs[2 * tp + 1]
    kv_width = near_refs[0].shape[1] // 2
    groups = kv_width // HEAD_SIZE
    blocks, rows_span, columns = w_ref.shape
    rows = rows_span // tp
    queries, grads, scores, grad_probs = [], [], [], []
    for at in range(blocks):
        span, group = at // groups, at % groups
        cols = slice(group * HEAD_SIZE, (group + 1) * HEAD_SIZE)
        vcols = slice(kv_width + group * HEAD_SIZE, kv_width + (group + 1) * HEAD_SIZE)
        queries.append(stacked_heads(q_ref, span * SPAN_TOKENS, SPAN_TOKENS, group))
        grads.append(stacked_heads(do_ref, span * SPAN_TOKENS, SPAN_TOKENS, group))
        scores.append(dot_nt(span_rows(near_refs, span, rows, cols), queries[at]))
        grad_probs.append(dot_nt(span_rows(near_refs, span, rows, vcols), grads[at]))
    weights, grad_scores = probs_and_grads(
        jnp.concatenate(scores, axis=1), jnp.concatenate(grad_probs, axis=1), None
    )
    for at in range(blocks):
        span, group = at // groups, at % groups
        here = slice(span * rows, (span + 1) * rows)
        cols = slice(group * HEAD_SIZE, (group + 1) * HEAD_SIZE)
        vcols = slice(kv_width + group * HEAD_SIZE, kv_width + (group + 1) * HEAD_SIZE)
        part = slice(at * columns, (at + 1) * columns)
        w_ref[at] = weights[:, part]
        ds_ref[at] = grad_scores[:, part]
        dk = dot_nn(grad_scores[:, part], queries[at]).astype(BF16)
        dv = dot_nn(weights[:, part], grads[at]).astype(BF16)
        for i, grad_ref in enumerate(grad_refs):
            grad_ref[here, cols] = dk[i * rows : (i + 1) * rows]
            grad_ref[here, vcols] = dv[i * rows : (i + 1) * rows]


def join_kernel(tp, w_ref, ds_ref, out_ref, dq_ref, dkv_ref, back_ref, *refs):
    near_refs, (att_ref, qg_ref, kg_ref, vg_ref) = refs[:tp], refs[tp:]
    tokens, kv_width = kg_ref.shape
    groups = kv_width // HEAD_SIZE
    blocks, rows_span, _ = w_ref.shape
    for span in range(blocks // groups):
        rows = slice(span * SPAN_TOKENS, (span + 1) * SPAN_TOKENS)
        for group in range(groups):
            cols = slice(group * HEAD_SIZE, (group + 1) * HEAD_SIZE)
            vcols = slice(kv_width + group * HEAD_SIZE, kv_width + (group + 1) * HEAD_SIZE)
            at = span * groups + group
            out = dot_tn(w_ref[at], span_rows(near_refs, span, rows_span // tp, vcols))
            dq = dot_tn(ds_ref[at], span_rows(near_refs, span, rows_span // tp, cols))
            for h in range(GROUP):
                head = slice((group * GROUP + h) * HEAD_SIZE, (group * GROUP + h + 1) * HEAD_SIZE)
                part = slice(h * SPAN_TOKENS, (h + 1) * SPAN_TOKENS)
                att_ref[rows, head] = (out_ref[rows, head] + out[part]).astype(BF16)
                qg_ref[rows, head] = (dq_ref[rows, head] + dq[part]).astype(BF16)
    halo = back_ref.shape[0]
    kg_ref[: tokens - halo] = dkv_ref[: tokens - halo, :kv_width].astype(BF16)
    vg_ref[: tokens - halo] = dkv_ref[: tokens - halo, kv_width:].astype(BF16)
    kg_ref[tokens - halo :] = (
        dkv_ref[tokens - halo :, :kv_width] + back_ref[:, :kv_width].astype(F32)
    ).astype(BF16)
    vg_ref[tokens - halo :] = (
        dkv_ref[tokens - halo :, kv_width:] + back_ref[:, kv_width:].astype(F32)
    ).astype(BF16)


def sum_kernel(
    chunks,
    rows_each,
    z_ref,
    target_ref,
    other_ref,
    same_rows,
    other_rows,
    kg_any,
    vg_any,
    kg_ref,
    vg_ref,
    sems,
):
    slots, tokens, features = kg_ref.shape
    tp = NEIGHBOUR_LENGTH // tokens
    width = features // tp
    got = []
    for m in range(same_rows.shape[0] // rows_each):
        here = slice(m * rows_each, (m + 1) * rows_each)
        got += [same_rows[here], other_rows[here]]
    got = jnp.concatenate(got, axis=0)
    lanes = target_ref.shape[1]
    odd = (lax.broadcasted_iota(jnp.int32, (1, lanes), 1) // rows_each) % 2
    target = jnp.where(odd == 0, target_ref[...], other_ref[...])
    row = lax.broadcasted_iota(jnp.int32, (slots * tokens, lanes), 0)
    owned = jnp.where(row == target, 1.0, 0.0).astype(BF16)
    step = slots // chunks
    copies = []
    for i in range(chunks):
        part = slice(i * step, (i + 1) * step)
        total = dot_nn(owned[i * step * tokens : (i + 1) * step * tokens], got).astype(BF16)
        for d, apart in enumerate(farthest_first(tp)):
            cols = pl.ds(pl.multiple_of((z_ref[0] ^ apart) * width, width), width)
            at = 2 * d * width
            kg_ref[part, :, cols] = total[:, at : at + width].reshape(step, tokens, width)
            vg_ref[part, :, cols] = total[:, at + width : at + 2 * width].reshape(
                step, tokens, width
            )
        for j, (ref, out) in enumerate(((kg_ref, kg_any), (vg_ref, vg_any))):
            copies.append(pltpu.make_async_copy(ref.at[part], out.at[part], sems.at[2 * i + j]))
            copies[-1].start()
    for copy in copies:
        copy.wait()


def call(kernel, name, ins, outs, flops, bytes_accessed, scratch=(), scalars=0, fetched=0, stores=False):
    direct = len(ins) - fetched
    ins = ins[:direct] + tuple(
        pltpu.with_memory_space_constraint(each, pltpu.HBM) for each in ins[direct:]
    )
    return pl.pallas_call(
        kernel,
        out_shape=tuple(outs),
        in_specs=[SMEM] * scalars + [VMEM] * (direct - scalars) + [ANY] * fetched,
        out_specs=(ANY if stores else VMEM,) * len(outs),
        scratch_shapes=list(scratch),
        compiler_params=pltpu.CompilerParams(vmem_limit_bytes=16 * 1024 * 1024),
        cost_estimate=pl.CostEstimate(
            flops=flops, bytes_accessed=bytes_accessed, transcendentals=0
        ),
        name=name,
    )(*ins)


def swapped(block, axis, apart):
    return lax.ppermute(block, axis, [(i, i ^ apart) for i in range(lax.axis_size(axis))])


def chip_order(chips):
    return [0] + sorted(range(1, chips), key=lambda m: (-bin(m).count("1"), m))


def by_chip(refs):
    order = chip_order(len(refs))
    return [refs[order.index(m)] for m in range(len(refs))]


def between_chips(blocks):
    order = chip_order(len(blocks))
    return [blocks[0]] + [swapped(b, "seq", 2 * m) for b, m in zip(blocks[1:], order[1:])]


def farthest_first(tp):
    return distances(tp)[1:] + [0]


def distances(tp):
    return [0] + sorted(range(1, tp), key=lambda j: (j < 2, j))


def exchanged(blocks):
    apart = distances(len(blocks))
    return [blocks[0]] + [swapped(b, "tp", j) for b, j in zip(blocks[1:], apart[1:])]


def body(
    queries,
    sequence_keys,
    sequence_values,
    output_gradient,
    enc_keys,
    encoded_values,
    nbr_owner,
    nbr_slot,
):
    tokens_here, query_width = queries.shape
    kv_width = sequence_keys.shape[1]
    both = 2 * kv_width
    groups = kv_width // HEAD_SIZE
    devices = lax.axis_size("seq")
    tp = lax.axis_size("tp")
    spans, per_span = nbr_owner.shape
    requests = spans * per_span
    cap = max(2, 2 * requests // devices)
    tokens = enc_keys.shape[1]
    rows_each = cap * tokens
    window = WINDOW_KEYS
    struct = jax.ShapeDtypeStruct
    store_rows = enc_keys.shape[0] * tokens
    lanes = devices * rows_each
    used = requests * tokens
    int32 = jnp.int32
    rank = lax.axis_index("seq").astype(int32).reshape(1)
    z_rank = lax.axis_index("tp").astype(int32).reshape(1)

    sibling_keys = swapped(enc_keys, "seq", 1)
    sibling_values = swapped(encoded_values, "seq", 1)
    (want,) = call(
        functools.partial(plan_kernel, tokens, cap),
        "plan_requests",
        (nbr_owner, nbr_slot),
        (struct((devices, min(lanes, LANES)), int32),),
        0,
        100_000,
        scratch=[
            pltpu.SMEM(nbr_owner.shape, int32),
            pltpu.SMEM(nbr_slot.shape, int32),
            pltpu.SemaphoreType.DMA((2,)),
        ],
        fetched=2,
    )
    chips = devices // 2
    order = chip_order(chips)
    pieces = [want] + [swapped(want, "seq", 2 * m) for m in order[1:]]

    chunks = 4
    features = enc_keys.shape[2]
    store, halo, placed = call(
        functools.partial(stage_kernel, rows_each, chunks),
        "stage_store",
        (rank, z_rank, sibling_keys, sibling_values, nbr_owner, sequence_keys, sequence_values)
        + (enc_keys, encoded_values),
        (
            struct((2 * store_rows, 2 * features), BF16),
            struct((window, both), BF16),
            struct((lanes, used), BF16),
        ),
        0,
        5_000_000,
        scratch=[pltpu.SMEM(nbr_owner.shape, int32)]
        + [pltpu.VMEM(enc_keys.shape, BF16)] * 2
        + [pltpu.SemaphoreType.DMA((3 + 2 * chunks,))],
        scalars=2,
        fetched=5,
    )
    block = struct((2 * rows_each, features), BF16)
    *sent, target = call(
        functools.partial(pack_kernel, rows_each),
        "pack_requests",
        (rank, store, *pieces),
        [block] * (2 * chips) + [struct((1, lanes), int32)],
        200_000_000,
        2_000_000,
        scalars=1,
    )
    parts = tp // 2
    moved = []
    far, near = between_chips(sent[:chips]), sent[chips:]
    for name, got in (("spread_far", far), ("spread_near", between_chips(near))):
        moved += call(
            functools.partial(spread_kernel, parts),
            name,
            (placed, *got),
            [struct((used, both), BF16)] * parts,
            1_000_000,
            10_000,
        )
    near = exchanged(moved[-1:] + moved[:-1])
    halo = lax.ppermute(halo, "seq", [(i, (i + 1) % devices) for i in range(devices)])
    other_target = swapped(target, "seq", 1)
    self_out, self_dq, self_dkv, back = call(
        self_kernel,
        "self_attention",
        (rank, queries, sequence_keys, sequence_values, output_gradient, halo),
        (
            struct((tokens_here, query_width), F32),
            struct((tokens_here, query_width), F32),
            struct((tokens_here, both), F32),
            struct((window, both), BF16),
        ),
        1_000_000,
        10_000,
        scalars=1,
    )
    back = lax.ppermute(back, "seq", [((i + 1) % devices, i) for i in range(devices)])
    near[1], self_out = lax.optimization_barrier((near[1], self_out))

    blocks = spans * groups
    rows_span = per_span * NEIGHBOUR_LENGTH
    *grads, weights, grad_scores = call(
        functools.partial(cross_kernel, tp),
        "cross_attention",
        (queries, output_gradient, *near),
        [struct((used, both), BF16)] * tp
        + [struct((blocks, rows_span, GROUP * SPAN_TOKENS), BF16)] * 2,
        600_000_000,
        3_000_000,
    )
    grads = exchanged(grads)
    grads = grads[1:] + grads[:1]
    returned = []
    for name, half in (("scatter_near", grads[parts:]), ("scatter_far", grads[:parts])):
        if not returned:
            half[0], back = lax.optimization_barrier((half[0], back))
        if returned:
            half, returned[2] = lax.optimization_barrier((half, returned[2]))
        sent = call(
            functools.partial(scatter_kernel, chips),
            name,
            (placed, *half),
            [block] * chips,
            1_000_000,
            10_000,
        )
        if returned:
            sent, weights = lax.optimization_barrier((sent, weights))
        returned += between_chips(sent)
    returned = returned[chips:] + returned[:chips]
    attended, query_gradient, key_gradient, value_gradient = call(
        functools.partial(join_kernel, tp),
        "join_outputs",
        (weights, grad_scores, self_out, self_dq, self_dkv, back, *near),
        (
            struct((tokens_here, query_width), BF16),
            struct((tokens_here, query_width), BF16),
            struct((tokens_here, kv_width), BF16),
            struct((tokens_here, kv_width), BF16),
        ),
        300_000_000,
        5_000_000,
    )
    returned[0], attended, other_target = lax.optimization_barrier(
        (returned[0], attended, other_target)
    )
    same, other = call(
        part_cores_kernel,
        "part_cores",
        tuple(returned),
        [struct((lanes // 2, 2 * features), BF16)] * 2,
        0,
        10_000,
    )
    other = swapped(other, "seq", 1)

    store_kgrad, store_vgrad = call(
        functools.partial(sum_kernel, chunks, rows_each),
        "sum_store_gradients",
        (z_rank, target, other_target, same, other),
        (struct(enc_keys.shape, BF16), struct(encoded_values.shape, BF16)),
        200_000_000,
        2_000_000,
        scratch=[
            pltpu.VMEM(enc_keys.shape, BF16),
            pltpu.VMEM(encoded_values.shape, BF16),
            pltpu.SemaphoreType.DMA((2 * chunks,)),
        ],
        scalars=1,
        stores=True,
    )
    return (
        attended,
        query_gradient,
        key_gradient,
        value_gradient,
        store_kgrad,
        store_vgrad,
    )


def solution(mesh):
    arguments = (P("seq", "tp"),) * 4 + (P("seq", "tp", None),) * 2 + (P("seq", None),) * 2
    results = (P("seq", "tp"),) * 4 + (P("seq", "tp", None),) * 2
    return jax.shard_map(
        body, mesh=mesh, in_specs=arguments, out_specs=results, check_vma=False
    )
```
